32 devices in a mesh: section: 2 (over core), dp: 16 (over z, y, x).
Axes of the slice: x: 2, y: 2, z: 4, core: 2. Of those that a mesh axis runs over, the one named last changes fastest.
Arguments:
- images: bfloat16 [2, 64, 14, 14, 1024], P(None, 'dp'), may hold values from 0 to 18
- out_grad: bfloat16 [2, 64, 7, 7, 2048], P(None, 'dp'), may hold values from -13.5 to 13.5
- live_counts: int32 [16, 2], replicated, may hold values from 2 to 4, as said below
- w_reduce0: bfloat16 [1024, 512], replicated, may hold values from -0.1875 to 0.1875
- w_short: bfloat16 [1024, 2048], replicated, may hold values from -0.1875 to 0.1875
- short_gain: float32 [2048], replicated, may hold values from 0.25 to 1.75
- short_bias: float32 [2048], replicated, may hold values from -2 to 2
- w_reduce1: bfloat16 [2048, 512], replicated, may hold values from -0.125 to 0.125
- w_mid: bfloat16 [2, 4608, 512], P('section'), may hold values from -0.09375 to 0.09375
- w_expand: bfloat16 [2, 512, 2048], P('section'), may hold values from -0.25 to 0.25
- gain_narrow: float32 [2, 2, 512], P('section'), may hold values from 0.25 to 1.75
- bias_narrow: float32 [2, 2, 512], P('section'), may hold values from -2 to 2
- gain_wide: float32 [2, 2048], P('section'), may hold values from 0.25 to 1.75
- bias_wide: float32 [2, 2048], P('section'), may hold values from -2 to 2
Outputs:
- block_out: bfloat16 [2, 64, 7, 7, 2048], P('section', 'dp')
- image_grad: bfloat16 [2, 64, 14, 14, 1024], P('section', 'dp')
- grad_reduce0: float32 [1024, 512], P(('section', 'dp'))
- grad_short: float32 [1024, 2048], P(('section', 'dp'))
- grad_short_norm: float32 [2, 2048], P(None, ('section', 'dp'))
- grad_reduce1: float32 [2048, 512], P(('section', 'dp'))
- grad_mid: float32 [2, 4608, 512], P('section', 'dp')
- grad_expand: float32 [2, 512, 2048], P('section', 'dp')
- grad_gain_narrow: float32 [2, 2, 512], P('section')
- grad_bias_narrow: float32 [2, 2, 512], P('section')
- grad_gain_wide: float32 [2, 2048], P('section')
- grad_bias_wide: float32 [2, 2048], P('section')
The draws below stay inside these ranges and needn't reach their ends.
Inputs may be any that keep to these rules, and one draw needn't show every extreme that they name: `live_counts`: slots of a dp index are live from its first one; in every micro-batch some dp index has all 4 slots live.
All inputs are finite; a program needn't handle non-finite values.
Results may differ from the reference program's by a relative error of at most 0.022.
Values may be sent and summed in bfloat16 or wider, within the bound.
No kernel may reach another device: no remote copies, remote signals or barrier semaphores. Data moves between devices by JAX's collectives and lax.ppermute only.
A program may use at most 192 MiB of HBM per device.

```python
import jax
import jax.numpy as jnp
from jax import lax

C_IN = 1024
MID = 512
OUT = 2048
HW = 7
CAP = 4
MB = 2
IMG = 64
N_DP = 16


def draw_images(key, part):
    key = jax.random.fold_in(key, 11)
    dims_all = (MB, IMG, 2 * HW, 2 * HW, C_IN)
    image_rows = jnp.arange(IMG, dtype=jnp.float32) / max(IMG - 1, 1)
    ramp_scale = 1.0 + 2.0 * image_rows
    base_draw = jax.nn.softplus(jnp.clip(jax.random.normal(key, dims_all, jnp.float32), -4.0, 4.0))
    return (base_draw * ramp_scale[None, :, None, None, None]).astype(jnp.bfloat16)


def draw_out_grad(key, part):
    key = jax.random.fold_in(key, 23)
    dims_all = (MB, IMG, HW, HW, OUT)
    image_rows = jnp.arange(IMG, dtype=jnp.float32) / max(IMG - 1, 1)
    ramp_scale = 1.0 + 2.0 * image_rows
    base_draw = jnp.clip(jax.random.normal(key, dims_all, jnp.float32), -4.0, 4.0)
    return (base_draw * ramp_scale[None, :, None, None, None]).astype(jnp.bfloat16)


def draw_live_counts(key, part):
    key = jax.random.fold_in(key, 37)
    count_key, fullest_key = jax.random.split(key)
    counts_drawn = jax.random.randint(count_key, (N_DP, MB), (CAP + 1) // 2, CAP + 1)
    fullest = jax.random.randint(fullest_key, (MB,), 0, N_DP)
    positions = jnp.arange(N_DP, dtype=jnp.int32)[:, None]
    return jnp.where(positions == fullest[None, :], CAP, counts_drawn).astype(jnp.int32)


def block_levels(own_key, extent, shards, smallest, largest):
    def one(dim, shards_of):
        draws = jax.random.uniform(jax.random.fold_in(jax.random.fold_in(own_key, 6), dim), (shards_of,), jnp.float32, smallest / len(shards), largest / len(shards))
        return jnp.repeat(jnp.exp(draws), extent[dim] // shards_of).reshape((-1,) + (1,) * (len(extent) - dim - 1))

    gain = one(*shards[0])
    for cut in shards[1:]:
        gain = gain * one(*cut)
    return gain


def gaussian(own_key, dims, width, most, cuts=(), kind=jnp.bfloat16):
    drawn = jax.random.normal(own_key, dims, jnp.float32) * width
    if len(cuts) > 0:
        drawn = block_levels(own_key, dims, cuts, -0.22, 0.18) * drawn
    return jnp.clip(drawn, min=-most, max=most).astype(kind)


def setup_inputs(seed: int = 0) -> dict:
    arg_keys = jax.random.split(jax.random.key(seed), 15)
    return {
        "images": draw_images(jax.random.fold_in(arg_keys[14], 71), 0),
        "out_grad": draw_out_grad(jax.random.fold_in(arg_keys[14], 71), 0),
        "live_counts": draw_live_counts(jax.random.fold_in(arg_keys[14], 71), 0),
        "w_reduce0": gaussian(arg_keys[3], (C_IN, MID), C_IN ** -0.5, 0.1875),
        "w_short": gaussian(arg_keys[4], (C_IN, OUT), C_IN ** -0.5, 0.1875),
        "short_gain": jnp.clip(1.0 + 0.15 * jax.random.normal(arg_keys[5], (OUT,), jnp.float32), 0.25, 1.75),
        "short_bias": gaussian(arg_keys[6], (OUT,), 0.5, 2.0, (), jnp.float32),
        "w_reduce1": gaussian(arg_keys[7], (OUT, MID), OUT ** -0.5, 0.125),
        "w_mid": gaussian(arg_keys[8], (2, 9 * MID, MID), (9 * MID) ** -0.5, 0.09375, ((0, 2),)),
        "w_expand": gaussian(arg_keys[9], (2, MID, OUT), MID ** -0.5, 0.25, ((0, 2),)),
        "gain_narrow": jnp.clip(1.0 + 0.15 * jax.random.normal(arg_keys[10], (2, 2, MID), jnp.float32), 0.25, 1.75),
        "bias_narrow": gaussian(arg_keys[11], (2, 2, MID), 0.5, 2.0, ((0, 2),), jnp.float32),
        "gain_wide": jnp.clip(1.0 + 0.15 * jax.random.normal(arg_keys[12], (2, OUT), jnp.float32), 0.25, 1.75),
        "bias_wide": gaussian(arg_keys[13], (2, OUT), 0.5, 2.0, ((0, 2),), jnp.float32),
    }


epsilon = 1e-05
highest = lax.Precision.HIGHEST

@jax.custom_vjp
def low(v):
    return lax.optimization_barrier(v.astype(jnp.bfloat16)).astype(jnp.float32)

@jax.custom_vjp
def low_back(v):
    return v

def low_keep(v):
    return (low(v), None)

def low_pass(kept, grad):
    return (grad,)

def back_keep(v):
    return (v, None)

def back_low(kept, grad):
    return (low(grad),)
low.defvjp(low_keep, low_pass)
low_back.defvjp(back_keep, back_low)

def point_map(values, weight):
    return jnp.einsum('nhwc,cd->nhwd', values, weight, precision=highest)

def tap_stack(values, stride, map_size):
    padded = jnp.pad(values, ((0, 0), (1, 1), (1, 1), (0, 0)))
    tap_span = stride * (map_size - 1) + 1
    pieces = []
    for tap_row in range(3):
        for column in range(3):
            pieces.append(padded[:, tap_row:tap_row + tap_span:stride, column:column + tap_span:stride, :])
    return jnp.concatenate(pieces, axis=3)

def batch_norm(values, live_mask, live_total, weight, offset):
    average = lax.optimization_barrier(jnp.sum(values * live_mask, axis=(0, 1, 2))) / live_total
    centered = values - average
    spread = lax.optimization_barrier(jnp.sum(centered * centered * live_mask, axis=(0, 1, 2))) / live_total
    return centered * lax.rsqrt(spread + epsilon) * weight + offset

def micro_step(params, inputs, live_mask, live_count):
    w_reduce0, w_short, short_gain, short_bias, w_reduce1, w_mid, w_expand, gain_narrow, bias_narrow, gain_wide, bias_wide = params
    inner_size = inputs.shape[1]
    map_size = inner_size // 2
    wide_total = live_count * inner_size * inner_size
    narrow_total = live_count * map_size * map_size
    reduced = low_back(point_map(inputs, w_reduce0))
    active_a = low(jax.nn.silu(batch_norm(reduced, live_mask, wide_total, gain_narrow[0, 0], bias_narrow[0, 0])))
    second = low_back(point_map(tap_stack(active_a, 2, map_size), w_mid[0]))
    active_b = low(jax.nn.silu(batch_norm(second, live_mask, narrow_total, gain_narrow[0, 1], bias_narrow[0, 1])))
    expanded = low_back(point_map(active_b, w_expand[0]))
    shortcut = low_back(point_map(inputs[:, ::2, ::2, :], w_short))
    joined = low_back(low(jax.nn.silu(batch_norm(expanded, live_mask, narrow_total, gain_wide[0], bias_wide[0]) + batch_norm(shortcut, live_mask, narrow_total, short_gain, short_bias))))
    reduced_b = low_back(point_map(joined, w_reduce1))
    active_c = low(jax.nn.silu(batch_norm(reduced_b, live_mask, narrow_total, gain_narrow[1, 0], bias_narrow[1, 0])))
    second_b = low_back(point_map(tap_stack(active_c, 1, map_size), w_mid[1]))
    active_d = low(jax.nn.silu(batch_norm(second_b, live_mask, narrow_total, gain_narrow[1, 1], bias_narrow[1, 1])))
    expanded_b = low_back(point_map(active_d, w_expand[1]))
    return jax.nn.silu(batch_norm(expanded_b, live_mask, narrow_total, gain_wide[1], bias_wide[1]) + joined)

def reference(images, out_grad, live_counts, w_reduce0, w_short, short_gain, short_bias, w_reduce1, w_mid, w_expand, gain_narrow, bias_narrow, gain_wide, bias_wide):
    float_args = []
    for weight in (w_reduce0, w_short, short_gain, short_bias, w_reduce1, w_mid, w_expand, gain_narrow, bias_narrow, gain_wide, bias_wide):
        float_args.append(weight.astype(jnp.float32))
    params = tuple(float_args)
    image_rows = jnp.arange(IMG, dtype=jnp.int32)
    owners = image_rows // CAP
    slot_index = image_rows % CAP
    live_masks = (slot_index[None, :] < live_counts[owners, :].T).astype(jnp.float32)
    live_totals = lax.optimization_barrier(jnp.sum(live_counts, axis=0)).astype(jnp.float32)
    inputs_float = images.astype(jnp.float32)

    def forward(params, inputs_float):

        def one_step(carry, pieces):
            inputs, live_row, live_count = pieces
            return (carry, micro_step(params, inputs, live_row[:, None, None, None], live_count))
        return lax.scan(jax.checkpoint(one_step), jnp.float32(0.0), (inputs_float, live_masks, live_totals))[1]
    block_float, pull_back = jax.vjp(forward, params, inputs_float)
    cotangent = out_grad.astype(jnp.float32) * live_masks[:, :, None, None, None]
    param_grads, input_grads = pull_back(cotangent)
    g_reduce0, g_short, g_short_gain, g_short_bias, g_reduce1, g_mid, g_expand, g_gain_narrow, g_bias_narrow, g_gain_wide, g_bias_wide = param_grads
    return (block_float.astype(jnp.bfloat16), input_grads.astype(jnp.bfloat16), g_reduce0, g_short, jnp.stack([g_short_gain, g_short_bias]), g_reduce1, g_mid, g_expand, g_gain_narrow, g_bias_narrow, g_gain_wide, g_bias_wide)
```

```python
import jax
import jax.numpy as jnp
from jax import lax
from jax.experimental import pallas as pl
from jax.experimental.pallas import tpu as pltpu
from jax.sharding import PartitionSpec as P


EPSILON = 1e-05
F32 = jnp.float32
BF16 = jnp.bfloat16
VMEM = pl.BlockSpec(memory_space=pltpu.VMEM)
SMEM = pl.BlockSpec(memory_space=pltpu.SMEM)
ANY = pl.BlockSpec(memory_space=pl.ANY)


def spec(shape, dtype=F32):
    return jax.ShapeDtypeStruct(shape, dtype)


def stage(kernel, outs, args, places, scratch=()):
    kinds = {"v": VMEM, "s": SMEM, "a": ANY}
    return pl.pallas_call(
        kernel,
        out_shape=list(outs),
        in_specs=[kinds[place] for place in places],
        out_specs=[VMEM] * len(outs),
        scratch_shapes=list(scratch),
        compiler_params=pltpu.CompilerParams(vmem_limit_bytes=58 << 20),
    )(*args)


class Geometry:
    def __init__(self, slots, side):
        self.slots = slots
        self.side = side
        self.pitch = side + 1
        self.per_image = self.pitch * self.pitch
        self.rows = slots * self.per_image
        self.pixels = side * side

    def mask(self, start, step, count=None):
        row = start + lax.broadcasted_iota(jnp.int32, (step, 1), 0)
        column = row % self.pitch
        line = (row // self.pitch) % self.pitch
        good = (column < self.side) & (line < self.side)
        if count is not None:
            image = (row // self.per_image) % self.slots
            good = good & (image < count)
        return jnp.where(good, 1.0, 0.0).astype(F32)


def over_rows(rows, step, body, init):
    def one(i, carry):
        return body(pl.multiple_of(i * step, step), carry)

    return lax.fori_loop(0, rows // step, one, init)


def fold_rows(block):
    rows, width = block.shape
    return jnp.sum(block.reshape(rows // 8, 8, width), axis=0)


def step_of(width):
    return 64 if width <= 512 else 16


def local_stats(z_ref, geo, count, planes):
    rows, width = z_ref.shape
    step = step_of(width)
    total = (count * (geo.pixels * planes)).astype(F32)

    def plain(start, acc):
        return acc + fold_rows(z_ref[pl.ds(start, step), :] * geo.mask(start, step, count))

    zero = jnp.zeros((8, width), F32)
    average = jnp.sum(over_rows(rows, step, plain, zero), axis=0, keepdims=True) / total

    def squared(start, acc):
        centered = z_ref[pl.ds(start, step), :] - average
        return acc + fold_rows(centered * centered * geo.mask(start, step, count))

    spread = jnp.sum(over_rows(rows, step, squared, zero), axis=0, keepdims=True)
    return average, spread


def send_rows(out_ref, values):
    for number, value in enumerate(values):
        for device in range(out_ref.shape[0]):
            out_ref[device, number : number + 1, :] = value


def total_of(counts, section, pixels):
    total = counts[0, section]
    for device in range(1, counts.shape[0]):
        total = total + counts[device, section]
    return (total * pixels).astype(F32)


def combined(got_ref, row, counts, section, pixels):
    devices = got_ref.shape[0]
    total = total_of(counts, section, pixels)
    sizes = [(counts[device, section] * pixels).astype(F32) for device in range(devices)]
    average = jnp.zeros((1, got_ref.shape[2]), F32)
    for device in range(devices):
        average = average + sizes[device] * got_ref[device, row : row + 1, :]
    average = average / total
    spread = jnp.zeros_like(average)
    for device in range(devices):
        apart = got_ref[device, row : row + 1, :] - average
        spread = spread + (got_ref[device, row + 1 : row + 2, :] + sizes[device] * (apart * apart))
    return average, lax.rsqrt(spread / total + EPSILON)


def summed(got_ref, row):
    total = got_ref[0, row : row + 1, :]
    for device in range(1, got_ref.shape[0]):
        total = total + got_ref[device, row : row + 1, :]
    return total


def sigmoid(values):
    return 1.0 / (1.0 + jnp.exp(-values))


def slope(values):
    part = sigmoid(values)
    return part * (1.0 + values * (1.0 - part))


class Choice:
    def __init__(self, section, wanted, own, other, target, sem):
        self.mine = section == wanted
        self.copies = (
            pltpu.make_async_copy(own.at[0], target, sem),
            pltpu.make_async_copy(other.at[0], target, sem),
        )

    def start(self):
        @pl.when(self.mine)
        def _():
            self.copies[0].start()

        @pl.when(jnp.logical_not(self.mine))
        def _():
            self.copies[1].start()

    def wait(self):
        @pl.when(self.mine)
        def _():
            self.copies[0].wait()

        @pl.when(jnp.logical_not(self.mine))
        def _():
            self.copies[1].wait()


def split_matrix(geo):
    side = 2 * geo.side
    rows, columns = 4 * geo.per_image, side * 16
    to = lax.broadcasted_iota(jnp.int32, (rows, columns), 0)
    at = lax.broadcasted_iota(jnp.int32, (rows, columns), 1)
    plane = to // geo.per_image
    line = (to // geo.pitch) % geo.pitch
    column = to % geo.pitch
    hit = (
        (line < geo.side)
        & (column < geo.side)
        & (at // 16 == 2 * line + plane // 2)
        & (at % 16 == 2 * column + plane % 2)
    )
    return jnp.where(hit, 1.0, 0.0).astype(BF16)


def join_matrix(geo):
    side = 2 * geo.side
    rows, columns = side * 16, 4 * geo.per_image
    at = lax.broadcasted_iota(jnp.int32, (rows, columns), 0)
    to = lax.broadcasted_iota(jnp.int32, (rows, columns), 1)
    plane = to // geo.per_image
    line = (to // geo.pitch) % geo.pitch
    column = to % geo.pitch
    hit = (
        (line < geo.side)
        & (column < geo.side)
        & (at // 16 == 2 * line + plane // 2)
        & (at % 16 == 2 * column + plane % 2)
    )
    return jnp.where(hit, 1.0, 0.0).astype(BF16)


def dot(left, right):
    return jnp.dot(left, right, preferred_element_type=F32)


def dot_back(left, right):
    return lax.dot_general(left, right, (((1,), (1,)), ((), ())), preferred_element_type=F32)


def rolled(values, shift):
    rows = values.shape[0]
    shift = shift % rows
    return values if shift == 0 else pltpu.roll(values, shift, 0)


def taps_of(stride, pitch):
    found = []
    for tap_row in range(3):
        for column in range(3):
            if stride == 1:
                found.append((0, (tap_row - 1) * pitch + column - 1))
            else:
                plane = 2 * (tap_row != 1) + (column != 1)
                found.append((plane, -pitch * (tap_row == 0) - (column == 0)))
    return found


def first_kernel(geo, place, counts, images, w_any, x_ref, z_ref, sent, raw, padded, weight, sem):
    section = place[1]
    count = counts[place[0], section]
    side = 2 * geo.side
    load = pltpu.make_async_copy(images.at[section], raw, sem.at[0])
    load.start()
    load_weight = pltpu.make_async_copy(w_any, weight, sem.at[1])
    load_weight.start()
    padded[...] = jnp.zeros_like(padded)
    matrix = split_matrix(geo)
    load.wait()
    for image in range(geo.slots):
        for line in range(side):
            at = (image * side + line) * 16
            padded[at : at + side, :] = raw[image, line]
    for image in range(geo.slots):
        flat = padded[image * side * 16 : (image + 1) * side * 16, :]
        parts = dot(matrix, flat).astype(BF16)
        for plane in range(4):
            at = plane * geo.rows + image * geo.per_image
            x_ref[at : at + geo.per_image, :] = parts[
                plane * geo.per_image : (plane + 1) * geo.per_image
            ]
    load_weight.wait()
    for plane in range(4):
        at = plane * geo.rows
        z_ref[at : at + geo.rows, :] = dot(x_ref[at : at + geo.rows, :], weight[...])
    send_rows(sent, local_stats(z_ref, geo, count, 4))


def short_kernel(geo, place, counts, x_any, weight, z_ref, stats, x_vmem, sem):
    count = counts[place[0], place[1]]
    load = pltpu.make_async_copy(x_any.at[pl.ds(0, geo.rows)], x_vmem, sem.at[0])
    load.start()
    load.wait()
    z_ref[...] = dot(x_vmem[...], weight[...])
    average, spread = local_stats(z_ref, geo, count, 1)
    stats[0:1, :] = average
    stats[1:2, :] = spread


def tap_kernel(geo, planes, block, which, place, counts, got, z_in, narrow, own, other, taps, z_ref, moments, sent,
               active, weight, sem):
    section = place[1]
    count = counts[place[0], section]
    choice = Choice(section, block, own, other, weight, sem.at[0])
    choice.start()
    average, inverse = combined(got, 0, counts, section, geo.pixels * planes)
    moments[0:1, :] = average
    moments[1:2, :] = inverse
    gain = narrow[which : which + 1, :] * inverse
    offset = narrow[2 + which : 3 + which, :]

    def activate(start, carry):
        pre = (z_in[pl.ds(start, 64), :] - average) * gain + offset
        active[pl.ds(start, 64), :] = pre * sigmoid(pre) * geo.mask(start, 64)
        return carry

    over_rows(z_in.shape[0], 64, activate, 0)
    width = z_in.shape[1]
    for tap, (plane, shift) in enumerate(taps_of(2 if planes == 4 else 1, geo.pitch)):
        block_rows = active[plane * geo.rows : (plane + 1) * geo.rows, :]
        taps[:, tap * width : (tap + 1) * width] = rolled(block_rows, -shift).astype(BF16)
    choice.wait()
    z_ref[...] = dot(taps[...], weight[...])
    send_rows(sent, local_stats(z_ref, geo, count, 1))


def expand_kernel(geo, block, extra, place, counts, got, z_in, narrow, own, other, *rest):
    if extra:
        stats, a_ref, z_ref, moments, sent, weight, sem = rest
    else:
        a_ref, z_ref, moments, sent, weight, sem = rest
    section = place[1]
    count = counts[place[0], section]
    choice = Choice(section, block, own, other, weight, sem.at[0])
    choice.start()
    average, inverse = combined(got, 0, counts, section, geo.pixels)
    moments[0:1, :] = average
    moments[1:2, :] = inverse
    gain = narrow[1:2, :] * inverse
    offset = narrow[3:4, :]

    def activate(start, carry):
        pre = (z_in[pl.ds(start, 64), :] - average) * gain + offset
        a_ref[pl.ds(start, 64), :] = (pre * sigmoid(pre)).astype(BF16)
        return carry

    over_rows(geo.rows, 64, activate, 0)
    choice.wait()
    z_ref[...] = dot(a_ref[...], weight[...])
    average, spread = local_stats(z_ref, geo, count, 1)
    if extra:
        send_rows(sent, (average, spread, stats[0:1, :], stats[1:2, :]))
    else:
        send_rows(sent, (average, spread))


def join_kernel(geo, place, counts, got, z3, zs, wide, short, w_any, joined, u_ref, moments, sent, weight, sem):
    section = place[1]
    count = counts[place[0], section]
    load = pltpu.make_async_copy(w_any, weight, sem.at[0])
    load.start()
    average_c, inverse_c = combined(got, 0, counts, section, geo.pixels)
    average_s, inverse_s = combined(got, 2, counts, section, geo.pixels)
    for number, value in enumerate((average_c, inverse_c, average_s, inverse_s)):
        moments[number : number + 1, :] = value
    gain_c = wide[0:1, :] * inverse_c
    gain_s = short[0:1, :] * inverse_s
    offset = wide[1:2, :] + short[1:2, :]

    def activate(start, carry):
        rows = pl.ds(start, 16)
        pre = (z3[rows, :] - average_c) * gain_c + (zs[rows, :] - average_s) * gain_s + offset
        joined[rows, :] = (pre * sigmoid(pre)).astype(BF16)
        return carry

    over_rows(geo.rows, 16, activate, 0)
    load.wait()
    u_ref[...] = dot(joined[...], weight[...])
    send_rows(sent, local_stats(u_ref, geo, count, 1))


def turn_kernel(geo, place, counts, got, u3, joined, wide, out_grad, out_ref, g_ref, moments, sent, raw, flat, sem):
    section = place[1]
    count = counts[place[0], section]
    load = pltpu.make_async_copy(out_grad.at[section], raw, sem.at[0])
    load.start()
    average, inverse = combined(got, 0, counts, section, geo.pixels)
    moments[0:1, :] = average
    moments[1:2, :] = inverse
    g_ref[...] = jnp.zeros_like(g_ref)
    load.wait()
    for image in range(geo.slots):
        for line in range(geo.side):
            at = image * geo.per_image + line * geo.pitch
            g_ref[at : at + geo.side, :] = raw[image, line].astype(F32)
    weight = wide[0:1, :]
    offset = wide[1:2, :]

    def activate(start, carry):
        plain, scaled = carry
        rows = pl.ds(start, 16)
        normed = (u3[rows, :] - average) * inverse
        pre = normed * weight + offset + joined[rows, :].astype(F32)
        part = sigmoid(pre)
        flat[rows, :] = pre * part
        upstream = g_ref[rows, :] * geo.mask(start, 16, count) * (part * (1.0 + pre * (1.0 - part)))
        g_ref[rows, :] = upstream
        return plain + fold_rows(upstream), scaled + fold_rows(upstream * normed)

    zero = jnp.zeros((8, u3.shape[1]), F32)
    plain, scaled = over_rows(geo.rows, 16, activate, (zero, zero))
    send_rows(sent, (jnp.sum(plain, axis=0, keepdims=True), jnp.sum(scaled, axis=0, keepdims=True)))
    for image in range(geo.slots):
        for line in range(geo.side):
            at = image * geo.per_image + line * geo.pitch
            out_ref[0, image, line] = flat[at : at + geo.side, :].astype(BF16)


def norm_grad(geo, rows_of, z_ref, g_ref, average, inverse, gain, plain, scaled, total, count, out_ref):
    width = z_ref.shape[1]
    step = step_of(width)
    factor = gain * inverse
    plain_part = plain / total
    scaled_part = scaled / total * inverse

    def one(start, carry):
        rows = pl.ds(start, step)
        centered = z_ref[rows, :] - average
        value = factor * (g_ref[rows, :] - plain_part - centered * scaled_part)
        value = jnp.where(geo.mask(start, step, count) > 0.0, value, 0.0)
        out_ref[rows, :] = value.astype(out_ref.dtype)
        return carry

    over_rows(rows_of, step, one, 0)


def silu_back(geo, z_ref, average, inverse, gain, offset, g_ref):
    rows_of, width = z_ref.shape
    step = step_of(width)

    def one(start, carry):
        plain, scaled = carry
        rows = pl.ds(start, step)
        normed = (z_ref[rows, :] - average) * inverse
        upstream = g_ref[rows, :] * slope(normed * gain + offset)
        upstream = jnp.where(geo.mask(start, step) > 0.0, upstream, 0.0)
        g_ref[rows, :] = upstream
        return plain + fold_rows(upstream), scaled + fold_rows(upstream * normed)

    zero = jnp.zeros((8, width), F32)
    plain, scaled = over_rows(rows_of, step, one, (zero, zero))
    return jnp.sum(plain, axis=0, keepdims=True), jnp.sum(scaled, axis=0, keepdims=True)


def expand_back(geo, block, two, place, counts, got, g_in, z3, mom3, wide, *rest):
    if two:
        zs, short, z2, mom2, narrow, own, other, dv, dvs, g_ref, sums, sent, weight, sem = rest
    else:
        z2, mom2, narrow, own, other, dv, g_ref, sums, sent, weight, sem = rest
    section = place[1]
    count = counts[place[0], section]
    choice = Choice(section, block, own, other, weight, sem.at[0])
    choice.start()
    total = total_of(counts, section, geo.pixels)
    plain, scaled = summed(got, 0), summed(got, 1)
    sums[0:1, :] = plain
    sums[1:2, :] = scaled
    norm_grad(geo, geo.rows, z3, g_in, mom3[0:1, :], mom3[1:2, :], wide[0:1, :], plain, scaled, total, count, dv)
    if two:
        scaled = summed(got, 2)
        sums[2:3, :] = scaled
        norm_grad(geo, geo.rows, zs, g_in, mom3[2:3, :], mom3[3:4, :], short[0:1, :], plain, scaled, total, count, dvs)
    choice.wait()
    g_ref[...] = dot_back(dv[...], weight[...])
    send_rows(
        sent, silu_back(geo, z2, mom2[0:1, :], mom2[1:2, :], narrow[1:2, :], narrow[3:4, :], g_ref)
    )


def tap_back(geo, planes, block, place, counts, got, g_in, z2, mom2, narrow, z1, mom1, own, other, dv, g_ref, sums, sent,
             wide_dv, weight, sem):
    section = place[1]
    count = counts[place[0], section]
    choice = Choice(section, block, own, other, weight, sem.at[0])
    choice.start()
    total = total_of(counts, section, geo.pixels)
    plain, scaled = summed(got, 0), summed(got, 1)
    sums[0:1, :] = plain
    sums[1:2, :] = scaled
    norm_grad(
        geo, geo.rows, z2, g_in, mom2[0:1, :], mom2[1:2, :], narrow[1:2, :], plain, scaled, total, count, wide_dv
    )
    values = wide_dv[...]
    dv[...] = values.astype(BF16)
    choice.wait()
    width = z1.shape[1]
    ready = {}
    done = [False] * planes
    for tap, (plane, shift) in enumerate(taps_of(2 if planes == 4 else 1, geo.pitch)):
        if shift not in ready:
            ready[shift] = rolled(values, shift).astype(BF16)
        product = dot_back(ready[shift], weight[tap * width : (tap + 1) * width, :])
        rows = slice(plane * geo.rows, (plane + 1) * geo.rows)
        if done[plane]:
            g_ref[rows, :] += product
        else:
            g_ref[rows, :] = product
        done[plane] = True
    send_rows(
        sent, silu_back(geo, z1, mom1[0:1, :], mom1[1:2, :], narrow[0:1, :], narrow[2:3, :], g_ref)
    )


def join_back(geo, place, counts, got, g_in, u1, mom4, narrow, w_any, g3, z3, zs, mom3, wide, short, dv, g_ref, sums, sent,
              weight, sem):
    section = place[1]
    count = counts[place[0], section]
    load = pltpu.make_async_copy(w_any, weight, sem.at[0])
    load.start()
    total = total_of(counts, section, geo.pixels)
    plain, scaled = summed(got, 0), summed(got, 1)
    sums[0:1, :] = plain
    sums[1:2, :] = scaled
    norm_grad(geo, geo.rows, u1, g_in, mom4[0:1, :], mom4[1:2, :], narrow[0:1, :], plain, scaled, total, count, dv)
    load.wait()
    g_ref[...] = dot_back(dv[...], weight[...])
    average_c, inverse_c = mom3[0:1, :], mom3[1:2, :]
    average_s, inverse_s = mom3[2:3, :], mom3[3:4, :]
    gain_c, gain_s = wide[0:1, :], short[0:1, :]
    offset = wide[1:2, :] + short[1:2, :]

    def one(start, carry):
        plain, scaled_c, scaled_s = carry
        rows = pl.ds(start, 16)
        normed_c = (z3[rows, :] - average_c) * inverse_c
        normed_s = (zs[rows, :] - average_s) * inverse_s
        arrived = (g_ref[rows, :] + g3[rows, :]).astype(BF16).astype(F32)
        upstream = arrived * slope(normed_c * gain_c + normed_s * gain_s + offset)
        upstream = jnp.where(geo.mask(start, 16) > 0.0, upstream, 0.0)
        g_ref[rows, :] = upstream
        return (
            plain + fold_rows(upstream),
            scaled_c + fold_rows(upstream * normed_c),
            scaled_s + fold_rows(upstream * normed_s),
        )

    zero = jnp.zeros((8, z3.shape[1]), F32)
    results = over_rows(geo.rows, 16, one, (zero, zero, zero))
    send_rows(sent, [jnp.sum(value, axis=0, keepdims=True) for value in results])


def last_kernel(geo, place, counts, got, g_in, z1, mom1, narrow, w_any, dvs, ws_any, dv, out_ref, sums, weight, weight_s,
                flat, sem):
    section = place[1]
    count = counts[place[0], section]
    load = pltpu.make_async_copy(w_any, weight, sem.at[0])
    load.start()
    load_s = pltpu.make_async_copy(ws_any, weight_s, sem.at[1])
    load_s.start()
    side = 2 * geo.side
    total = total_of(counts, section, geo.pixels * 4)
    plain, scaled = summed(got, 0), summed(got, 1)
    sums[0:1, :] = plain
    sums[1:2, :] = scaled
    norm_grad(
        geo, 4 * geo.rows, z1, g_in, mom1[0:1, :], mom1[1:2, :], narrow[0:1, :], plain, scaled, total, count, dv
    )
    load.wait()
    for plane in range(1, 4):
        at = plane * geo.rows
        flat[at : at + geo.rows, :] = dot_back(dv[at : at + geo.rows, :], weight[...]).astype(BF16)
    load_s.wait()
    flat[0 : geo.rows, :] = (
        dot_back(dv[0 : geo.rows, :], weight[...]) + dot_back(dvs[...], weight_s[...])
    ).astype(BF16)
    matrix = join_matrix(geo)
    for image in range(geo.slots):
        parts = []
        for plane in range(4):
            at = plane * geo.rows + image * geo.per_image
            parts.append(flat[at : at + geo.per_image, :])
        natural = dot(matrix, jnp.concatenate(parts, axis=0)).astype(BF16)
        for line in range(side):
            out_ref[0, image, line] = natural[line * 16 : line * 16 + side]


def weight_product(values, gradient):
    return lax.dot_general(values, gradient, (((0,), (0,)), ((), ())), preferred_element_type=F32).astype(BF16)


def exchange(sent):
    return lax.all_to_all(sent, "dp", 0, 0)


def swapped(value):
    return lax.ppermute(value, "section", [(0, 1), (1, 0)])


def across(value, mask):
    return lax.ppermute(value, "dp", [(i, i ^ mask) for i in range(lax.axis_size("dp"))])


def halved(part, bit, place_bit, mask):
    keep = lax.dynamic_index_in_dim(part, place_bit, bit, keepdims=False)
    send = lax.dynamic_index_in_dim(part, 1 - place_bit, bit, keepdims=False)
    return keep + across(send, mask)


def scattered(gradient, dp_index):
    devices, rows, columns = gradient.shape
    bits = devices.bit_length() - 1
    place = [(dp_index >> bit) & 1 for bit in range(bits)]
    half = columns // 2
    shape = (2,) * bits + (rows, half)
    first = gradient[..., :half].reshape(shape)
    second = gradient[..., half:].reshape(shape)
    last = bits - 1
    first = halved(first, last, place[0], 1)
    second = halved(second, last - 1, place[1], 2)
    first = halved(first, last - 1, place[1], 2)
    second = halved(second, last - 1, place[0], 1)
    both = jnp.concatenate([first, second], axis=-1)
    rest = list(range(2, bits))
    while len(rest) > 2:
        bit = rest.pop()
        both = halved(both, 0, place[bit], 1 << bit)
    upper = (dp_index >> 2) & ((1 << len(rest)) - 1)
    both = both.reshape(-1, rows, columns)
    total = lax.dynamic_index_in_dim(both, upper, 0, keepdims=False).astype(F32)
    arrived = []
    for mask in range(1, both.shape[0]):
        piece = lax.dynamic_index_in_dim(both, upper ^ mask, 0, keepdims=False)
        arrived.append(across(piece, mask << 2))
    for piece in arrived:
        total = total + piece.astype(F32)
    return total


def between_cores(gradient, section):
    keep = lax.dynamic_index_in_dim(gradient, section, 0, keepdims=False)
    send = lax.dynamic_index_in_dim(gradient, 1 - section, 0, keepdims=False)
    return keep + swapped(send)


def by_columns(gradient, section, dp_index, devices):
    rows, columns = gradient.shape
    half = columns // 2
    keep = lax.dynamic_slice_in_dim(gradient, section * half, half, 1)
    send = lax.dynamic_slice_in_dim(gradient, (1 - section) * half, half, 1)
    chip = keep + swapped(send)
    return scattered(chip.reshape(devices, rows // devices, half), dp_index)


def by_rows(gradient, section, dp_index, devices):
    rows, columns = gradient.shape
    chip = between_cores(gradient.reshape(2, rows // 2, columns), section)
    return scattered(chip.reshape(devices, rows // 2 // devices, columns), dp_index)


def body(
    images,
    out_grad,
    live_counts,
    w_reduce0,
    w_short,
    short_gain,
    short_bias,
    w_reduce1,
    w_mid,
    w_expand,
    gain_narrow,
    bias_narrow,
    gain_wide,
    bias_wide,
):
    section = lax.axis_index("section")
    dp_index = lax.axis_index("dp")
    devices = lax.axis_size("dp")
    slots = images.shape[1]
    side = images.shape[2] // 2
    geo = Geometry(slots, side)
    c_in = images.shape[4]
    mid = w_mid.shape[2]
    out = w_expand.shape[2]
    rows = geo.rows
    all_rows = 4 * rows
    place = jnp.stack([dp_index, section]).astype(jnp.int32)

    def bound(kernel, *fixed):
        def run(*refs):
            kernel(geo, *fixed, *refs)

        return run

    own_narrow = jnp.concatenate([gain_narrow[0], bias_narrow[0]], axis=0)
    own_wide = jnp.concatenate([gain_wide, bias_wide], axis=0)
    mid_other = swapped(w_mid)
    expand_other = swapped(w_expand)
    other_narrow = swapped(own_narrow)
    other_wide = swapped(own_wide)
    front = section == 0
    narrow0 = jnp.where(front, own_narrow, other_narrow)
    narrow1 = jnp.where(front, other_narrow, own_narrow)
    wide0 = jnp.where(front, own_wide, other_wide)
    wide1 = jnp.where(front, other_wide, own_wide)
    short = jnp.stack([short_gain, short_bias])

    def dma(number):
        return pltpu.SemaphoreType.DMA((number,))

    x, z1, sent = stage(
        bound(first_kernel),
        (spec((all_rows, c_in), BF16), spec((all_rows, mid)), spec((devices, 2, mid))),
        (place, live_counts, images, w_reduce0),
        "ssaa",
        (
            pltpu.VMEM((slots, 2 * side, 2 * side, c_in), BF16),
            pltpu.VMEM((slots * 2 * side * 16, c_in), BF16),
            pltpu.VMEM((c_in, mid), BF16),
            dma(2),
        ),
    )
    got = exchange(sent)
    zs, stats_s = stage(
        bound(short_kernel),
        (spec((rows, out)), spec((2, out))),
        (place, live_counts, x, w_short),
        "ssav",
        (pltpu.VMEM((rows, c_in), BF16), dma(1)),
    )
    tap_scratch = (pltpu.VMEM((9 * mid, mid), BF16), dma(1))
    taps0, z2, mom1, sent = stage(
        bound(tap_kernel, 4, 0, 0),
        (spec((rows, 9 * mid), BF16), spec((rows, mid)), spec((2, mid)), spec((devices, 2, mid))),
        (place, live_counts, got, z1, narrow0, w_mid, mid_other),
        "ssvvvaa",
        (pltpu.VMEM((all_rows, mid), F32),) + tap_scratch,
    )
    got = exchange(sent)
    expand_scratch = (pltpu.VMEM((mid, out), BF16), dma(1))
    a2, z3, mom2, sent = stage(
        bound(expand_kernel, 0, True),
        (spec((rows, mid), BF16), spec((rows, out)), spec((2, mid)), spec((devices, 4, out))),
        (place, live_counts, got, z2, narrow0, w_expand, expand_other, stats_s),
        "ssvvvaav",
        expand_scratch,
    )
    got = exchange(sent)
    reduce_scratch = (pltpu.VMEM((out, mid), BF16), dma(1))
    joined, u1, mom3, sent = stage(
        bound(join_kernel),
        (spec((rows, out), BF16), spec((rows, mid)), spec((4, out)), spec((devices, 2, mid))),
        (place, live_counts, got, z3, zs, wide0, short, w_reduce1),
        "ssvvvvva",
        reduce_scratch,
    )
    got = exchange(sent)
    taps1, u2, mom4, sent = stage(
        bound(tap_kernel, 1, 1, 0),
        (spec((rows, 9 * mid), BF16), spec((rows, mid)), spec((2, mid)), spec((devices, 2, mid))),
        (place, live_counts, got, u1, narrow1, w_mid, mid_other),
        "ssvvvaa",
        (pltpu.VMEM((rows, mid), F32),) + tap_scratch,
    )
    got = exchange(sent)
    c2, u3, mom5, sent = stage(
        bound(expand_kernel, 1, False),
        (spec((rows, mid), BF16), spec((rows, out)), spec((2, mid)), spec((devices, 2, out))),
        (place, live_counts, got, u2, narrow1, w_expand, expand_other),
        "ssvvvaa",
        expand_scratch,
    )
    got = exchange(sent)
    block_out, g3, mom6, sent = stage(
        bound(turn_kernel),
        (
            spec((1, slots, side, side, out), BF16),
            spec((rows, out)),
            spec((2, out)),
            spec((devices, 2, out)),
        ),
        (place, live_counts, got, u3, joined, wide1, out_grad),
        "ssvvvva",
        (pltpu.VMEM((slots, side, side, out), BF16), pltpu.VMEM((rows, out), F32), dma(1)),
    )
    got = exchange(sent)
    du3, g2, sums6, sent = stage(
        bound(expand_back, 1, False),
        (spec((rows, out), BF16), spec((rows, mid)), spec((2, out)), spec((devices, 2, mid))),
        (place, live_counts, got, g3, u3, mom6, wide1, u2, mom5, narrow1, w_expand, expand_other),
        "ssvvvvvvvvaa",
        expand_scratch,
    )
    got = exchange(sent)
    expand1 = by_columns(weight_product(c2, du3), section, dp_index, devices)
    tap_back_scratch = (pltpu.VMEM((rows, mid), F32),) + tap_scratch
    du2, g1, sums5, sent = stage(
        bound(tap_back, 1, 1),
        (spec((rows, mid), BF16), spec((rows, mid)), spec((2, mid)), spec((devices, 2, mid))),
        (place, live_counts, got, g2, u2, mom5, narrow1, u1, mom4, w_mid, mid_other),
        "ssvvvvvvvaa",
        tap_back_scratch,
    )
    got = exchange(sent)
    mid1 = by_columns(weight_product(taps1, du2), section, dp_index, devices)
    du1, gj, sums4, sent = stage(
        bound(join_back),
        (spec((rows, mid), BF16), spec((rows, out)), spec((2, mid)), spec((devices, 3, out))),
        (place, live_counts, got, g1, u1, mom4, narrow1, w_reduce1, g3, z3, zs, mom3, wide0, short),
        "ssvvvvvavvvvvv",
        reduce_scratch,
    )
    got = exchange(sent)
    reduce1 = by_rows(weight_product(joined, du1), section, dp_index, devices)
    dz3, dzs, g2, sums3, sent = stage(
        bound(expand_back, 0, True),
        (
            spec((rows, out), BF16),
            spec((rows, out), BF16),
            spec((rows, mid)),
            spec((3, out)),
            spec((devices, 2, mid)),
        ),
        (place, live_counts, got, gj, z3, mom3, wide0, zs, short, z2, mom2, narrow0, w_expand, expand_other),
        "ssvvvvvvvvvvaa",
        expand_scratch,
    )
    got = exchange(sent)
    expand0 = by_columns(weight_product(a2, dz3), section, dp_index, devices)
    short_grad = by_rows(weight_product(x[:rows], dzs), section, dp_index, devices)
    dz2, g1, sums2, sent = stage(
        bound(tap_back, 4, 0),
        (spec((rows, mid), BF16), spec((all_rows, mid)), spec((2, mid)), spec((devices, 2, mid))),
        (place, live_counts, got, g2, z2, mom2, narrow0, z1, mom1, w_mid, mid_other),
        "ssvvvvvvvaa",
        tap_back_scratch,
    )
    got = exchange(sent)
    mid0 = by_columns(weight_product(taps0, dz2), section, dp_index, devices)
    dz1, image_grad, sums1 = stage(
        bound(last_kernel),
        (
            spec((all_rows, mid), BF16),
            spec((1, slots, 2 * side, 2 * side, c_in), BF16),
            spec((2, mid)),
        ),
        (place, live_counts, got, g1, z1, mom1, narrow0, w_reduce0, dzs, w_short),
        "ssvvvvvava",
        (
            pltpu.VMEM((c_in, mid), BF16),
            pltpu.VMEM((c_in, out), BF16),
            pltpu.VMEM((all_rows, c_in), BF16),
            dma(2),
        ),
    )
    reduce0 = by_rows(weight_product(x, dz1), section, dp_index, devices)

    def to_owner(front_half, back_half):
        mine = jnp.where(front, front_half, back_half)
        other = swapped(jnp.where(front, back_half, front_half))
        left = jnp.where(front, mine, other)
        right = jnp.where(front, other, mine)
        return jnp.concatenate([left, right], axis=1)

    grad_mid = to_owner(mid0, mid1)
    grad_expand = to_owner(expand0, expand1)
    front_narrow = jnp.stack([sums1, sums2])
    back_narrow = jnp.stack([sums4, sums5])
    narrow_sums = jnp.where(front, front_narrow, back_narrow) + swapped(
        jnp.where(front, back_narrow, front_narrow)
    )
    wide_front = sums3[:2]
    wide_sums = jnp.where(front, wide_front, sums6) + swapped(jnp.where(front, sums6, wide_front))
    short_sums = jnp.stack([sums3[2], sums3[0]])
    width = out // (2 * devices)
    both_short = short_sums + swapped(short_sums)
    short_norm = lax.dynamic_slice_in_dim(both_short, (section * devices + dp_index) * width, width, 1)
    return (
        block_out,
        image_grad,
        reduce0,
        short_grad,
        short_norm,
        reduce1,
        grad_mid[None],
        grad_expand[None],
        narrow_sums[None, :, 1],
        narrow_sums[None, :, 0],
        wide_sums[None, 1],
        wide_sums[None, 0],
    )


def solution(mesh):
    return jax.shard_map(
        body,
        mesh=mesh,
        in_specs=(
            P(None, "dp", None, None, None),
            P(None, "dp", None, None, None),
            P(),
            P(),
            P(),
            P(),
            P(),
            P(),
            P("section", None, None),
            P("section", None, None),
            P("section", None, None),
            P("section", None, None),
            P("section", None),
            P("section", None),
        ),
        out_specs=(
            P("section", "dp", None, None, None),
            P("section", "dp", None, None, None),
            P(("section", "dp"), None),
            P(("section", "dp"), None),
            P(None, ("section", "dp")),
            P(("section", "dp"), None),
            P("section", "dp", None),
            P("section", "dp", None),
            P("section", None, None),
            P("section", None, None),
            P("section", None),
            P("section", None),
        ),
        check_vma=False,
    )
```

```python
import jax
import jax.numpy as jnp
from jax import lax
from jax.experimental import pallas as pl
from jax.experimental.pallas import tpu as pltpu
from jax.sharding import PartitionSpec as P


EPSILON = 1e-05
F32 = jnp.float32
BF16 = jnp.bfloat16
VMEM = pl.BlockSpec(memory_space=pltpu.VMEM)
SMEM = pl.BlockSpec(memory_space=pltpu.SMEM)
ANY = pl.BlockSpec(memory_space=pl.ANY)


def spec(shape, dtype=F32):
    return jax.ShapeDtypeStruct(shape, dtype)


def stage(kernel, outs, args, places, scratch=()):
    kinds = {"v": VMEM, "s": SMEM, "a": ANY}
    return pl.pallas_call(
        kernel,
        out_shape=list(outs),
        in_specs=[kinds[place] for place in places],
        out_specs=[VMEM] * len(outs),
        scratch_shapes=list(scratch),
        compiler_params=pltpu.CompilerParams(vmem_limit_bytes=58 << 20),
    )(*args)


class Geometry:
    def __init__(self, slots, side):
        self.slots = slots
        self.side = side
        self.pitch = side + 1
        self.per_image = self.pitch * self.pitch
        self.rows = slots * self.per_image
        self.pixels = side * side

    def mask(self, start, step, count=None):
        row = start + lax.broadcasted_iota(jnp.int32, (step, 1), 0)
        column = row % self.pitch
        line = (row // self.pitch) % self.pitch
        good = (column < self.side) & (line < self.side)
        if count is not None:
            image = (row // self.per_image) % self.slots
            good = good & (image < count)
        return jnp.where(good, 1.0, 0.0).astype(F32)


def over_rows(rows, step, body, init):
    def one(i, carry):
        return body(pl.multiple_of(i * step, step), carry)

    return lax.fori_loop(0, rows // step, one, init)


def fold_rows(block):
    rows, width = block.shape
    return jnp.sum(block.reshape(rows // 8, 8, width), axis=0)


def step_of(width):
    return 64 if width <= 512 else 16


def local_stats(z_ref, geo, count, planes):
    rows, width = z_ref.shape
    step = step_of(width)
    total = (count * (geo.pixels * planes)).astype(F32)

    def plain(start, acc):
        return acc + fold_rows(z_ref[pl.ds(start, step), :] * geo.mask(start, step, count))

    zero = jnp.zeros((8, width), F32)
    average = jnp.sum(over_rows(rows, step, plain, zero), axis=0, keepdims=True) / total

    def squared(start, acc):
        centered = z_ref[pl.ds(start, step), :] - average
        return acc + fold_rows(centered * centered * geo.mask(start, step, count))

    spread = jnp.sum(over_rows(rows, step, squared, zero), axis=0, keepdims=True)
    return average, spread


def send_rows(out_ref, values):
    for number, value in enumerate(values):
        for device in range(out_ref.shape[0]):
            out_ref[device, number : number + 1, :] = value


def total_of(counts, section, pixels):
    total = counts[0, section]
    for device in range(1, counts.shape[0]):
        total = total + counts[device, section]
    return (total * pixels).astype(F32)


def combined(got_ref, row, counts, section, pixels):
    devices = got_ref.shape[0]
    total = total_of(counts, section, pixels)
    sizes = [(counts[device, section] * pixels).astype(F32) for device in range(devices)]
    average = jnp.zeros((1, got_ref.shape[2]), F32)
    for device in range(devices):
        average = average + sizes[device] * got_ref[device, row : row + 1, :]
    average = average / total
    spread = jnp.zeros_like(average)
    for device in range(devices):
        apart = got_ref[device, row : row + 1, :] - average
        spread = spread + (got_ref[device, row + 1 : row + 2, :] + sizes[device] * (apart * apart))
    return average, lax.rsqrt(spread / total + EPSILON)


def summed(got_ref, row):
    total = got_ref[0, row : row + 1, :]
    for device in range(1, got_ref.shape[0]):
        total = total + got_ref[device, row : row + 1, :]
    return total


def sigmoid(values):
    return 1.0 / (1.0 + jnp.exp(-values))


def slope(values):
    part = sigmoid(values)
    return part * (1.0 + values * (1.0 - part))


class Choice:
    def __init__(self, section, wanted, own, other, target, sem):
        self.mine = section == wanted
        self.copies = (
            pltpu.make_async_copy(own.at[0], target, sem),
            pltpu.make_async_copy(other.at[0], target, sem),
        )

    def start(self):
        @pl.when(self.mine)
        def _():
            self.copies[0].start()

        @pl.when(jnp.logical_not(self.mine))
        def _():
            self.copies[1].start()

    def wait(self):
        @pl.when(self.mine)
        def _():
            self.copies[0].wait()

        @pl.when(jnp.logical_not(self.mine))
        def _():
            self.copies[1].wait()


def split_matrix(geo):
    side = 2 * geo.side
    rows, columns = 4 * geo.per_image, side * 16
    to = lax.broadcasted_iota(jnp.int32, (rows, columns), 0)
    at = lax.broadcasted_iota(jnp.int32, (rows, columns), 1)
    plane = to // geo.per_image
    line = (to // geo.pitch) % geo.pitch
    column = to % geo.pitch
    hit = (
        (line < geo.side)
        & (column < geo.side)
        & (at // 16 == 2 * line + plane // 2)
        & (at % 16 == 2 * column + plane % 2)
    )
    return jnp.where(hit, 1.0, 0.0).astype(BF16)


def join_matrix(geo):
    side = 2 * geo.side
    rows, columns = side * 16, 4 * geo.per_image
    at = lax.broadcasted_iota(jnp.int32, (rows, columns), 0)
    to = lax.broadcasted_iota(jnp.int32, (rows, columns), 1)
    plane = to // geo.per_image
    line = (to // geo.pitch) % geo.pitch
    column = to % geo.pitch
    hit = (
        (line < geo.side)
        & (column < geo.side)
        & (at // 16 == 2 * line + plane // 2)
        & (at % 16 == 2 * column + plane % 2)
    )
    return jnp.where(hit, 1.0, 0.0).astype(BF16)


def dot(left, right):
    return jnp.dot(left, right, preferred_element_type=F32)


def dot_back(left, right):
    return lax.dot_general(left, right, (((1,), (1,)), ((), ())), preferred_element_type=F32)


def rolled(values, shift):
    rows = values.shape[0]
    shift = shift % rows
    return values if shift == 0 else pltpu.roll(values, shift, 0)


def taps_of(stride, pitch):
    found = []
    for tap_row in range(3):
        for column in range(3):
            if stride == 1:
                found.append((0, (tap_row - 1) * pitch + column - 1))
            else:
                plane = 2 * (tap_row != 1) + (column != 1)
                found.append((plane, -pitch * (tap_row == 0) - (column == 0)))
    return found


def first_kernel(geo, place, counts, images, w_any, x_ref, z_ref, sent, raw, padded, weight, sem):
    section = place[1]
    count = counts[place[0], section]
    side = 2 * geo.side
    load = pltpu.make_async_copy(images.at[section], raw, sem.at[0])
    load.start()
    load_weight = pltpu.make_async_copy(w_any, weight, sem.at[1])
    load_weight.start()
    padded[...] = jnp.zeros_like(padded)
    matrix = split_matrix(geo)
    load.wait()
    for image in range(geo.slots):
        for line in range(side):
            at = (image * side + line) * 16
            padded[at : at + side, :] = raw[image, line]
    for image in range(geo.slots):
        flat = padded[image * side * 16 : (image + 1) * side * 16, :]
        parts = dot(matrix, flat).astype(BF16)
        for plane in range(4):
            at = plane * geo.rows + image * geo.per_image
            x_ref[at : at + geo.per_image, :] = parts[
                plane * geo.per_image : (plane + 1) * geo.per_image
            ]
    load_weight.wait()
    for plane in range(4):
        at = plane * geo.rows
        z_ref[at : at + geo.rows, :] = dot(x_ref[at : at + geo.rows, :], weight[...])
    send_rows(sent, local_stats(z_ref, geo, count, 4))


def short_kernel(geo, place, counts, x_any, weight, z_ref, stats, x_vmem, sem):
    count = counts[place[0], place[1]]
    load = pltpu.make_async_copy(x_any.at[pl.ds(0, geo.rows)], x_vmem, sem.at[0])
    load.start()
    load.wait()
    z_ref[...] = dot(x_vmem[...], weight[...])
    average, spread = local_stats(z_ref, geo, count, 1)
    stats[0:1, :] = average
    stats[1:2, :] = spread


def tap_kernel(geo, planes, block, which, place, counts, got, z_in, narrow, own, other, taps, z_ref, moments, sent,
               active, weight, sem):
    section = place[1]
    count = counts[place[0], section]
    choice = Choice(section, block, own, other, weight, sem.at[0])
    choice.start()
    average, inverse = combined(got, 0, counts, section, geo.pixels * planes)
    moments[0:1, :] = average
    moments[1:2, :] = inverse
    gain = narrow[which : which + 1, :] * inverse
    offset = narrow[2 + which : 3 + which, :]

    def activate(start, carry):
        pre = (z_in[pl.ds(start, 64), :] - average) * gain + offset
        active[pl.ds(start, 64), :] = pre * sigmoid(pre) * geo.mask(start, 64)
        return carry

    over_rows(z_in.shape[0], 64, activate, 0)
    width = z_in.shape[1]
    for tap, (plane, shift) in enumerate(taps_of(2 if planes == 4 else 1, geo.pitch)):
        block_rows = active[plane * geo.rows : (plane + 1) * geo.rows, :]
        taps[:, tap * width : (tap + 1) * width] = rolled(block_rows, -shift).astype(BF16)
    choice.wait()
    z_ref[...] = dot(taps[...], weight[...])
    send_rows(sent, local_stats(z_ref, geo, count, 1))


def expand_kernel(geo, block, extra, place, counts, got, z_in, narrow, own, other, *rest):
    if extra:
        stats, a_ref, z_ref, moments, sent, weight, sem = rest
    else:
        a_ref, z_ref, moments, sent, weight, sem = rest
    section = place[1]
    count = counts[place[0], section]
    choice = Choice(section, block, own, other, weight, sem.at[0])
    choice.start()
    average, inverse = combined(got, 0, counts, section, geo.pixels)
    moments[0:1, :] = average
    moments[1:2, :] = inverse
    gain = narrow[1:2, :] * inverse
    offset = narrow[3:4, :]

    def activate(start, carry):
        pre = (z_in[pl.ds(start, 64), :] - average) * gain + offset
        a_ref[pl.ds(start, 64), :] = (pre * sigmoid(pre)).astype(BF16)
        return carry

    over_rows(geo.rows, 64, activate, 0)
    choice.wait()
    z_ref[...] = dot(a_ref[...], weight[...])
    average, spread = local_stats(z_ref, geo, count, 1)
    if extra:
        send_rows(sent, (average, spread, stats[0:1, :], stats[1:2, :]))
    else:
        send_rows(sent, (average, spread))


def join_kernel(geo, place, counts, got, z3, zs, wide, short, w_any, joined, u_ref, moments, sent, weight, sem):
    section = place[1]
    count = counts[place[0], section]
    load = pltpu.make_async_copy(w_any, weight, sem.at[0])
    load.start()
    average_c, inverse_c = combined(got, 0, counts, section, geo.pixels)
    average_s, inverse_s = combined(got, 2, counts, section, geo.pixels)
    for number, value in enumerate((average_c, inverse_c, average_s, inverse_s)):
        moments[number : number + 1, :] = value
    gain_c = wide[0:1, :] * inverse_c
    gain_s = short[0:1, :] * inverse_s
    offset = wide[1:2, :] + short[1:2, :]

    def activate(start, carry):
        rows = pl.ds(start, 16)
        pre = (z3[rows, :] - average_c) * gain_c + (zs[rows, :] - average_s) * gain_s + offset
        joined[rows, :] = (pre * sigmoid(pre)).astype(BF16)
        return carry

    over_rows(geo.rows, 16, activate, 0)
    load.wait()
    u_ref[...] = dot(joined[...], weight[...])
    send_rows(sent, local_stats(u_ref, geo, count, 1))


def turn_kernel(geo, place, counts, got, u3, joined, wide, out_grad, out_ref, g_ref, moments, sent, raw, flat, sem):
    section = place[1]
    count = counts[place[0], section]
    load = pltpu.make_async_copy(out_grad.at[section], raw, sem.at[0])
    load.start()
    average, inverse = combined(got, 0, counts, section, geo.pixels)
    moments[0:1, :] = average
    moments[1:2, :] = inverse
    g_ref[...] = jnp.zeros_like(g_ref)
    load.wait()
    for image in range(geo.slots):
        for line in range(geo.side):
            at = image * geo.per_image + line * geo.pitch
            g_ref[at : at + geo.side, :] = raw[image, line].astype(F32)
    weight = wide[0:1, :]
    offset = wide[1:2, :]

    def activate(start, carry):
        plain, scaled = carry
        rows = pl.ds(start, 16)
        normed = (u3[rows, :] - average) * inverse
        pre = normed * weight + offset + joined[rows, :].astype(F32)
        part = sigmoid(pre)
        flat[rows, :] = pre * part
        upstream = g_ref[rows, :] * geo.mask(start, 16, count) * (part * (1.0 + pre * (1.0 - part)))
        g_ref[rows, :] = upstream
        return plain + fold_rows(upstream), scaled + fold_rows(upstream * normed)

    zero = jnp.zeros((8, u3.shape[1]), F32)
    plain, scaled = over_rows(geo.rows, 16, activate, (zero, zero))
    send_rows(sent, (jnp.sum(plain, axis=0, keepdims=True), jnp.sum(scaled, axis=0, keepdims=True)))
    for image in range(geo.slots):
        for line in range(geo.side):
            at = image * geo.per_image + line * geo.pitch
            out_ref[0, image, line] = flat[at : at + geo.side, :].astype(BF16)


def norm_grad(geo, rows_of, z_ref, g_ref, average, inverse, gain, plain, scaled, total, count, out_ref):
    width = z_ref.shape[1]
    step = step_of(width)
    factor = gain * inverse
    plain_part = plain / total
    scaled_part = scaled / total * inverse

    def one(start, carry):
        rows = pl.ds(start, step)
        centered = z_ref[rows, :] - average
        value = factor * (g_ref[rows, :] - plain_part - centered * scaled_part)
        value = jnp.where(geo.mask(start, step, count) > 0.0, value, 0.0)
        out_ref[rows, :] = value.astype(out_ref.dtype)
        return carry

    over_rows(rows_of, step, one, 0)


def silu_back(geo, z_ref, average, inverse, gain, offset, g_ref):
    rows_of, width = z_ref.shape
    step = step_of(width)

    def one(start, carry):
        plain, scaled = carry
        rows = pl.ds(start, step)
        normed = (z_ref[rows, :] - average) * inverse
        upstream = g_ref[rows, :] * slope(normed * gain + offset)
        upstream = jnp.where(geo.mask(start, step) > 0.0, upstream, 0.0)
        g_ref[rows, :] = upstream
        return plain + fold_rows(upstream), scaled + fold_rows(upstream * normed)

    zero = jnp.zeros((8, width), F32)
    plain, scaled = over_rows(rows_of, step, one, (zero, zero))
    return jnp.sum(plain, axis=0, keepdims=True), jnp.sum(scaled, axis=0, keepdims=True)


def expand_back(geo, block, two, place, counts, got, g_in, z3, mom3, wide, *rest):
    if two:
        zs, short, z2, mom2, narrow, own, other, dv, dvs, g_ref, sums, sent, weight, sem = rest
    else:
        z2, mom2, narrow, own, other, dv, g_ref, sums, sent, weight, sem = rest
    section = place[1]
    count = counts[place[0], section]
    choice = Choice(section, block, own, other, weight, sem.at[0])
    choice.start()
    total = total_of(counts, section, geo.pixels)
    plain, scaled = summed(got, 0), summed(got, 1)
    sums[0:1, :] = plain
    sums[1:2, :] = scaled
    norm_grad(geo, geo.rows, z3, g_in, mom3[0:1, :], mom3[1:2, :], wide[0:1, :], plain, scaled, total, count, dv)
    if two:
        scaled = summed(got, 2)
        sums[2:3, :] = scaled
        norm_grad(geo, geo.rows, zs, g_in, mom3[2:3, :], mom3[3:4, :], short[0:1, :], plain, scaled, total, count, dvs)
    choice.wait()
    g_ref[...] = dot_back(dv[...], weight[...])
    send_rows(
        sent, silu_back(geo, z2, mom2[0:1, :], mom2[1:2, :], narrow[1:2, :], narrow[3:4, :], g_ref)
    )


def tap_back(geo, planes, block, place, counts, got, g_in, z2, mom2, narrow, z1, mom1, own, other, dv, g_ref, sums, sent,
             wide_dv, weight, sem):
    section = place[1]
    count = counts[place[0], section]
    choice = Choice(section, block, own, other, weight, sem.at[0])
    choice.start()
    total = total_of(counts, section, geo.pixels)
    plain, scaled = summed(got, 0), summed(got, 1)
    sums[0:1, :] = plain
    sums[1:2, :] = scaled
    norm_grad(
        geo, geo.rows, z2, g_in, mom2[0:1, :], mom2[1:2, :], narrow[1:2, :], plain, scaled, total, count, wide_dv
    )
    values = wide_dv[...]
    dv[...] = values.astype(BF16)
    choice.wait()
    width = z1.shape[1]
    ready = {}
    done = [False] * planes
    for tap, (plane, shift) in enumerate(taps_of(2 if planes == 4 else 1, geo.pitch)):
        if shift not in ready:
            ready[shift] = rolled(values, shift).astype(BF16)
        product = dot_back(ready[shift], weight[tap * width : (tap + 1) * width, :])
        rows = slice(plane * geo.rows, (plane + 1) * geo.rows)
        if done[plane]:
            g_ref[rows, :] += product
        else:
            g_ref[rows, :] = product
        done[plane] = True
    send_rows(
        sent, silu_back(geo, z1, mom1[0:1, :], mom1[1:2, :], narrow[0:1, :], narrow[2:3, :], g_ref)
    )


def join_back(geo, place, counts, got, g_in, u1, mom4, narrow, w_any, g3, z3, zs, mom3, wide, short, dv, g_ref, sums, sent,
              weight, sem):
    section = place[1]
    count = counts[place[0], section]
    load = pltpu.make_async_copy(w_any, weight, sem.at[0])
    load.start()
    total = total_of(counts, section, geo.pixels)
    plain, scaled = summed(got, 0), summed(got, 1)
    sums[0:1, :] = plain
    sums[1:2, :] = scaled
    norm_grad(geo, geo.rows, u1, g_in, mom4[0:1, :], mom4[1:2, :], narrow[0:1, :], plain, scaled, total, count, dv)
    load.wait()
    g_ref[...] = dot_back(dv[...], weight[...])
    average_c, inverse_c = mom3[0:1, :], mom3[1:2, :]
    average_s, inverse_s = mom3[2:3, :], mom3[3:4, :]
    gain_c, gain_s = wide[0:1, :], short[0:1, :]
    offset = wide[1:2, :] + short[1:2, :]

    def one(start, carry):
        plain, scaled_c, scaled_s = carry
        rows = pl.ds(start, 16)
        normed_c = (z3[rows, :] - average_c) * inverse_c
        normed_s = (zs[rows, :] - average_s) * inverse_s
        arrived = (g_ref[rows, :] + g3[rows, :]).astype(BF16).astype(F32)
        upstream = arrived * slope(normed_c * gain_c + normed_s * gain_s + offset)
        upstream = jnp.where(geo.mask(start, 16) > 0.0, upstream, 0.0)
        g_ref[rows, :] = upstream
        return (
            plain + fold_rows(upstream),
            scaled_c + fold_rows(upstream * normed_c),
            scaled_s + fold_rows(upstream * normed_s),
        )

    zero = jnp.zeros((8, z3.shape[1]), F32)
    results = over_rows(geo.rows, 16, one, (zero, zero, zero))
    send_rows(sent, [jnp.sum(value, axis=0, keepdims=True) for value in results])


def last_kernel(geo, place, counts, got, g_in, z1, mom1, narrow, w_any, dvs, ws_any, dv, out_ref, sums, weight, weight_s,
                flat, sem):
    section = place[1]
    count = counts[place[0], section]
    load = pltpu.make_async_copy(w_any, weight, sem.at[0])
    load.start()
    load_s = pltpu.make_async_copy(ws_any, weight_s, sem.at[1])
    load_s.start()
    side = 2 * geo.side
    total = total_of(counts, section, geo.pixels * 4)
    plain, scaled = summed(got, 0), summed(got, 1)
    sums[0:1, :] = plain
    sums[1:2, :] = scaled
    norm_grad(
        geo, 4 * geo.rows, z1, g_in, mom1[0:1, :], mom1[1:2, :], narrow[0:1, :], plain, scaled, total, count, dv
    )
    load.wait()
    for plane in range(1, 4):
        at = plane * geo.rows
        flat[at : at + geo.rows, :] = dot_back(dv[at : at + geo.rows, :], weight[...]).astype(BF16)
    load_s.wait()
    flat[0 : geo.rows, :] = (
        dot_back(dv[0 : geo.rows, :], weight[...]) + dot_back(dvs[...], weight_s[...])
    ).astype(BF16)
    matrix = join_matrix(geo)
    for image in range(geo.slots):
        parts = []
        for plane in range(4):
            at = plane * geo.rows + image * geo.per_image
            parts.append(flat[at : at + geo.per_image, :])
        natural = dot(matrix, jnp.concatenate(parts, axis=0)).astype(BF16)
        for line in range(side):
            out_ref[0, image, line] = natural[line * 16 : line * 16 + side]


def dot_rows(left, right):
    return lax.dot_general(left, right, (((0,), (0,)), ((), ())), preferred_element_type=F32)


def exchange(sent):
    return lax.all_to_all(sent, "dp", 0, 0)


def swapped(value):
    return lax.ppermute(value, "section", [(0, 1), (1, 0)])


def across(value, mask):
    return lax.ppermute(value, "dp", [(i, i ^ mask) for i in range(lax.axis_size("dp"))])


class Piece:
    def __init__(self, rows, columns, devices, split, width):
        self.rows = rows
        self.columns = columns
        self.split = split
        self.width = width
        if split == "owner":
            self.height = rows // (2 * devices)
            self.blocks = columns // width
        elif split == "rows":
            self.height = rows // (2 * devices)
            self.blocks = columns // width
        else:
            self.height = rows // devices
            self.blocks = columns // 2 // width
        self.lines = self.height * self.blocks

    def at(self, owner, half, block):
        if self.split == "owner":
            return half * (self.rows // 2) + owner * self.height, block * self.width
        if self.split == "rows":
            return (2 * owner + half) * self.height, block * self.width
        return owner * self.height, half * (self.columns // 2) + block * self.width


def pieces_kernel(pieces, place, *refs):
    count = len(pieces)
    inputs = refs[: 2 * count]
    keep, send, total = refs[2 * count :]
    me, section = place[0], place[1]
    line = 0
    for number, piece in enumerate(pieces):
        left, right = inputs[2 * number], inputs[2 * number + 1]
        total[0 : piece.rows, 0 : piece.columns] = dot_rows(left[0 : right.shape[0], :], right[...])
        for step in range(keep.shape[0]):
            owner = me ^ step
            for out, half in ((keep, section), (send, 1 - section)):
                for block in range(piece.blocks):
                    row, column = piece.at(owner, half, block)
                    row = pl.multiple_of(row, piece.height)
                    if piece.split == "columns":
                        column = pl.multiple_of(column, piece.width)
                    value = total[pl.ds(row, piece.height), pl.ds(column, piece.width)]
                    to = line + block * piece.height
                    out[step, to : to + piece.height, :] = value.astype(BF16)
        line += piece.lines


class Reduction:
    def __init__(self, place, pieces, pairs):
        devices = lax.axis_size("dp")
        lines = sum(piece.lines for piece in pieces)
        width = pieces[0].width
        shape = spec((devices, lines, width), BF16)
        self.pieces = pieces
        args = [place]
        for left, right in pairs:
            args += [left, right]
        tall = max(piece.rows for piece in pieces)
        wide = max(piece.columns for piece in pieces)
        self.keep, self.out = stage(
            lambda *refs: pieces_kernel(pieces, *refs),
            (shape, shape),
            args,
            "s" + "v" * (len(args) - 1),
            (pltpu.VMEM((tall, wide), F32),),
        )
        self.step = 0

    def advance(self):
        step = self.step
        self.step += 1
        if step == 0:
            self.sent = (self.out,)
            self.moves = (swapped,)
            self.rest = (self.keep,)
        elif step == 1:
            total = (self.rest[0] + self.got[0]).reshape((-1, 2, 2) + self.keep.shape[1:])
            half = total.shape[-1] // 2
            self.sent = (total[:, :, 1, :, :half], total[:, 1, :, :, half:])
            self.rest = (total[:, :, 0, :, :half], total[:, 0, :, :, half:])
            self.moves = (lambda v: across(v, 1), lambda v: across(v, 2))
        elif step == 2:
            totals = [rest + got for rest, got in zip(self.rest, self.got)]
            self.sent = (totals[0][:, 1], totals[1][:, 1])
            self.rest = (totals[0][:, 0], totals[1][:, 0])
            self.moves = (lambda v: across(v, 2), lambda v: across(v, 1))
        elif step == 3:
            total = jnp.concatenate([rest + got for rest, got in zip(self.rest, self.got)], axis=-1)
            self.rest = (total[0],)
            self.sent = tuple(total[number] for number in range(1, total.shape[0]))
            self.moves = tuple(
                lambda v, number=number: across(v, number << 2) for number in range(1, total.shape[0])
            )
        self.fly()

    def fly(self):
        self.got = tuple(move(value) for move, value in zip(self.moves, self.sent))

    def finish(self):
        total = self.rest[0].astype(F32)
        for value in self.got:
            total = total + value.astype(F32)
        results = []
        line = 0
        for piece in self.pieces:
            blocks = [
                total[line + block * piece.height : line + (block + 1) * piece.height]
                for block in range(piece.blocks)
            ]
            results.append(blocks[0] if len(blocks) == 1 else jnp.concatenate(blocks, axis=1))
            line += piece.lines
        return results


def body(
    images,
    out_grad,
    live_counts,
    w_reduce0,
    w_short,
    short_gain,
    short_bias,
    w_reduce1,
    w_mid,
    w_expand,
    gain_narrow,
    bias_narrow,
    gain_wide,
    bias_wide,
):
    section = lax.axis_index("section")
    dp_index = lax.axis_index("dp")
    devices = lax.axis_size("dp")
    slots = images.shape[1]
    side = images.shape[2] // 2
    geo = Geometry(slots, side)
    c_in = images.shape[4]
    mid = w_mid.shape[2]
    out = w_expand.shape[2]
    rows = geo.rows
    all_rows = 4 * rows
    place = jnp.stack([dp_index, section]).astype(jnp.int32)

    def bound(kernel, *fixed):
        def run(*refs):
            kernel(geo, *fixed, *refs)

        return run

    own_narrow = jnp.concatenate([gain_narrow[0], bias_narrow[0]], axis=0)
    own_wide = jnp.concatenate([gain_wide, bias_wide], axis=0)
    mid_other = swapped(w_mid)
    expand_other = swapped(w_expand)
    other_narrow = swapped(own_narrow)
    other_wide = swapped(own_wide)
    front = section == 0
    narrow0 = jnp.where(front, own_narrow, other_narrow)
    narrow1 = jnp.where(front, other_narrow, own_narrow)
    wide0 = jnp.where(front, own_wide, other_wide)
    wide1 = jnp.where(front, other_wide, own_wide)
    short = jnp.stack([short_gain, short_bias])

    def dma(number):
        return pltpu.SemaphoreType.DMA((number,))

    x, z1, sent = stage(
        bound(first_kernel),
        (spec((all_rows, c_in), BF16), spec((all_rows, mid)), spec((devices, 2, mid))),
        (place, live_counts, images, w_reduce0),
        "ssaa",
        (
            pltpu.VMEM((slots, 2 * side, 2 * side, c_in), BF16),
            pltpu.VMEM((slots * 2 * side * 16, c_in), BF16),
            pltpu.VMEM((c_in, mid), BF16),
            dma(2),
        ),
    )
    got = exchange(sent)
    zs, stats_s = stage(
        bound(short_kernel),
        (spec((rows, out)), spec((2, out))),
        (place, live_counts, x, w_short),
        "ssav",
        (pltpu.VMEM((rows, c_in), BF16), dma(1)),
    )
    tap_scratch = (pltpu.VMEM((9 * mid, mid), BF16), dma(1))
    taps0, z2, mom1, sent = stage(
        bound(tap_kernel, 4, 0, 0),
        (spec((rows, 9 * mid), BF16), spec((rows, mid)), spec((2, mid)), spec((devices, 2, mid))),
        (place, live_counts, got, z1, narrow0, w_mid, mid_other),
        "ssvvvaa",
        (pltpu.VMEM((all_rows, mid), F32),) + tap_scratch,
    )
    got = exchange(sent)
    expand_scratch = (pltpu.VMEM((mid, out), BF16), dma(1))
    a2, z3, mom2, sent = stage(
        bound(expand_kernel, 0, True),
        (spec((rows, mid), BF16), spec((rows, out)), spec((2, mid)), spec((devices, 4, out))),
        (place, live_counts, got, z2, narrow0, w_expand, expand_other, stats_s),
        "ssvvvaav",
        expand_scratch,
    )
    got = exchange(sent)
    reduce_scratch = (pltpu.VMEM((out, mid), BF16), dma(1))
    joined, u1, mom3, sent = stage(
        bound(join_kernel),
        (spec((rows, out), BF16), spec((rows, mid)), spec((4, out)), spec((devices, 2, mid))),
        (place, live_counts, got, z3, zs, wide0, short, w_reduce1),
        "ssvvvvva",
        reduce_scratch,
    )
    got = exchange(sent)
    taps1, u2, mom4, sent = stage(
        bound(tap_kernel, 1, 1, 0),
        (spec((rows, 9 * mid), BF16), spec((rows, mid)), spec((2, mid)), spec((devices, 2, mid))),
        (place, live_counts, got, u1, narrow1, w_mid, mid_other),
        "ssvvvaa",
        (pltpu.VMEM((rows, mid), F32),) + tap_scratch,
    )
    got = exchange(sent)
    c2, u3, mom5, sent = stage(
        bound(expand_kernel, 1, False),
        (spec((rows, mid), BF16), spec((rows, out)), spec((2, mid)), spec((devices, 2, out))),
        (place, live_counts, got, u2, narrow1, w_expand, expand_other),
        "ssvvvaa",
        expand_scratch,
    )
    got = exchange(sent)
    block_out, g3, mom6, sent = stage(
        bound(turn_kernel),
        (
            spec((1, slots, side, side, out), BF16),
            spec((rows, out)),
            spec((2, out)),
            spec((devices, 2, out)),
        ),
        (place, live_counts, got, u3, joined, wide1, out_grad),
        "ssvvvva",
        (pltpu.VMEM((slots, side, side, out), BF16), pltpu.VMEM((rows, out), F32), dma(1)),
    )
    got = exchange(sent)
    du3, g2, sums6, sent = stage(
        bound(expand_back, 1, False),
        (spec((rows, out), BF16), spec((rows, mid)), spec((2, out)), spec((devices, 2, mid))),
        (place, live_counts, got, g3, u3, mom6, wide1, u2, mom5, narrow1, w_expand, expand_other),
        "ssvvvvvvvvaa",
        expand_scratch,
    )
    got = exchange(sent)
    tap_back_scratch = (pltpu.VMEM((rows, mid), F32),) + tap_scratch
    du2, g1, sums5, sent = stage(
        bound(tap_back, 1, 1),
        (spec((rows, mid), BF16), spec((rows, mid)), spec((2, mid)), spec((devices, 2, mid))),
        (place, live_counts, got, g2, u2, mom5, narrow1, u1, mom4, w_mid, mid_other),
        "ssvvvvvvvaa",
        tap_back_scratch,
    )
    got = exchange(sent)
    piece_mid = Piece(9 * mid, mid, devices, "rows", mid)
    piece_expand = Piece(mid, out, devices, "columns", mid)
    piece_reduce1 = Piece(out, mid, devices, "owner", mid)
    piece_short = Piece(c_in, out, devices, "owner", mid)
    piece_reduce0 = Piece(c_in, mid, devices, "owner", mid)
    heights = [piece.height for piece in (piece_mid, piece_expand, piece_reduce1, piece_short, piece_reduce0)]
    packed = devices == 16 and all(height % 16 == 0 for height in heights)

    def tied(got, *reductions):
        values = lax.optimization_barrier((got,) + tuple(one.sent for one in reductions))
        for one, sent in zip(reductions, values[1:]):
            one.sent = sent
            one.fly()
        return values[0]

    if packed:
        first = Reduction(place, (piece_expand, piece_mid), ((c2, du3), (taps1, du2)))
        first.advance()
        got = tied(got, first)
    du1, gj, sums4, sent = stage(
        bound(join_back),
        (spec((rows, mid), BF16), spec((rows, out)), spec((2, mid)), spec((devices, 3, out))),
        (place, live_counts, got, g1, u1, mom4, narrow1, w_reduce1, g3, z3, zs, mom3, wide0, short),
        "ssvvvvvavvvvvv",
        reduce_scratch,
    )
    got = exchange(sent)
    if packed:
        first.advance()
        got = tied(got, first)
    dz3, dzs, g2, sums3, sent = stage(
        bound(expand_back, 0, True),
        (
            spec((rows, out), BF16),
            spec((rows, out), BF16),
            spec((rows, mid)),
            spec((3, out)),
            spec((devices, 2, mid)),
        ),
        (place, live_counts, got, gj, z3, mom3, wide0, zs, short, z2, mom2, narrow0, w_expand, expand_other),
        "ssvvvvvvvvvvaa",
        expand_scratch,
    )
    got = exchange(sent)
    if packed:
        first.advance()
        second = Reduction(
            place, (piece_reduce1, piece_expand, piece_short), ((joined, du1), (a2, dz3), (x, dzs))
        )
        second.advance()
        got = tied(got, first, second)
    dz2, g1, sums2, sent = stage(
        bound(tap_back, 4, 0),
        (spec((rows, mid), BF16), spec((all_rows, mid)), spec((2, mid)), spec((devices, 2, mid))),
        (place, live_counts, got, g2, z2, mom2, narrow0, z1, mom1, w_mid, mid_other),
        "ssvvvvvvvaa",
        tap_back_scratch,
    )
    got = exchange(sent)
    if packed:
        first.advance()
        second.advance()
        third = Reduction(place, (piece_mid,), ((taps0, dz2),))
        third.advance()
        got = tied(got, first, second, third)
    dz1, image_grad, sums1 = stage(
        bound(last_kernel),
        (
            spec((all_rows, mid), BF16),
            spec((1, slots, 2 * side, 2 * side, c_in), BF16),
            spec((2, mid)),
        ),
        (place, live_counts, got, g1, z1, mom1, narrow0, w_reduce0, dzs, w_short),
        "ssvvvvvava",
        (
            pltpu.VMEM((c_in, mid), BF16),
            pltpu.VMEM((c_in, out), BF16),
            pltpu.VMEM((all_rows, c_in), BF16),
            dma(2),
        ),
    )
    wide_front = sums3[:2]
    wide_sent = jnp.concatenate([jnp.where(front, sums6, wide_front), sums3[0:1], sums3[2:3]], axis=0)
    wide_got = swapped(wide_sent)
    wide_sums = jnp.where(front, wide_front, sums6) + wide_got[:2]
    width = out // (2 * devices)
    both_short = jnp.stack([sums3[2] + wide_got[3], sums3[0] + wide_got[2]])
    short_norm = lax.dynamic_slice_in_dim(both_short, (section * devices + dp_index) * width, width, 1)
    front_narrow = jnp.stack([sums1, sums2])
    back_narrow = jnp.stack([sums4, sums5])
    narrow_sums = jnp.where(front, front_narrow, back_narrow) + swapped(
        jnp.where(front, back_narrow, front_narrow)
    )
    if packed:
        second.advance()
        third.advance()
        fourth = Reduction(place, (piece_reduce0,), ((x, dz1),))
        fourth.advance()
        expand1, mid1 = first.finish()
        second.advance()
        third.advance()
        fourth.advance()
        reduce1, expand0, short_grad = second.finish()
        third.advance()
        fourth.advance()
        (mid0,) = third.finish()
        fourth.advance()
        (reduce0,) = fourth.finish()

        def to_owner(front_half, back_half, axis):
            mine = jnp.where(front, front_half, back_half)
            other = swapped(jnp.where(front, back_half, front_half))
            first_half = jnp.where(front, mine, other)
            second_half = jnp.where(front, other, mine)
            return jnp.concatenate([first_half, second_half], axis=axis)

        grad_mid = to_owner(mid0, mid1, 0)
        grad_expand = to_owner(expand0, expand1, 1)
    else:

        def product(left, right):
            return dot_rows(left, right).astype(BF16)

        def of_block(front_grad, back_grad):
            mine = jnp.where(front, front_grad, back_grad)
            both = mine + swapped(jnp.where(front, back_grad, front_grad))
            return lax.psum_scatter(both, "dp", scatter_dimension=0, tiled=True).astype(F32)

        def of_both(grad):
            return lax.psum_scatter(grad, ("section", "dp"), scatter_dimension=0, tiled=True).astype(F32)

        grad_mid = of_block(product(taps0, dz2), product(taps1, du2))
        grad_expand = of_block(product(a2, dz3), product(c2, du3))
        reduce1 = of_both(product(joined, du1))
        short_grad = of_both(product(x[:rows], dzs))
        reduce0 = of_both(product(x, dz1))
    return (
        block_out,
        image_grad,
        reduce0,
        short_grad,
        short_norm,
        reduce1,
        grad_mid[None],
        grad_expand[None],
        narrow_sums[None, :, 1],
        narrow_sums[None, :, 0],
        wide_sums[None, 1],
        wide_sums[None, 0],
    )


def solution(mesh):
    return jax.shard_map(
        body,
        mesh=mesh,
        in_specs=(
            P(None, "dp", None, None, None),
            P(None, "dp", None, None, None),
            P(),
            P(),
            P(),
            P(),
            P(),
            P(),
            P("section", None, None),
            P("section", None, None),
            P("section", None, None),
            P("section", None, None),
            P("section", None),
            P("section", None),
        ),
        out_specs=(
            P("section", "dp", None, None, None),
            P("section", "dp", None, None, None),
            P(("section", "dp"), None),
            P(("section", "dp"), None),
            P(None, ("section", "dp")),
            P(("section", "dp"), None),
            P("section", "dp", None),
            P("section", "dp", None),
            P("section", None, None),
            P("section", None, None),
            P("section", None),
            P("section", None),
        ),
        check_vma=False,
    )
```

```python
import jax
import jax.numpy as jnp
from jax import lax
from jax.experimental import pallas as pl
from jax.experimental.pallas import tpu as pltpu
from jax.sharding import PartitionSpec as P


EPSILON = 1e-05
F32 = jnp.float32
BF16 = jnp.bfloat16
VMEM = pl.BlockSpec(memory_space=pltpu.VMEM)
SMEM = pl.BlockSpec(memory_space=pltpu.SMEM)
ANY = pl.BlockSpec(memory_space=pl.ANY)


def spec(shape, dtype=F32):
    return jax.ShapeDtypeStruct(shape, dtype)


class Late:
    def __init__(self, source, target, sem):
        self.copy = pltpu.make_async_copy(source, target, sem)
        self.copy.start()
        self.target = target
        self.waiting = True

    def get(self):
        if self.waiting:
            self.copy.wait()
            self.waiting = False
        return self.target


class Out:
    def __init__(self, buffer, target, sem):
        self.ref = buffer
        self.copy = pltpu.make_async_copy(buffer, target, sem)
        self.sent = False

    def send(self):
        self.copy.start()
        self.sent = True


def stage(kernel, outs, out_places, args, places, scratch=()):
    kinds = {"v": VMEM, "g": VMEM, "s": SMEM, "a": ANY, "d": ANY}
    late = [n for n, kind in enumerate(places) if kind == "d"]
    late_out = [n for n, kind in enumerate(out_places) if kind == "d"]
    buffers = [pltpu.VMEM(args[n].shape, args[n].dtype) for n in late]
    buffers += [pltpu.VMEM(outs[n].shape, outs[n].dtype) for n in late_out]
    args = [
        pltpu.with_memory_space_constraint(arg, pltpu.VMEM) if kind == "g" else arg
        for arg, kind in zip(args, places)
    ]

    def run(*refs):
        inputs = list(refs[: len(args)])
        results = list(refs[len(args) : len(args) + len(outs)])
        rest = refs[len(args) + len(outs) :]
        own, held, sem = rest[: len(scratch)], rest[len(scratch) : -1], rest[-1]
        for place, n in enumerate(late):
            inputs[n] = Late(inputs[n], held[place], sem.at[place])
        waiting = []
        for place, n in enumerate(late_out):
            place += len(late)
            results[n] = Out(held[place], results[n], sem.at[place])
            waiting.append(results[n])
        kernel(*inputs, *results, *own)
        for one in inputs:
            if isinstance(one, Late):
                one.get()
        for one in waiting:
            if not one.sent:
                one.send()
        for one in waiting:
            one.copy.wait()

    return pl.pallas_call(
        run,
        out_shape=list(outs),
        in_specs=[kinds[kind] for kind in places],
        out_specs=[kinds[kind] for kind in out_places],
        scratch_shapes=list(scratch) + buffers + [pltpu.SemaphoreType.DMA((max(1, len(buffers)),))],
        compiler_params=pltpu.CompilerParams(vmem_limit_bytes=58 << 20),
    )(*args)


def split(value, size):
    if size & (size - 1) == 0:
        return value >> (size.bit_length() - 1), value & (size - 1)
    return value // size, value % size


class Geometry:
    def __init__(self, slots, side):
        self.slots = slots
        self.side = side
        self.pitch = side + 1
        self.line = self.pitch * slots
        self.rows = self.pitch * self.line
        self.pixels = side * side

    def mask(self, start, step, width, count=None):
        row = start + lax.broadcasted_iota(jnp.int32, (step, 128), 0)
        position, image = split(row, self.slots)
        line, column = split(position, self.pitch)
        line = split(line, self.pitch)[1]
        good = (column < self.side) & (line < self.side)
        if count is not None:
            good = good & (image < count)
        value = jnp.where(good, 1.0, 0.0).astype(F32)
        return jnp.concatenate([value] * (width // 128), axis=1) if width > 128 else value


def over_rows(rows, step, body, init):
    def one(i, carry):
        return body(pl.multiple_of(i * step, step), carry)

    return lax.fori_loop(0, rows // step, one, init)


def fold_rows(block):
    rows, width = block.shape
    return jnp.sum(block.reshape(rows // 8, 8, width), axis=0)


def step_of(width):
    return 64 if width <= 512 else 16


def local_stats(z_ref, geo, count, planes):
    rows, width = z_ref.shape
    step = step_of(width)
    total = (count * (geo.pixels * planes)).astype(F32)

    def plain(start, acc):
        return acc + fold_rows(z_ref[pl.ds(start, step), :] * geo.mask(start, step, width, count))

    zero = jnp.zeros((8, width), F32)
    average = jnp.sum(over_rows(rows, step, plain, zero), axis=0, keepdims=True) / total

    def squared(start, acc):
        centered = z_ref[pl.ds(start, step), :] - average
        return acc + fold_rows(centered * centered * geo.mask(start, step, width, count))

    spread = jnp.sum(over_rows(rows, step, squared, zero), axis=0, keepdims=True)
    return average, spread


def send_rows(out_ref, values):
    for number, value in enumerate(values):
        for device in range(out_ref.shape[0]):
            out_ref[device, number : number + 1, :] = value


def total_of(counts, section, pixels):
    total = counts[0, section]
    for device in range(1, counts.shape[0]):
        total = total + counts[device, section]
    return (total * pixels).astype(F32)


def combined(got_ref, row, counts, section, pixels):
    devices = got_ref.shape[0]
    total = total_of(counts, section, pixels)
    sizes = [(counts[device, section] * pixels).astype(F32) for device in range(devices)]
    average = jnp.zeros((1, got_ref.shape[2]), F32)
    for device in range(devices):
        average = average + sizes[device] * got_ref[device, row : row + 1, :]
    average = average / total
    spread = jnp.zeros_like(average)
    for device in range(devices):
        apart = got_ref[device, row : row + 1, :] - average
        spread = spread + (got_ref[device, row + 1 : row + 2, :] + sizes[device] * (apart * apart))
    return average, lax.rsqrt(spread / total + EPSILON)


def summed(got_ref, row):
    total = got_ref[0, row : row + 1, :]
    for device in range(1, got_ref.shape[0]):
        total = total + got_ref[device, row : row + 1, :]
    return total


def sigmoid(values):
    return 1.0 / (1.0 + jnp.exp(-values))


def slope(values):
    part = sigmoid(values)
    return part * (1.0 + values * (1.0 - part))


class Choice:
    def __init__(self, section, wanted, own, other, target, sem):
        self.mine = section == wanted
        self.copies = (
            pltpu.make_async_copy(own.at[0], target, sem),
            pltpu.make_async_copy(other.at[0], target, sem),
        )

    def start(self):
        @pl.when(self.mine)
        def _():
            self.copies[0].start()

        @pl.when(jnp.logical_not(self.mine))
        def _():
            self.copies[1].start()

    def wait(self):
        @pl.when(self.mine)
        def _():
            self.copies[0].wait()

        @pl.when(jnp.logical_not(self.mine))
        def _():
            self.copies[1].wait()


def dot(left, right):
    return jnp.dot(left, right, preferred_element_type=F32)


def dot_back(left, right):
    return lax.dot_general(left, right, (((1,), (1,)), ((), ())), preferred_element_type=F32)


def dot_rows(left, right):
    return lax.dot_general(left, right, (((0,), (0,)), ((), ())), preferred_element_type=F32)


def turned(values, shift):
    shift = shift % values.shape[0]
    if shift == 0:
        return values
    return jnp.concatenate([values[-shift:], values[:-shift]], axis=0)


def taps_of(stride):
    found = []
    for tap_row in range(3):
        for column in range(3):
            if stride == 1:
                found.append((0, tap_row - 1, column - 1))
            else:
                plane = 2 * (tap_row != 1) + (column != 1)
                found.append((plane, -(tap_row == 0), -(column == 0)))
    return found


def first_kernel(geo, place, counts, images, weight, x_out, z_out, sent, raw, slabs, sem):
    section = place[1]
    count = counts[place[0], section]
    load = pltpu.make_async_copy(images.at[section], raw, sem.at[0])
    load.start()
    used = geo.side * geo.slots
    x_ref = x_out.ref
    for plane in range(4):
        last = (plane + 1) * geo.rows
        x_ref[last - geo.line : last, :] = jnp.zeros((geo.line, x_ref.shape[1]), BF16)
        slabs[plane, used : geo.line, :] = jnp.zeros((geo.slots, x_ref.shape[1]), F32)
    load.wait()
    for line in range(geo.side):
        for plane in range(4):
            for column in range(geo.side):
                at = column * geo.slots
                slabs[plane, at : at + geo.slots, :] = raw[
                    2 * line + plane // 2, 2 * column + plane % 2
                ].astype(F32)
            at = plane * geo.rows + line * geo.line
            x_ref[at : at + geo.line, :] = slabs[plane].astype(BF16)
    x_out.send()
    weight = weight.get()
    z_ref = z_out.ref
    for plane in range(4):
        at = plane * geo.rows
        z_ref[at : at + geo.rows, :] = dot(x_ref[at : at + geo.rows, :], weight[...])
    z_out.send()
    send_rows(sent, local_stats(z_ref, geo, count, 4))


def short_kernel(geo, place, counts, x_any, weight, z_out, stats, x_vmem, sem):
    count = counts[place[0], place[1]]
    load = pltpu.make_async_copy(x_any.at[pl.ds(0, geo.rows)], x_vmem, sem.at[0])
    load.start()
    load.wait()
    z_ref = z_out.ref
    z_ref[...] = dot(x_vmem[...], weight.get()[...])
    z_out.send()
    average, spread = local_stats(z_ref, geo, count, 1)
    stats[0:1, :] = average
    stats[1:2, :] = spread


def tap_kernel(geo, planes, block, which, place, counts, got, z_in, narrow, own, other, taps, z_out, moments, sent,
               active, weight, sem):
    section = place[1]
    count = counts[place[0], section]
    choice = Choice(section, block, own, other, weight, sem.at[0])
    choice.start()
    average, inverse = combined(got, 0, counts, section, geo.pixels * planes)
    moments[0:1, :] = average
    moments[1:2, :] = inverse
    gain = narrow[which : which + 1, :] * inverse
    offset = narrow[2 + which : 3 + which, :]
    z_ref = z_in.get()
    rows_of, width = z_ref.shape

    def activate(start, carry):
        pre = (z_ref[pl.ds(start, 64), :] - average) * gain + offset
        active[pl.ds(start, 64), :] = pre * sigmoid(pre) * geo.mask(start, 64, width)
        return carry

    over_rows(rows_of, 64, activate, 0)
    ready = {}
    for tap, (plane, line, column) in enumerate(taps_of(2 if planes == 4 else 1)):
        if (plane, column) not in ready:
            values = active[plane * geo.rows : (plane + 1) * geo.rows, :]
            if column != 0:
                values = pltpu.roll(values, (-column * geo.slots) % geo.rows, 0)
            ready[plane, column] = values.astype(BF16)
        taps.ref[:, tap * width : (tap + 1) * width] = turned(ready[plane, column], -line * geo.line)
    taps.send()
    choice.wait()
    z_out.ref[...] = dot(taps.ref[...], weight[...])
    z_out.send()
    send_rows(sent, local_stats(z_out.ref, geo, count, 1))


def expand_kernel(geo, block, extra, place, counts, got, z_in, narrow, own, other, *rest):
    if extra:
        stats, a_out, z_out, moments, sent, weight, sem = rest
    else:
        a_out, z_out, moments, sent, weight, sem = rest
    section = place[1]
    count = counts[place[0], section]
    choice = Choice(section, block, own, other, weight, sem.at[0])
    choice.start()
    average, inverse = combined(got, 0, counts, section, geo.pixels)
    moments[0:1, :] = average
    moments[1:2, :] = inverse
    gain = narrow[1:2, :] * inverse
    offset = narrow[3:4, :]
    z_ref = z_in.get()

    def activate(start, carry):
        pre = (z_ref[pl.ds(start, 64), :] - average) * gain + offset
        a_out.ref[pl.ds(start, 64), :] = (pre * sigmoid(pre)).astype(BF16)
        return carry

    over_rows(geo.rows, 64, activate, 0)
    a_out.send()
    choice.wait()
    z_out.ref[...] = dot(a_out.ref[...], weight[...])
    z_out.send()
    average, spread = local_stats(z_out.ref, geo, count, 1)
    if extra:
        send_rows(sent, (average, spread, stats[0:1, :], stats[1:2, :]))
    else:
        send_rows(sent, (average, spread))


def join_kernel(geo, place, counts, got, z3, zs, wide, short, weight, joined, u_out, moments, sent):
    section = place[1]
    count = counts[place[0], section]
    average_c, inverse_c = combined(got, 0, counts, section, geo.pixels)
    average_s, inverse_s = combined(got, 2, counts, section, geo.pixels)
    for number, value in enumerate((average_c, inverse_c, average_s, inverse_s)):
        moments[number : number + 1, :] = value
    gain_c = wide[0:1, :] * inverse_c
    gain_s = short[0:1, :] * inverse_s
    offset = wide[1:2, :] + short[1:2, :]
    z3, zs = z3.get(), zs.get()

    def activate(start, carry):
        rows = pl.ds(start, 16)
        pre = (z3[rows, :] - average_c) * gain_c + (zs[rows, :] - average_s) * gain_s + offset
        joined.ref[rows, :] = (pre * sigmoid(pre)).astype(BF16)
        return carry

    over_rows(geo.rows, 16, activate, 0)
    joined.send()
    u_out.ref[...] = dot(joined.ref[...], weight.get()[...])
    u_out.send()
    send_rows(sent, local_stats(u_out.ref, geo, count, 1))


def turn_kernel(geo, place, counts, got, u3, joined, wide, out_grad, block_out, g_out, moments, sent, raw, flat, sem):
    section = place[1]
    count = counts[place[0], section]
    load = pltpu.make_async_copy(out_grad.at[section], raw, sem.at[0])
    load.start()
    average, inverse = combined(got, 0, counts, section, geo.pixels)
    moments[0:1, :] = average
    moments[1:2, :] = inverse
    g_ref = g_out.ref
    width = g_ref.shape[1]
    empty = jnp.zeros((geo.slots, width), F32)
    for line in range(geo.side):
        at = line * geo.line + geo.side * geo.slots
        g_ref[at : at + geo.slots, :] = empty
    g_ref[geo.rows - geo.line : geo.rows, :] = jnp.zeros((geo.line, width), F32)
    load.wait()
    for line in range(geo.side):
        for column in range(geo.side):
            at = line * geo.line + column * geo.slots
            g_ref[at : at + geo.slots, :] = raw[line, column].astype(F32)
    weight = wide[0:1, :]
    offset = wide[1:2, :]
    u3, joined = u3.get(), joined.get()

    def activate(start, carry):
        plain, scaled = carry
        rows = pl.ds(start, 16)
        normed = (u3[rows, :] - average) * inverse
        pre = normed * weight + offset + joined[rows, :].astype(F32)
        part = sigmoid(pre)
        flat[rows, :] = pre * part
        upstream = g_ref[rows, :] * geo.mask(start, 16, width, count) * (part * (1.0 + pre * (1.0 - part)))
        g_ref[rows, :] = upstream
        return plain + fold_rows(upstream), scaled + fold_rows(upstream * normed)

    zero = jnp.zeros((8, width), F32)
    plain, scaled = over_rows(geo.rows, 16, activate, (zero, zero))
    g_out.send()
    send_rows(sent, (jnp.sum(plain, axis=0, keepdims=True), jnp.sum(scaled, axis=0, keepdims=True)))
    for line in range(geo.side):
        for column in range(geo.side):
            at = line * geo.line + column * geo.slots
            block_out.ref[0, line, column] = flat[at : at + geo.slots, :].astype(BF16)


def norm_grad(geo, rows_of, z_ref, g_ref, average, inverse, gain, plain, scaled, total, count, out_ref):
    width = z_ref.shape[1]
    step = step_of(width)
    factor = gain * inverse
    plain_part = plain / total
    scaled_part = scaled / total * inverse

    def one(start, carry):
        rows = pl.ds(start, step)
        centered = z_ref[rows, :] - average
        value = factor * (g_ref[rows, :] - plain_part - centered * scaled_part)
        out_ref[rows, :] = (value * geo.mask(start, step, width, count)).astype(out_ref.dtype)
        return carry

    over_rows(rows_of, step, one, 0)


def silu_back(geo, z_ref, average, inverse, gain, offset, g_ref):
    rows_of, width = z_ref.shape
    step = step_of(width)

    def one(start, carry):
        plain, scaled = carry
        rows = pl.ds(start, step)
        normed = (z_ref[rows, :] - average) * inverse
        upstream = g_ref[rows, :] * slope(normed * gain + offset) * geo.mask(start, step, width)
        g_ref[rows, :] = upstream
        return plain + fold_rows(upstream), scaled + fold_rows(upstream * normed)

    zero = jnp.zeros((8, width), F32)
    plain, scaled = over_rows(rows_of, step, one, (zero, zero))
    return jnp.sum(plain, axis=0, keepdims=True), jnp.sum(scaled, axis=0, keepdims=True)


def expand_back(geo, block, two, place, counts, got, g_in, z3, mom3, wide, *rest):
    if two:
        zs, short, z2, mom2, narrow, own, other, dv, dvs, g_out, sums, sent, weight, sem = rest
    else:
        z2, mom2, narrow, own, other, dv, g_out, sums, sent, weight, sem = rest
    section = place[1]
    count = counts[place[0], section]
    choice = Choice(section, block, own, other, weight, sem.at[0])
    choice.start()
    total = total_of(counts, section, geo.pixels)
    plain, scaled = summed(got, 0), summed(got, 1)
    sums[0:1, :] = plain
    sums[1:2, :] = scaled
    g_ref = g_in.get()
    norm_grad(
        geo, geo.rows, z3.get(), g_ref, mom3[0:1, :], mom3[1:2, :], wide[0:1, :], plain, scaled, total, count, dv.ref
    )
    dv.send()
    choice.wait()
    g_out.ref[...] = dot_back(dv.ref[...], weight[...])
    send_rows(
        sent,
        silu_back(geo, z2.get(), mom2[0:1, :], mom2[1:2, :], narrow[1:2, :], narrow[3:4, :], g_out.ref),
    )
    g_out.send()
    if two:
        scaled = summed(got, 2)
        sums[2:3, :] = scaled
        norm_grad(
            geo, geo.rows, zs.get(), g_ref, mom3[2:3, :], mom3[3:4, :], short[0:1, :], plain, scaled, total, count,
            dvs.ref,
        )
        dvs.send()


def tap_back(geo, planes, block, place, counts, got, g_in, z2, mom2, narrow, z1, mom1, own, other, dv, g_out, sums, sent,
             wide_dv, weight, sem):
    section = place[1]
    count = counts[place[0], section]
    choice = Choice(section, block, own, other, weight, sem.at[0])
    choice.start()
    total = total_of(counts, section, geo.pixels)
    plain, scaled = summed(got, 0), summed(got, 1)
    sums[0:1, :] = plain
    sums[1:2, :] = scaled
    norm_grad(
        geo, geo.rows, z2.get(), g_in.get(), mom2[0:1, :], mom2[1:2, :], narrow[1:2, :], plain, scaled, total, count,
        wide_dv,
    )
    dv.ref[...] = wide_dv[...].astype(BF16)
    dv.send()
    choice.wait()
    g_ref = g_out.ref
    width = g_ref.shape[1]
    ready = {}
    totals = [None] * planes
    for tap, (plane, line, column) in enumerate(taps_of(2 if planes == 4 else 1)):
        if column not in ready:
            values = wide_dv[...]
            if column != 0:
                values = pltpu.roll(values, (column * geo.slots) % geo.rows, 0)
            ready[column] = values.astype(BF16)
        left = turned(ready[column], line * geo.line)
        product = dot_back(left, weight[tap * width : (tap + 1) * width, :])
        totals[plane] = product if totals[plane] is None else totals[plane] + product
    for plane in range(planes):
        g_ref[plane * geo.rows : (plane + 1) * geo.rows, :] = totals[plane]
    send_rows(
        sent,
        silu_back(geo, z1.get(), mom1[0:1, :], mom1[1:2, :], narrow[0:1, :], narrow[2:3, :], g_ref),
    )


def join_back(geo, place, counts, got, g_in, u1, mom4, narrow, weight, g3, z3, zs, mom3, wide, short, dv, g_out, sums,
              sent):
    section = place[1]
    count = counts[place[0], section]
    total = total_of(counts, section, geo.pixels)
    plain, scaled = summed(got, 0), summed(got, 1)
    sums[0:1, :] = plain
    sums[1:2, :] = scaled
    norm_grad(
        geo, geo.rows, u1.get(), g_in.get(), mom4[0:1, :], mom4[1:2, :], narrow[0:1, :], plain, scaled, total, count,
        dv.ref,
    )
    dv.send()
    g_ref = g_out.ref
    g_ref[...] = dot_back(dv.ref[...], weight.get()[...])
    average_c, inverse_c = mom3[0:1, :], mom3[1:2, :]
    average_s, inverse_s = mom3[2:3, :], mom3[3:4, :]
    gain_c, gain_s = wide[0:1, :], short[0:1, :]
    offset = wide[1:2, :] + short[1:2, :]
    width = g_ref.shape[1]
    g3, z3, zs = g3.get(), z3.get(), zs.get()

    def one(start, carry):
        plain, scaled_c, scaled_s = carry
        rows = pl.ds(start, 16)
        normed_c = (z3[rows, :] - average_c) * inverse_c
        normed_s = (zs[rows, :] - average_s) * inverse_s
        arrived = (g_ref[rows, :] + g3[rows, :]).astype(BF16).astype(F32)
        upstream = arrived * slope(normed_c * gain_c + normed_s * gain_s + offset) * geo.mask(start, 16, width)
        g_ref[rows, :] = upstream
        return (
            plain + fold_rows(upstream),
            scaled_c + fold_rows(upstream * normed_c),
            scaled_s + fold_rows(upstream * normed_s),
        )

    zero = jnp.zeros((8, width), F32)
    results = over_rows(geo.rows, 16, one, (zero, zero, zero))
    g_out.send()
    send_rows(sent, [jnp.sum(value, axis=0, keepdims=True) for value in results])


def reduce_back(geo, place, counts, got, g_in, z1, mom1, narrow, dv, sums):
    section = place[1]
    count = counts[place[0], section]
    total = total_of(counts, section, geo.pixels * 4)
    plain, scaled = summed(got, 0), summed(got, 1)
    sums[0:1, :] = plain
    sums[1:2, :] = scaled
    norm_grad(
        geo, 4 * geo.rows, z1.get(), g_in.get(), mom1[0:1, :], mom1[1:2, :], narrow[0:1, :], plain, scaled, total, count,
        dv.ref,
    )


def image_kernel(geo, dv, weight, dvs, weight_s, image_grad, flat):
    dv, weight = dv.get(), weight.get()
    for plane in (1, 2, 3, 0):
        at = plane * geo.rows
        product = dot_back(dv[at : at + geo.rows, :], weight[...])
        if plane == 0:
            product = product + dot_back(dvs.get()[...], weight_s.get()[...])
        flat[at : at + geo.rows, :] = product
        for line in range(geo.side):
            for column in range(geo.side):
                row = at + line * geo.line + column * geo.slots
                image_grad.ref[0, 2 * line + plane // 2, 2 * column + plane % 2] = flat[
                    row : row + geo.slots, :
                ].astype(BF16)


def exchange(sent):
    return lax.all_to_all(sent, "dp", 0, 0)


def swapped(value):
    return lax.ppermute(value, "section", [(0, 1), (1, 0)])


def across(value, mask):
    return lax.ppermute(value, "dp", [(i, i ^ mask) for i in range(lax.axis_size("dp"))])


class Piece:
    def __init__(self, rows, columns, devices, split, width):
        self.rows = rows
        self.columns = columns
        self.split = split
        self.width = width
        if split == "owner":
            self.height = rows // (2 * devices)
            self.blocks = columns // width
        elif split == "rows":
            self.height = rows // (2 * devices)
            self.blocks = columns // width
        else:
            self.height = rows // devices
            self.blocks = columns // 2 // width
        self.lines = self.height * self.blocks

    def at(self, owner, half, block):
        if self.split == "owner":
            return half * (self.rows // 2) + owner * self.height, block * self.width
        if self.split == "rows":
            return (2 * owner + half) * self.height, block * self.width
        return owner * self.height, half * (self.columns // 2) + block * self.width


def pieces_kernel(pieces, place, *refs):
    count = len(pieces)
    inputs = refs[: 2 * count]
    keep, send, total = refs[2 * count :]
    me, section = place[0], place[1]
    line = 0
    for number, piece in enumerate(pieces):
        left, right = inputs[2 * number].get(), inputs[2 * number + 1].get()
        total[0 : piece.rows, 0 : piece.columns] = dot_rows(left[0 : right.shape[0], :], right[...])
        for step in range(keep.ref.shape[0]):
            owner = me ^ step
            for out, half in ((keep.ref, section), (send.ref, 1 - section)):
                for block in range(piece.blocks):
                    row, column = piece.at(owner, half, block)
                    row = pl.multiple_of(row, piece.height)
                    if piece.split == "columns":
                        column = pl.multiple_of(column, piece.width)
                    value = total[pl.ds(row, piece.height), pl.ds(column, piece.width)]
                    to = line + block * piece.height
                    out[step, to : to + piece.height, :] = value.astype(BF16)
        line += piece.lines


class Reduction:
    def __init__(self, place, pieces, pairs):
        devices = lax.axis_size("dp")
        lines = sum(piece.lines for piece in pieces)
        width = pieces[0].width
        shape = spec((devices, lines, width), BF16)
        self.pieces = pieces
        args = [place]
        for left, right in pairs:
            args += [left, right]
        tall = max(piece.rows for piece in pieces)
        wide = max(piece.columns for piece in pieces)
        self.keep, self.out = stage(
            lambda *refs: pieces_kernel(pieces, *refs),
            (shape, shape),
            "dd",
            args,
            "s" + "d" * (len(args) - 1),
            (pltpu.VMEM((tall, wide), F32),),
        )
        self.step = 0
        self.joined = None

    def join(self, other):
        self.joined = other

    def advance(self):
        step = self.step
        self.step += 1
        if step == 0:
            self.sent = (self.out,)
            self.moves = (swapped,)
            self.rest = (self.keep,)
        elif step == 1:
            total = self.rest[0] + self.got[0]
            if self.joined is not None:
                total = jnp.concatenate([total, self.joined.rest[0] + self.joined.got[0]], axis=1)
                self.pieces = self.pieces + self.joined.pieces
            total = total.reshape((-1, 2, 2) + total.shape[1:])
            half = total.shape[-1] // 2
            self.sent = (total[:, :, 1, :, :half], total[:, 1, :, :, half:])
            self.rest = (total[:, :, 0, :, :half], total[:, 0, :, :, half:])
            self.moves = (lambda v: across(v, 1), lambda v: across(v, 2))
        elif step == 2:
            totals = [rest + got for rest, got in zip(self.rest, self.got)]
            self.sent = (totals[0][:, 1], totals[1][:, 1])
            self.rest = (totals[0][:, 0], totals[1][:, 0])
            self.moves = (lambda v: across(v, 2), lambda v: across(v, 1))
        elif step == 3:
            total = jnp.concatenate([rest + got for rest, got in zip(self.rest, self.got)], axis=-1)
            self.rest = (total[0],)
            self.sent = tuple(total[number] for number in range(1, total.shape[0]))
            self.moves = tuple(
                lambda v, number=number: across(v, number << 2) for number in range(1, total.shape[0])
            )
        self.fly()

    def fly(self):
        self.got = tuple(move(value) for move, value in zip(self.moves, self.sent))

    def finish(self):
        total = self.rest[0].astype(F32)
        for value in self.got:
            total = total + value.astype(F32)
        results = []
        line = 0
        for piece in self.pieces:
            blocks = [
                total[line + block * piece.height : line + (block + 1) * piece.height]
                for block in range(piece.blocks)
            ]
            results.append(blocks[0] if len(blocks) == 1 else jnp.concatenate(blocks, axis=1))
            line += piece.lines
        return results


def body(
    images,
    out_grad,
    live_counts,
    w_reduce0,
    w_short,
    short_gain,
    short_bias,
    w_reduce1,
    w_mid,
    w_expand,
    gain_narrow,
    bias_narrow,
    gain_wide,
    bias_wide,
):
    section = lax.axis_index("section")
    dp_index = lax.axis_index("dp")
    devices = lax.axis_size("dp")
    slots = images.shape[1]
    side = images.shape[2] // 2
    geo = Geometry(slots, side)
    c_in = images.shape[4]
    mid = w_mid.shape[2]
    out = w_expand.shape[2]
    rows = geo.rows
    all_rows = 4 * rows
    place = jnp.stack([dp_index, section]).astype(jnp.int32)

    def bound(kernel, *fixed):
        def run(*refs):
            kernel(geo, *fixed, *refs)

        return run

    own_narrow = jnp.concatenate([gain_narrow[0], bias_narrow[0]], axis=0)
    own_wide = jnp.concatenate([gain_wide, bias_wide], axis=0)
    mid_other = swapped(w_mid)
    expand_other = swapped(w_expand)
    other_narrow = swapped(own_narrow)
    other_wide = swapped(own_wide)
    front = section == 0
    narrow0 = jnp.where(front, own_narrow, other_narrow)
    narrow1 = jnp.where(front, other_narrow, own_narrow)
    wide0 = jnp.where(front, own_wide, other_wide)
    wide1 = jnp.where(front, other_wide, own_wide)
    short = jnp.stack([short_gain, short_bias])
    images = images.transpose(0, 2, 3, 1, 4)
    out_grad = out_grad.transpose(0, 2, 3, 1, 4)

    def dma(number):
        return pltpu.SemaphoreType.DMA((number,))

    x, z1, sent = stage(
        bound(first_kernel),
        (spec((all_rows, c_in), BF16), spec((all_rows, mid)), spec((devices, 2, mid))),
        "ddv",
        (place, live_counts, images, w_reduce0),
        "ssad",
        (
            pltpu.VMEM((2 * side, 2 * side, slots, c_in), BF16),
            pltpu.VMEM((4, geo.line, c_in), F32),
            dma(1),
        ),
    )
    got = exchange(sent)
    zs, stats_s = stage(
        bound(short_kernel),
        (spec((rows, out)), spec((2, out))),
        "dv",
        (place, live_counts, x, w_short),
        "ssad",
        (pltpu.VMEM((rows, c_in), BF16), dma(1)),
    )
    tap_scratch = (pltpu.VMEM((9 * mid, mid), BF16), dma(1))
    taps0, z2, mom1, sent = stage(
        bound(tap_kernel, 4, 0, 0),
        (spec((rows, 9 * mid), BF16), spec((rows, mid)), spec((2, mid)), spec((devices, 2, mid))),
        "ddvv",
        (place, live_counts, got, z1, narrow0, w_mid, mid_other),
        "ssgdvaa",
        (pltpu.VMEM((all_rows, mid), F32),) + tap_scratch,
    )
    got = exchange(sent)
    expand_scratch = (pltpu.VMEM((mid, out), BF16), dma(1))
    a2, z3, mom2, sent = stage(
        bound(expand_kernel, 0, True),
        (spec((rows, mid), BF16), spec((rows, out)), spec((2, mid)), spec((devices, 4, out))),
        "ddvv",
        (place, live_counts, got, z2, narrow0, w_expand, expand_other, stats_s),
        "ssgdvaav",
        expand_scratch,
    )
    got = exchange(sent)
    joined, u1, mom3, sent = stage(
        bound(join_kernel),
        (spec((rows, out), BF16), spec((rows, mid)), spec((4, out)), spec((devices, 2, mid))),
        "ddvv",
        (place, live_counts, got, z3, zs, wide0, short, w_reduce1),
        "ssgddvvd",
    )
    got = exchange(sent)
    taps1, u2, mom4, sent = stage(
        bound(tap_kernel, 1, 1, 0),
        (spec((rows, 9 * mid), BF16), spec((rows, mid)), spec((2, mid)), spec((devices, 2, mid))),
        "ddvv",
        (place, live_counts, got, u1, narrow1, w_mid, mid_other),
        "ssgdvaa",
        (pltpu.VMEM((rows, mid), F32),) + tap_scratch,
    )
    got = exchange(sent)
    c2, u3, mom5, sent = stage(
        bound(expand_kernel, 1, False),
        (spec((rows, mid), BF16), spec((rows, out)), spec((2, mid)), spec((devices, 2, out))),
        "ddvv",
        (place, live_counts, got, u2, narrow1, w_expand, expand_other),
        "ssgdvaa",
        expand_scratch,
    )
    got = exchange(sent)
    block_out, g3, mom6, sent = stage(
        bound(turn_kernel),
        (
            spec((1, side, side, slots, out), BF16),
            spec((rows, out)),
            spec((2, out)),
            spec((devices, 2, out)),
        ),
        "ddvv",
        (place, live_counts, got, u3, joined, wide1, out_grad),
        "ssgddva",
        (pltpu.VMEM((side, side, slots, out), BF16), pltpu.VMEM((rows, out), F32), dma(1)),
    )
    got = exchange(sent)
    du3, g2, sums6, sent = stage(
        bound(expand_back, 1, False),
        (spec((rows, out), BF16), spec((rows, mid)), spec((2, out)), spec((devices, 2, mid))),
        "ddvv",
        (place, live_counts, got, g3, u3, mom6, wide1, u2, mom5, narrow1, w_expand, expand_other),
        "ssgddvvdvvaa",
        expand_scratch,
    )
    got = exchange(sent)
    tap_back_scratch = (pltpu.VMEM((rows, mid), F32),) + tap_scratch
    du2, g1, sums5, sent = stage(
        bound(tap_back, 1, 1),
        (spec((rows, mid), BF16), spec((rows, mid)), spec((2, mid)), spec((devices, 2, mid))),
        "ddvv",
        (place, live_counts, got, g2, u2, mom5, narrow1, u1, mom4, w_mid, mid_other),
        "ssgddvvdvaa",
        tap_back_scratch,
    )
    got = exchange(sent)
    piece_mid = Piece(9 * mid, mid, devices, "rows", mid)
    piece_expand = Piece(mid, out, devices, "columns", mid)
    piece_reduce1 = Piece(out, mid, devices, "owner", mid)
    piece_short = Piece(c_in, out, devices, "owner", mid)
    piece_reduce0 = Piece(c_in, mid, devices, "owner", mid)
    heights = [piece.height for piece in (piece_mid, piece_expand, piece_reduce1, piece_short, piece_reduce0)]
    packed = devices == 16 and all(height % 16 == 0 for height in heights)

    def tied(value, starting=(), arrived=()):
        values = lax.optimization_barrier(
            (value, tuple(one.sent for one in starting), tuple(one.got for one in arrived))
        )
        for one, sent in zip(starting, values[1]):
            one.sent = sent
            one.fly()
        for one, got in zip(arrived, values[2]):
            one.got = got
        return values[0]

    if packed:
        first = Reduction(place, (piece_expand, piece_mid), ((c2, du3), (taps1, du2)))
        first.advance()
        got = tied(got, (first,))
    du1, gj, sums4, sent = stage(
        bound(join_back),
        (spec((rows, mid), BF16), spec((rows, out)), spec((2, mid)), spec((devices, 3, out))),
        "ddvv",
        (place, live_counts, got, g1, u1, mom4, narrow1, w_reduce1, g3, z3, zs, mom3, wide0, short),
        "ssgddvvddddvvv",
    )
    got = exchange(sent)
    if packed:
        first.advance()
        got = tied(got, (first,))
    dz3, dzs, g2, sums3, sent = stage(
        bound(expand_back, 0, True),
        (
            spec((rows, out), BF16),
            spec((rows, out), BF16),
            spec((rows, mid)),
            spec((3, out)),
            spec((devices, 2, mid)),
        ),
        "dddvv",
        (place, live_counts, got, gj, z3, mom3, wide0, zs, short, z2, mom2, narrow0, w_expand, expand_other),
        "ssgddvvdvdvvaa",
        expand_scratch,
    )
    got = exchange(sent)
    if packed:
        second = Reduction(
            place, (piece_reduce1, piece_expand, piece_short), ((joined, du1), (a2, dz3), (x[:rows], dzs))
        )
        second.advance()
        first.advance()
        got = tied(got, (first, second))
    dz2, g1, sums2, sent = stage(
        bound(tap_back, 4, 0),
        (spec((rows, mid), BF16), spec((all_rows, mid)), spec((2, mid)), spec((devices, 2, mid))),
        "ddvv",
        (place, live_counts, got, g2, z2, mom2, narrow0, z1, mom1, w_mid, mid_other),
        "ssgddvvdvaa",
        tap_back_scratch,
    )
    got = exchange(sent)
    if packed:
        second.advance()
        first.advance()
        third = Reduction(place, (piece_mid,), ((taps0, dz2),))
        third.advance()
        got = tied(got, (second, first, third))
    dz1, sums1 = stage(
        bound(reduce_back),
        (spec((all_rows, mid), BF16), spec((2, mid))),
        "dv",
        (place, live_counts, got, g1, z1, mom1, narrow0),
        "ssgddvv",
    )
    if packed:
        fourth = Reduction(place, (piece_reduce0,), ((x, dz1),))
        fourth.advance()
        dz1 = tied(dz1, (fourth,), (first, second, third))
        second.advance()
        third.join(fourth)
        third.advance()
        dz1 = tied(dz1, (second, third))
    (image_grad,) = stage(
        bound(image_kernel),
        (spec((1, 2 * side, 2 * side, slots, c_in), BF16),),
        "d",
        (dz1, w_reduce0, dzs, w_short),
        "dddd",
        (pltpu.VMEM((all_rows, c_in), F32),),
    )
    block_out = block_out.transpose(0, 3, 1, 2, 4)
    wide_front = sums3[:2]
    wide_sent = jnp.concatenate([jnp.where(front, sums6, wide_front), sums3[0:1], sums3[2:3]], axis=0)
    wide_got = swapped(wide_sent)
    wide_sums = jnp.where(front, wide_front, sums6) + wide_got[:2]
    width = out // (2 * devices)
    both_short = jnp.stack([sums3[2] + wide_got[3], sums3[0] + wide_got[2]])
    short_norm = lax.dynamic_slice_in_dim(both_short, (section * devices + dp_index) * width, width, 1)
    front_narrow = jnp.stack([sums1, sums2])
    back_narrow = jnp.stack([sums4, sums5])
    narrow_sums = jnp.where(front, front_narrow, back_narrow) + swapped(
        jnp.where(front, back_narrow, front_narrow)
    )
    if packed:
        image_grad = tied(image_grad, (), (second, third))
        second.advance()
        third.advance()
        image_grad = tied(image_grad, (second, third))
        expand1, mid1 = first.finish()
        image_grad = tied(image_grad, (), (second, third))
        third.advance()
        reduce1, expand0, short_grad = second.finish()
        mid0, reduce0 = third.finish()

        def to_owner(front_half, back_half, axis):
            mine = jnp.where(front, front_half, back_half)
            other = swapped(jnp.where(front, back_half, front_half))
            first_half = jnp.where(front, mine, other)
            second_half = jnp.where(front, other, mine)
            return jnp.concatenate([first_half, second_half], axis=axis)

        grad_mid = to_owner(mid0, mid1, 0)
        grad_expand = to_owner(expand0, expand1, 1)
    else:

        def product(left, right):
            return dot_rows(left, right).astype(BF16)

        def of_block(front_grad, back_grad):
            mine = jnp.where(front, front_grad, back_grad)
            both = mine + swapped(jnp.where(front, back_grad, front_grad))
            return lax.psum_scatter(both, "dp", scatter_dimension=0, tiled=True).astype(F32)

        def of_both(grad):
            return lax.psum_scatter(grad, ("section", "dp"), scatter_dimension=0, tiled=True).astype(F32)

        grad_mid = of_block(product(taps0, dz2), product(taps1, du2))
        grad_expand = of_block(product(a2, dz3), product(c2, du3))
        reduce1 = of_both(product(joined, du1))
        short_grad = of_both(product(x[:rows], dzs))
        reduce0 = of_both(product(x, dz1))
    return (
        block_out,
        image_grad.transpose(0, 3, 1, 2, 4),
        reduce0,
        short_grad,
        short_norm,
        reduce1,
        grad_mid[None],
        grad_expand[None],
        narrow_sums[None, :, 1],
        narrow_sums[None, :, 0],
        wide_sums[None, 1],
        wide_sums[None, 0],
    )


def solution(mesh):
    return jax.shard_map(
        body,
        mesh=mesh,
        in_specs=(
            P(None, "dp", None, None, None),
            P(None, "dp", None, None, None),
            P(),
            P(),
            P(),
            P(),
            P(),
            P(),
            P("section", None, None),
            P("section", None, None),
            P("section", None, None),
            P("section", None, None),
            P("section", None),
            P("section", None),
        ),
        out_specs=(
            P("section", "dp", None, None, None),
            P("section", "dp", None, None, None),
            P(("section", "dp"), None),
            P(("section", "dp"), None),
            P(None, ("section", "dp")),
            P(("section", "dp"), None),
            P("section", "dp", None),
            P("section", "dp", None),
            P("section", None, None),
            P("section", None, None),
            P("section", None),
            P("section", None),
        ),
        check_vma=False,
    )
```

```python
import jax
import jax.numpy as jnp
from jax import lax
from jax.experimental import pallas as pl
from jax.experimental.pallas import tpu as pltpu
from jax.sharding import PartitionSpec as P


EPSILON = 1e-05
F32 = jnp.float32
BF16 = jnp.bfloat16
VMEM = pl.BlockSpec(memory_space=pltpu.VMEM)
SMEM = pl.BlockSpec(memory_space=pltpu.SMEM)
ANY = pl.BlockSpec(memory_space=pl.ANY)


def spec(shape, dtype=F32):
    return jax.ShapeDtypeStruct(shape, dtype)


class Late:
    def __init__(self, source, target, sem):
        self.copy = pltpu.make_async_copy(source, target, sem)
        self.copy.start()
        self.target = target
        self.shape = target.shape
        self.waiting = True

    def get(self):
        if self.waiting:
            self.copy.wait()
            self.waiting = False
        return self.target

    def __getitem__(self, index):
        return self.get()[index]


class Out:
    def __init__(self, buffer, target, sem):
        self.ref = buffer
        self.shape = buffer.shape
        self.copy = pltpu.make_async_copy(buffer, target, sem)
        self.sent = False

    def __setitem__(self, index, value):
        self.ref[index] = value

    def send(self):
        self.copy.start()
        self.sent = True


def stage(kernel, outs, out_places, args, places, scratch=()):
    kinds = {"g": VMEM, "s": SMEM, "a": ANY, "d": ANY}
    late = [n for n, kind in enumerate(places) if kind == "d"]
    late_out = [n for n, kind in enumerate(out_places) if kind == "d"]
    buffers = [pltpu.VMEM(args[n].shape, args[n].dtype) for n in late]
    buffers += [pltpu.VMEM(outs[n].shape, outs[n].dtype) for n in late_out]
    args = [
        pltpu.with_memory_space_constraint(arg, pltpu.VMEM) if kind == "g" else arg
        for arg, kind in zip(args, places)
    ]

    def run(*refs):
        inputs = list(refs[: len(args)])
        results = list(refs[len(args) : len(args) + len(outs)])
        rest = refs[len(args) + len(outs) :]
        own, held, sem = rest[: len(scratch)], rest[len(scratch) : -1], rest[-1]
        for place, n in enumerate(late):
            inputs[n] = Late(inputs[n], held[place], sem.at[place])
        waiting = []
        for place, n in enumerate(late_out):
            place += len(late)
            results[n] = Out(held[place], results[n], sem.at[place])
            waiting.append(results[n])
        kernel(*inputs, *results, *own)
        for one in inputs:
            if isinstance(one, Late):
                one.get()
        for one in waiting:
            if not one.sent:
                one.send()
        for one in waiting:
            one.copy.wait()

    return pl.pallas_call(
        run,
        out_shape=list(outs),
        in_specs=[kinds[kind] for kind in places],
        out_specs=[kinds[kind] for kind in out_places],
        scratch_shapes=list(scratch) + buffers + [pltpu.SemaphoreType.DMA((max(1, len(buffers)),))],
        compiler_params=pltpu.CompilerParams(vmem_limit_bytes=58 << 20),
    )(*args)


def split(value, size):
    if size & (size - 1) == 0:
        return value >> (size.bit_length() - 1), value & (size - 1)
    return value // size, value % size


class Geometry:
    def __init__(self, slots, side):
        self.slots = slots
        self.side = side
        self.pitch = side + 1
        self.line = self.pitch * slots
        self.rows = self.pitch * self.line
        self.pixels = side * side

    def mask(self, start, step, width, count=None):
        row = start + lax.broadcasted_iota(jnp.int32, (step, 128), 0)
        position, image = split(row, self.slots)
        line, column = split(position, self.pitch)
        line = split(line, self.pitch)[1]
        good = (column < self.side) & (line < self.side)
        if count is not None:
            good = good & (image < count)
        value = jnp.where(good, 1.0, 0.0).astype(F32)
        return jnp.concatenate([value] * (width // 128), axis=1) if width > 128 else value


def over_rows(rows, step, body, init):
    def one(i, carry):
        return body(pl.multiple_of(i * step, step), carry)

    return lax.fori_loop(0, rows // step, one, init)


def fold_rows(block):
    rows, width = block.shape
    return jnp.sum(block.reshape(rows // 8, 8, width), axis=0)


def step_of(width):
    return 64 if width <= 512 else 16


def local_stats(z_ref, geo, count, planes):
    rows, width = z_ref.shape
    step = step_of(width)
    total = (count * (geo.pixels * planes)).astype(F32)

    def plain(start, acc):
        return acc + fold_rows(z_ref[pl.ds(start, step), :] * geo.mask(start, step, width, count))

    zero = jnp.zeros((8, width), F32)
    average = jnp.sum(over_rows(rows, step, plain, zero), axis=0, keepdims=True) / total

    def squared(start, acc):
        centered = z_ref[pl.ds(start, step), :] - average
        return acc + fold_rows(centered * centered * geo.mask(start, step, width, count))

    spread = jnp.sum(over_rows(rows, step, squared, zero), axis=0, keepdims=True)
    return average, spread


def send_short(out_ref, values):
    values = values.astype(BF16)
    for device in range(out_ref.shape[0]):
        out_ref[device] = values


def packed_stats(pairs):
    average = jnp.concatenate([pair[0] for pair in pairs], axis=1)
    spread = jnp.concatenate([pair[1] for pair in pairs], axis=1)
    high = average.astype(BF16).astype(F32)
    half = spread.shape[1] // 2
    return jnp.concatenate(
        [
            jnp.concatenate([high, spread[:, :half]], axis=1),
            jnp.concatenate([average - high, spread[:, half:]], axis=1),
        ],
        axis=0,
    )


class Unpacked:
    def __init__(self, got):
        self.devices = got.shape[0]
        width = got.shape[2] * 2 // 3
        self.average, self.spread = [], []
        for device in range(self.devices):
            rows = got[device].astype(F32)
            self.average.append(rows[0:1, :width] + rows[1:2, :width])
            self.spread.append(jnp.concatenate([rows[0:1, width:], rows[1:2, width:]], axis=1))
        self.shape = (self.devices, 2, width)

    def __getitem__(self, index):
        device, row, lanes = index
        return (self.average if row.start == 0 else self.spread)[device][:, lanes]


def send_rows(out_ref, values):
    lane = 0
    for pair in values:
        width = pair[0].shape[1]
        for row, value in enumerate(pair):
            for device in range(out_ref.shape[0]):
                out_ref[device, row : row + 1, lane : lane + width] = value
        lane += width


def total_of(counts, section, pixels):
    total = counts[section, 0]
    for device in range(1, counts.shape[1]):
        total = total + counts[section, device]
    return (total * pixels).astype(F32)


def combined(got_ref, lanes, counts, section, pixels):
    devices = got_ref.shape[0]
    total = total_of(counts, section, pixels)
    sizes = [(counts[section, device] * pixels).astype(F32) for device in range(devices)]
    average = sizes[0] * got_ref[0, 0:1, lanes]
    for device in range(1, devices):
        average = average + sizes[device] * got_ref[device, 0:1, lanes]
    average = average / total
    spread = jnp.zeros_like(average)
    for device in range(devices):
        apart = got_ref[device, 0:1, lanes] - average
        spread = spread + (got_ref[device, 1:2, lanes] + sizes[device] * (apart * apart))
    return average, lax.rsqrt(spread / total + EPSILON)


def summed(got_ref):
    total = got_ref[0].astype(F32)
    for device in range(1, got_ref.shape[0]):
        total = total + got_ref[device].astype(F32)
    return total


def sigmoid(values):
    return 1.0 / (1.0 + jnp.exp(-values))


def slope(values):
    part = sigmoid(values)
    return part * (1.0 + values * (1.0 - part))


class Choice:
    def __init__(self, section, wanted, own, other, target, sem):
        self.mine = section == wanted
        self.copies = (
            pltpu.make_async_copy(own.at[0], target, sem),
            pltpu.make_async_copy(other.at[0], target, sem),
        )

    def start(self):
        @pl.when(self.mine)
        def _():
            self.copies[0].start()

        @pl.when(jnp.logical_not(self.mine))
        def _():
            self.copies[1].start()

    def wait(self):
        @pl.when(self.mine)
        def _():
            self.copies[0].wait()

        @pl.when(jnp.logical_not(self.mine))
        def _():
            self.copies[1].wait()


def dot(left, right):
    return jnp.dot(left, right, preferred_element_type=F32)


def dot_back(left, right):
    return lax.dot_general(left, right, (((1,), (1,)), ((), ())), preferred_element_type=F32)


def dot_rows(left, right):
    return lax.dot_general(left, right, (((0,), (0,)), ((), ())), preferred_element_type=F32)


def turned(values, shift):
    shift = shift % values.shape[0]
    if shift == 0:
        return values
    return jnp.concatenate([values[-shift:], values[:-shift]], axis=0)


def taps_of(stride):
    found = []
    for tap_row in range(3):
        for column in range(3):
            if stride == 1:
                found.append((0, tap_row - 1, column - 1))
            else:
                plane = 2 * (tap_row != 1) + (column != 1)
                found.append((plane, -(tap_row == 0), -(column == 0)))
    return found


def first_kernel(geo, place, counts, images, weight, x_out, z_out, sent, raw, slabs, sem):
    section = place[1]
    count = counts[section, place[0]]
    load = pltpu.make_async_copy(images.at[section], raw, sem.at[0])
    load.start()
    used = geo.side * geo.slots
    x_ref = x_out.ref
    for plane in range(4):
        last = (plane + 1) * geo.rows
        x_ref[last - geo.line : last, :] = jnp.zeros((geo.line, x_ref.shape[1]), BF16)
        slabs[plane, used : geo.line, :] = jnp.zeros((geo.slots, x_ref.shape[1]), F32)
    load.wait()
    for line in range(geo.side):
        for plane in range(4):
            for column in range(geo.side):
                at = column * geo.slots
                slabs[plane, at : at + geo.slots, :] = raw[
                    2 * line + plane // 2, 2 * column + plane % 2
                ].astype(F32)
            at = plane * geo.rows + line * geo.line
            x_ref[at : at + geo.line, :] = slabs[plane].astype(BF16)
    x_out.send()
    weight = weight.get()
    z_ref = z_out.ref
    for plane in range(4):
        at = plane * geo.rows
        z_ref[at : at + geo.rows, :] = dot(x_ref[at : at + geo.rows, :], weight[...])
    z_out.send()
    send_rows(sent, (local_stats(z_ref, geo, count, 4),))


def short_kernel(geo, place, counts, x_any, weight, z_out, stats, x_vmem, sem):
    count = counts[place[1], place[0]]
    load = pltpu.make_async_copy(x_any.at[pl.ds(0, geo.rows)], x_vmem, sem.at[0])
    load.start()
    load.wait()
    z_ref = z_out.ref
    z_ref[...] = dot(x_vmem[...], weight.get()[...])
    z_out.send()
    average, spread = local_stats(z_ref, geo, count, 1)
    stats[0:1, :] = average
    stats[1:2, :] = spread


def tap_kernel(geo, planes, block, place, counts, got, z_in, narrow, own, other, *rest):
    if planes == 4:
        stats, taps, z_out, moments, sent, active, weight, sem = rest
    else:
        taps, z_out, moments, sent, active, weight, sem = rest
    section = place[1]
    count = counts[section, place[0]]
    choice = Choice(section, block, own, other, weight, sem.at[0])
    choice.start()
    average, inverse = combined(got, slice(None), counts, section, geo.pixels * planes)
    moments[0:1, :] = average
    moments[1:2, :] = inverse
    gain = narrow[0:1, :] * inverse
    offset = narrow[2:3, :]
    z_ref = z_in.get()
    rows_of, width = z_ref.shape

    def activate(start, carry):
        pre = (z_ref[pl.ds(start, 64), :] - average) * gain + offset
        active[pl.ds(start, 64), :] = pre * sigmoid(pre) * geo.mask(start, 64, width)
        return carry

    over_rows(rows_of, 64, activate, 0)
    ready = {}
    for tap, (plane, line, column) in enumerate(taps_of(2 if planes == 4 else 1)):
        if (plane, column) not in ready:
            values = active[plane * geo.rows : (plane + 1) * geo.rows, :]
            if column != 0:
                values = pltpu.roll(values, (-column * geo.slots) % geo.rows, 0)
            ready[plane, column] = values.astype(BF16)
        taps.ref[:, tap * width : (tap + 1) * width] = turned(ready[plane, column], -line * geo.line)
    taps.send()
    choice.wait()
    z_out.ref[...] = dot(taps.ref[...], weight[...])
    z_out.send()
    values = local_stats(z_out.ref, geo, count, 1)
    if planes == 4:
        send_short(sent, packed_stats((values, (stats[0:1, :], stats[1:2, :]))))
    else:
        send_rows(sent, (values,))


def expand_kernel(geo, block, extra, place, counts, got, z_in, narrow, own, other, *rest):
    if extra:
        a_out, z_out, moments, moments_s, sent, weight, sem = rest
    else:
        a_out, z_out, moments, sent, weight, sem = rest
    section = place[1]
    count = counts[section, place[0]]
    choice = Choice(section, block, own, other, weight, sem.at[0])
    choice.start()
    if extra:
        got = Unpacked(got)
    average, inverse = combined(got, slice(0, z_in.shape[1]), counts, section, geo.pixels)
    moments[0:1, :] = average
    moments[1:2, :] = inverse
    gain = narrow[1:2, :] * inverse
    offset = narrow[3:4, :]
    z_ref = z_in.get()

    def activate(start, carry):
        pre = (z_ref[pl.ds(start, 64), :] - average) * gain + offset
        a_out.ref[pl.ds(start, 64), :] = (pre * sigmoid(pre)).astype(BF16)
        return carry

    over_rows(geo.rows, 64, activate, 0)
    a_out.send()
    choice.wait()
    z_out.ref[...] = dot(a_out.ref[...], weight[...])
    z_out.send()
    send_rows(sent, (local_stats(z_out.ref, geo, count, 1),))
    sent.send()
    if extra:
        lanes = slice(z_ref.shape[1], got.shape[2])
        for row, value in enumerate(combined(got, lanes, counts, section, geo.pixels)):
            moments_s[row : row + 1, :] = value


def join_kernel(geo, place, counts, got, z3, zs, moments_s, wide, short, weight, joined, u_out, moments, sent):
    section = place[1]
    count = counts[section, place[0]]
    average_c, inverse_c = combined(got, slice(None), counts, section, geo.pixels)
    average_s, inverse_s = moments_s[0:1, :], moments_s[1:2, :]
    for number, value in enumerate((average_c, inverse_c, average_s, inverse_s)):
        moments[number : number + 1, :] = value
    gain_c = wide[0:1, :] * inverse_c
    gain_s = short[0:1, :] * inverse_s
    offset = wide[1:2, :] + short[1:2, :]
    z3, zs = z3.get(), zs.get()

    def activate(start, carry):
        rows = pl.ds(start, 16)
        pre = (z3[rows, :] - average_c) * gain_c + (zs[rows, :] - average_s) * gain_s + offset
        joined.ref[rows, :] = (pre * sigmoid(pre)).astype(BF16)
        return carry

    over_rows(geo.rows, 16, activate, 0)
    joined.send()
    u_out.ref[...] = dot(joined.ref[...], weight.get()[...])
    u_out.send()
    send_rows(sent, (local_stats(u_out.ref, geo, count, 1),))


def turn_kernel(geo, place, counts, got, u3, joined, wide, out_grad, block_out, g_out, moments, sent, raw, flat, sem):
    section = place[1]
    count = counts[section, place[0]]
    load = pltpu.make_async_copy(out_grad.at[section], raw, sem.at[0])
    load.start()
    average, inverse = combined(got, slice(None), counts, section, geo.pixels)
    moments[0:1, :] = average
    moments[1:2, :] = inverse
    g_ref = g_out.ref
    width = g_ref.shape[1]
    empty = jnp.zeros((geo.slots, width), F32)
    for line in range(geo.side):
        at = line * geo.line + geo.side * geo.slots
        g_ref[at : at + geo.slots, :] = empty
    g_ref[geo.rows - geo.line : geo.rows, :] = jnp.zeros((geo.line, width), F32)
    load.wait()
    for line in range(geo.side):
        for column in range(geo.side):
            at = line * geo.line + column * geo.slots
            g_ref[at : at + geo.slots, :] = raw[line, column].astype(F32)
    weight = wide[0:1, :]
    offset = wide[1:2, :]
    u3, joined = u3.get(), joined.get()

    def activate(start, carry):
        plain, scaled = carry
        rows = pl.ds(start, 16)
        normed = (u3[rows, :] - average) * inverse
        pre = normed * weight + offset + joined[rows, :].astype(F32)
        part = sigmoid(pre)
        flat[rows, :] = pre * part
        upstream = g_ref[rows, :] * geo.mask(start, 16, width, count) * (part * (1.0 + pre * (1.0 - part)))
        g_ref[rows, :] = upstream
        return plain + fold_rows(upstream), scaled + fold_rows(upstream * normed)

    zero = jnp.zeros((8, width), F32)
    plain, scaled = over_rows(geo.rows, 16, activate, (zero, zero))
    g_out.send()
    send_rows(sent, ((jnp.sum(plain, axis=0, keepdims=True), jnp.sum(scaled, axis=0, keepdims=True)),))
    sent.send()
    for line in range(geo.side):
        for column in range(geo.side):
            at = line * geo.line + column * geo.slots
            block_out.ref[0, line, column] = flat[at : at + geo.slots, :].astype(BF16)


def norm_grad(geo, rows_of, z_ref, g_ref, average, inverse, gain, plain, scaled, total, count, out_ref):
    width = z_ref.shape[1]
    step = step_of(width)
    factor = gain * inverse
    plain_part = plain / total
    scaled_part = scaled / total * inverse

    def one(start, carry):
        rows = pl.ds(start, step)
        centered = z_ref[rows, :] - average
        value = factor * (g_ref[rows, :] - plain_part - centered * scaled_part)
        out_ref[rows, :] = (value * geo.mask(start, step, width, count)).astype(out_ref.dtype)
        return carry

    over_rows(rows_of, step, one, 0)


def silu_back(geo, z_ref, average, inverse, gain, offset, g_ref):
    rows_of, width = z_ref.shape
    step = step_of(width)

    def one(start, carry):
        plain, scaled = carry
        rows = pl.ds(start, step)
        normed = (z_ref[rows, :] - average) * inverse
        upstream = g_ref[rows, :] * slope(normed * gain + offset) * geo.mask(start, step, width)
        g_ref[rows, :] = upstream
        return plain + fold_rows(upstream), scaled + fold_rows(upstream * normed)

    zero = jnp.zeros((8, width), F32)
    plain, scaled = over_rows(rows_of, step, one, (zero, zero))
    return jnp.sum(plain, axis=0, keepdims=True), jnp.sum(scaled, axis=0, keepdims=True)


def expand_back(geo, block, two, place, counts, got, g_in, z3, mom3, wide, *rest):
    if two:
        zs, short, z2, mom2, narrow, own, other, dv, dvs, g_out, sums, sent, weight, sem = rest
    else:
        z2, mom2, narrow, own, other, dv, g_out, sums, sent, weight, sem = rest
    section = place[1]
    count = counts[section, place[0]]
    choice = Choice(section, block, own, other, weight, sem.at[0])
    choice.start()
    total = total_of(counts, section, geo.pixels)
    main = dv.shape[1]
    both = summed(got)
    plain, scaled = both[0:1, :main], both[1:2, :main]
    sums[0:1, :] = plain
    sums[1:2, :] = scaled
    g_ref = g_in.get()
    norm_grad(
        geo, geo.rows, z3.get(), g_ref, mom3[0:1, :], mom3[1:2, :], wide[0:1, :], plain, scaled, total, count, dv.ref
    )
    dv.send()
    choice.wait()
    g_out.ref[...] = dot_back(dv.ref[...], weight[...])
    send_rows(
        sent,
        (silu_back(geo, z2.get(), mom2[0:1, :], mom2[1:2, :], narrow[1:2, :], narrow[3:4, :], g_out.ref),),
    )
    sent.send()
    g_out.send()
    if two:
        scaled = jnp.concatenate([both[0:1, main:], both[1:2, main:]], axis=1)
        sums[2:3, :] = scaled
        norm_grad(
            geo, geo.rows, zs.get(), g_ref, mom3[2:3, :], mom3[3:4, :], short[0:1, :], plain, scaled, total, count,
            dvs.ref,
        )
        dvs.send()


def tap_back(geo, planes, block, place, counts, got, g_in, z2, mom2, narrow, z1, mom1, own, other, dv, g_out, sums, sent,
             wide_dv, weight, sem):
    section = place[1]
    count = counts[section, place[0]]
    choice = Choice(section, block, own, other, weight, sem.at[0])
    choice.start()
    total = total_of(counts, section, geo.pixels)
    both = summed(got)
    plain, scaled = both[0:1, :], both[1:2, :]
    sums[0:1, :] = plain
    sums[1:2, :] = scaled
    norm_grad(
        geo, geo.rows, z2.get(), g_in.get(), mom2[0:1, :], mom2[1:2, :], narrow[1:2, :], plain, scaled, total, count,
        wide_dv,
    )
    dv.ref[...] = wide_dv[...].astype(BF16)
    dv.send()
    choice.wait()
    g_ref = g_out.ref
    width = g_ref.shape[1]
    ready = {}
    totals = [None] * planes
    for tap, (plane, line, column) in enumerate(taps_of(2 if planes == 4 else 1)):
        if column not in ready:
            values = wide_dv[...]
            if column != 0:
                values = pltpu.roll(values, (column * geo.slots) % geo.rows, 0)
            ready[column] = values.astype(BF16)
        left = turned(ready[column], line * geo.line)
        product = dot_back(left, weight[tap * width : (tap + 1) * width, :])
        totals[plane] = product if totals[plane] is None else totals[plane] + product
    for plane in range(planes):
        g_ref[plane * geo.rows : (plane + 1) * geo.rows, :] = totals[plane]
    send_rows(
        sent,
        (silu_back(geo, z1.get(), mom1[0:1, :], mom1[1:2, :], narrow[0:1, :], narrow[2:3, :], g_ref),),
    )


def join_back(geo, place, counts, got, g_in, u1, mom4, narrow, weight, g3, z3, zs, mom3, wide, short, dv, g_out, sums,
              sent):
    section = place[1]
    count = counts[section, place[0]]
    total = total_of(counts, section, geo.pixels)
    both = summed(got)
    plain, scaled = both[0:1, :], both[1:2, :]
    sums[0:1, :] = plain
    sums[1:2, :] = scaled
    norm_grad(
        geo, geo.rows, u1.get(), g_in.get(), mom4[0:1, :], mom4[1:2, :], narrow[0:1, :], plain, scaled, total, count,
        dv.ref,
    )
    dv.send()
    g_ref = g_out.ref
    g_ref[...] = dot_back(dv.ref[...], weight.get()[...])
    average_c, inverse_c = mom3[0:1, :], mom3[1:2, :]
    average_s, inverse_s = mom3[2:3, :], mom3[3:4, :]
    gain_c, gain_s = wide[0:1, :], short[0:1, :]
    offset = wide[1:2, :] + short[1:2, :]
    width = g_ref.shape[1]
    g3, z3, zs = g3.get(), z3.get(), zs.get()

    def one(start, carry):
        plain, scaled_c, scaled_s = carry
        rows = pl.ds(start, 16)
        normed_c = (z3[rows, :] - average_c) * inverse_c
        normed_s = (zs[rows, :] - average_s) * inverse_s
        arrived = (g_ref[rows, :] + g3[rows, :]).astype(BF16).astype(F32)
        upstream = arrived * slope(normed_c * gain_c + normed_s * gain_s + offset) * geo.mask(start, 16, width)
        g_ref[rows, :] = upstream
        return (
            plain + fold_rows(upstream),
            scaled_c + fold_rows(upstream * normed_c),
            scaled_s + fold_rows(upstream * normed_s),
        )

    zero = jnp.zeros((8, width), F32)
    results = over_rows(geo.rows, 16, one, (zero, zero, zero))
    g_out.send()
    plain, scaled_c, scaled_s = [jnp.sum(value, axis=0, keepdims=True) for value in results]
    half = width // 2
    send_short(
        sent,
        jnp.concatenate(
            [
                jnp.concatenate([plain, scaled_s[:, :half]], axis=1),
                jnp.concatenate([scaled_c, scaled_s[:, half:]], axis=1),
            ],
            axis=0,
        ),
    )


def reduce_back(geo, place, counts, got, g_in, z1, mom1, narrow, dv, sums):
    section = place[1]
    count = counts[section, place[0]]
    total = total_of(counts, section, geo.pixels * 4)
    both = summed(got)
    plain, scaled = both[0:1, :], both[1:2, :]
    sums[0:1, :] = plain
    sums[1:2, :] = scaled
    norm_grad(
        geo, 4 * geo.rows, z1.get(), g_in.get(), mom1[0:1, :], mom1[1:2, :], narrow[0:1, :], plain, scaled, total, count,
        dv.ref,
    )


def image_kernel(geo, dv, weight, dvs, weight_s, image_grad, flat):
    dv, weight = dv.get(), weight.get()
    for plane in (1, 2, 3, 0):
        at = plane * geo.rows
        product = dot_back(dv[at : at + geo.rows, :], weight[...])
        if plane == 0:
            product = product + dot_back(dvs.get()[...], weight_s.get()[...])
        flat[at : at + geo.rows, :] = product
        for line in range(geo.side):
            for column in range(geo.side):
                row = at + line * geo.line + column * geo.slots
                image_grad.ref[0, 2 * line + plane // 2, 2 * column + plane % 2] = flat[
                    row : row + geo.slots, :
                ].astype(BF16)


def exchange(sent):
    return lax.all_to_all(sent, "dp", 0, 0)


def swapped(value):
    return lax.ppermute(value, "section", [(0, 1), (1, 0)])


def across(value, mask):
    return lax.ppermute(value, "dp", [(i, i ^ mask) for i in range(lax.axis_size("dp"))])


class Piece:
    def __init__(self, rows, columns, devices, split, width):
        self.rows = rows
        self.columns = columns
        self.split = split
        self.width = width
        if split == "owner":
            self.height = rows // (2 * devices)
            self.blocks = columns // width
        elif split == "rows":
            self.height = rows // (2 * devices)
            self.blocks = columns // width
        else:
            self.height = rows // devices
            self.blocks = columns // 2 // width
        self.lines = self.height * self.blocks

    def at(self, owner, half, block):
        if self.split == "owner":
            return half * (self.rows // 2) + owner * self.height, block * self.width
        if self.split == "rows":
            return (2 * owner + half) * self.height, block * self.width
        return owner * self.height, half * (self.columns // 2) + block * self.width


def pieces_kernel(pieces, place, *refs):
    count = len(pieces)
    inputs = refs[: 2 * count]
    keep, send, total = refs[2 * count :]
    me, section = place[0], place[1]
    line = 0
    for number, piece in enumerate(pieces):
        left, right = inputs[2 * number].get(), inputs[2 * number + 1].get()
        total[0 : piece.rows, 0 : piece.columns] = dot_rows(left[0 : right.shape[0], :], right[...])
        for step in range(keep.ref.shape[0]):
            owner = me ^ step
            for out, half in ((keep.ref, section), (send.ref, 1 - section)):
                for block in range(piece.blocks):
                    row, column = piece.at(owner, half, block)
                    row = pl.multiple_of(row, piece.height)
                    if piece.split == "columns":
                        column = pl.multiple_of(column, piece.width)
                    value = total[pl.ds(row, piece.height), pl.ds(column, piece.width)]
                    to = line + block * piece.height
                    out[step, to : to + piece.height, :] = value.astype(BF16)
        line += piece.lines


class Reduction:
    def __init__(self, place, pieces, pairs):
        devices = lax.axis_size("dp")
        lines = sum(piece.lines for piece in pieces)
        width = pieces[0].width
        shape = spec((devices, lines, width), BF16)
        self.pieces = pieces
        args = [place]
        for left, right in pairs:
            args += [left, right]
        tall = max(piece.rows for piece in pieces)
        wide = max(piece.columns for piece in pieces)
        self.keep, self.out = stage(
            lambda *refs: pieces_kernel(pieces, *refs),
            (shape, shape),
            "dd",
            args,
            "s" + "d" * (len(args) - 1),
            (pltpu.VMEM((tall, wide), F32),),
        )
        self.step = 0

    def advance(self):
        step = self.step
        self.step += 1
        if step == 0:
            self.sent = (self.out,)
            self.moves = (swapped,)
            self.rest = (self.keep,)
        elif step == 1:
            total = self.rest[0] + self.got[0]
            total = total.reshape((-1, 2, 2) + total.shape[1:])
            half = total.shape[-1] // 2
            self.sent = (total[:, :, 1, :, :half], total[:, 1, :, :, half:])
            self.rest = (total[:, :, 0, :, :half], total[:, 0, :, :, half:])
            self.moves = (lambda v: across(v, 1), lambda v: across(v, 2))
        elif step == 2:
            totals = [rest + got for rest, got in zip(self.rest, self.got)]
            self.sent = (totals[0][:, 1], totals[1][:, 1])
            self.rest = (totals[0][:, 0], totals[1][:, 0])
            self.moves = (lambda v: across(v, 2), lambda v: across(v, 1))
        elif step == 3:
            total = jnp.concatenate([rest + got for rest, got in zip(self.rest, self.got)], axis=-1)
            self.rest = (total[0],)
            self.sent = tuple(total[number] for number in range(1, total.shape[0]))
            self.moves = tuple(
                lambda v, number=number: across(v, number << 2) for number in range(1, total.shape[0])
            )
        self.fly()

    def fly(self):
        self.got = tuple(move(value) for move, value in zip(self.moves, self.sent))

    def finish(self):
        total = self.rest[0].astype(F32)
        for value in self.got:
            total = total + value.astype(F32)
        results = []
        line = 0
        for piece in self.pieces:
            blocks = [
                total[line + block * piece.height : line + (block + 1) * piece.height]
                for block in range(piece.blocks)
            ]
            results.append(blocks[0] if len(blocks) == 1 else jnp.concatenate(blocks, axis=1))
            line += piece.lines
        return results


def body(
    images,
    out_grad,
    live_counts,
    w_reduce0,
    w_short,
    short_gain,
    short_bias,
    w_reduce1,
    w_mid,
    w_expand,
    gain_narrow,
    bias_narrow,
    gain_wide,
    bias_wide,
):
    section = lax.axis_index("section")
    dp_index = lax.axis_index("dp")
    devices = lax.axis_size("dp")
    slots = images.shape[1]
    side = images.shape[2] // 2
    geo = Geometry(slots, side)
    c_in = images.shape[4]
    mid = w_mid.shape[2]
    out = w_expand.shape[2]
    rows = geo.rows
    all_rows = 4 * rows
    place = jnp.stack([dp_index, section]).astype(jnp.int32)

    def bound(kernel, *fixed):
        def run(*refs):
            kernel(geo, *fixed, *refs)

        return run

    own_narrow = jnp.concatenate([gain_narrow[0], bias_narrow[0]], axis=0)
    own_wide = jnp.concatenate([gain_wide, bias_wide], axis=0)
    mid_other = swapped(w_mid)
    expand_other = swapped(w_expand)
    other_narrow = swapped(own_narrow)
    other_wide = swapped(own_wide)
    front = section == 0
    narrow0 = jnp.where(front, own_narrow, other_narrow)
    narrow1 = jnp.where(front, other_narrow, own_narrow)
    wide0 = jnp.where(front, own_wide, other_wide)
    wide1 = jnp.where(front, other_wide, own_wide)
    short = jnp.stack([short_gain, short_bias])
    counts = live_counts.T
    images = images.transpose(0, 2, 3, 1, 4)
    out_grad = out_grad.transpose(0, 2, 3, 1, 4)

    def dma(number):
        return pltpu.SemaphoreType.DMA((number,))

    x, z1, sent = stage(
        bound(first_kernel),
        (spec((all_rows, c_in), BF16), spec((all_rows, mid)), spec((devices, 2, mid))),
        "ddd",
        (place, counts, images, w_reduce0),
        "ssad",
        (
            pltpu.VMEM((2 * side, 2 * side, slots, c_in), BF16),
            pltpu.VMEM((4, geo.line, c_in), F32),
            dma(1),
        ),
    )
    got = exchange(sent)
    zs, stats_s = stage(
        bound(short_kernel),
        (spec((rows, out)), spec((2, out))),
        "dd",
        (place, counts, x, w_short),
        "ssad",
        (pltpu.VMEM((rows, c_in), BF16), dma(1)),
    )
    tap_scratch = (pltpu.VMEM((9 * mid, mid), BF16), dma(1))
    taps0, z2, mom1, sent = stage(
        bound(tap_kernel, 4, 0),
        (spec((rows, 9 * mid), BF16), spec((rows, mid)), spec((2, mid)), spec((devices, 2, 3 * (mid + out) // 2), BF16)),
        "dddd",
        (place, counts, got, z1, narrow0, w_mid, mid_other, stats_s),
        "ssgddaad",
        (pltpu.VMEM((all_rows, mid), F32),) + tap_scratch,
    )
    got = exchange(sent)
    expand_scratch = (pltpu.VMEM((mid, out), BF16), dma(1))
    a2, z3, mom2, moments_s, sent = stage(
        bound(expand_kernel, 0, True),
        (spec((rows, mid), BF16), spec((rows, out)), spec((2, mid)), spec((2, out)), spec((devices, 2, out))),
        "ddddd",
        (place, counts, got, z2, narrow0, w_expand, expand_other),
        "ssgddaa",
        expand_scratch,
    )
    got = exchange(sent)
    joined, u1, mom3, sent = stage(
        bound(join_kernel),
        (spec((rows, out), BF16), spec((rows, mid)), spec((4, out)), spec((devices, 2, mid))),
        "dddd",
        (place, counts, got, z3, zs, moments_s, wide0, short, w_reduce1),
        "ssgdddddd",
    )
    got = exchange(sent)
    taps1, u2, mom4, sent = stage(
        bound(tap_kernel, 1, 1),
        (spec((rows, 9 * mid), BF16), spec((rows, mid)), spec((2, mid)), spec((devices, 2, mid))),
        "dddd",
        (place, counts, got, u1, narrow1, w_mid, mid_other),
        "ssgddaa",
        (pltpu.VMEM((rows, mid), F32),) + tap_scratch,
    )
    got = exchange(sent)
    c2, u3, mom5, sent = stage(
        bound(expand_kernel, 1, False),
        (spec((rows, mid), BF16), spec((rows, out)), spec((2, mid)), spec((devices, 2, out))),
        "dddd",
        (place, counts, got, u2, narrow1, w_expand, expand_other),
        "ssgddaa",
        expand_scratch,
    )
    got = exchange(sent)
    block_out, g3, mom6, sent = stage(
        bound(turn_kernel),
        (
            spec((1, side, side, slots, out), BF16),
            spec((rows, out)),
            spec((2, out)),
            spec((devices, 2, out)),
        ),
        "dddd",
        (place, counts, got, u3, joined, wide1, out_grad),
        "ssgddda",
        (pltpu.VMEM((side, side, slots, out), BF16), pltpu.VMEM((rows, out), F32), dma(1)),
    )
    got = exchange(sent)
    du3, g2, sums6, sent = stage(
        bound(expand_back, 1, False),
        (spec((rows, out), BF16), spec((rows, mid)), spec((2, out)), spec((devices, 2, mid))),
        "dddd",
        (place, counts, got, g3, u3, mom6, wide1, u2, mom5, narrow1, w_expand, expand_other),
        "ssgdddddddaa",
        expand_scratch,
    )
    got = exchange(sent)
    tap_back_scratch = (pltpu.VMEM((rows, mid), F32),) + tap_scratch
    du2, g1, sums5, sent = stage(
        bound(tap_back, 1, 1),
        (spec((rows, mid), BF16), spec((rows, mid)), spec((2, mid)), spec((devices, 2, mid))),
        "dddd",
        (place, counts, got, g2, u2, mom5, narrow1, u1, mom4, w_mid, mid_other),
        "ssgddddddaa",
        tap_back_scratch,
    )
    got = exchange(sent)
    piece_mid = Piece(9 * mid, mid, devices, "rows", mid)
    piece_expand = Piece(mid, out, devices, "columns", mid)
    piece_reduce1 = Piece(out, mid, devices, "owner", mid)
    piece_short = Piece(c_in, out, devices, "owner", mid)
    piece_reduce0 = Piece(c_in, mid, devices, "owner", mid)
    heights = [piece.height for piece in (piece_mid, piece_expand, piece_reduce1, piece_short, piece_reduce0)]
    packed = devices == 16 and all(height % 16 == 0 for height in heights)

    def tied(value, starting=(), arrived=()):
        values = lax.optimization_barrier(
            (value, tuple(one.sent for one in starting), tuple(one.got for one in arrived))
        )
        for one, sent in zip(starting, values[1]):
            one.sent = sent
            one.fly()
        for one, got in zip(arrived, values[2]):
            one.got = got
        return values[0]

    if packed:
        first = Reduction(place, (piece_expand, piece_mid), ((c2, du3), (taps1, du2)))
        first.advance()
        got = tied(got, (first,))
    du1, gj, sums4, sent = stage(
        bound(join_back),
        (spec((rows, mid), BF16), spec((rows, out)), spec((2, mid)), spec((devices, 2, out + out // 2), BF16)),
        "dddd",
        (place, counts, got, g1, u1, mom4, narrow1, w_reduce1, g3, z3, zs, mom3, wide0, short),
        "ssgddddddddddd",
    )
    got = exchange(sent)
    if packed:
        first.advance()
        got = tied(got, (first,))
    dz3, dzs, g2, sums3, sent = stage(
        bound(expand_back, 0, True),
        (
            spec((rows, out), BF16),
            spec((rows, out), BF16),
            spec((rows, mid)),
            spec((3, out)),
            spec((devices, 2, mid)),
        ),
        "ddddd",
        (place, counts, got, gj, z3, mom3, wide0, zs, short, z2, mom2, narrow0, w_expand, expand_other),
        "ssgdddddddddaa",
        expand_scratch,
    )
    got = exchange(sent)
    if packed:
        second = Reduction(
            place, (piece_reduce1, piece_expand, piece_short), ((joined, du1), (a2, dz3), (x, dzs))
        )
        second.advance()
        first.advance()
        got = tied(got, (first, second))
    dz2, g1, sums2, sent = stage(
        bound(tap_back, 4, 0),
        (spec((rows, mid), BF16), spec((all_rows, mid)), spec((2, mid)), spec((devices, 2, mid))),
        "dddd",
        (place, counts, got, g2, z2, mom2, narrow0, z1, mom1, w_mid, mid_other),
        "ssgddddddaa",
        tap_back_scratch,
    )
    got = exchange(sent)
    if packed:
        second.advance()
        first.advance()
        got = tied(got, (second, first))
    dz1, sums1 = stage(
        bound(reduce_back),
        (spec((all_rows, mid), BF16), spec((2, mid))),
        "dd",
        (place, counts, got, g1, z1, mom1, narrow0),
        "ssgdddd",
    )
    if packed:
        third = Reduction(place, (piece_mid, piece_reduce0), ((taps0, dz2), (x, dz1)))
        third.advance()
        dz1 = tied(dz1, (third,), (second, first))
        second.advance()
        dz1 = tied(dz1, (second,))
        dz1 = tied(dz1, (), (third,))
        third.advance()
        dz1 = tied(dz1, (third,), (second,))
        second.advance()
        dz1 = tied(dz1, (second,))
    wide_front = sums3[:2]
    wide_sent = jnp.concatenate([jnp.where(front, sums6, wide_front), sums3[0:1], sums3[2:3]], axis=0)
    front_narrow = jnp.stack([sums1, sums2])
    back_narrow = jnp.stack([sums4, sums5])
    narrow_sent = jnp.where(front, back_narrow, front_narrow)
    dz1, wide_sent, narrow_sent = lax.optimization_barrier((dz1, wide_sent, narrow_sent))
    wide_got = swapped(wide_sent)
    narrow_got = swapped(narrow_sent)
    (image_grad,) = stage(
        bound(image_kernel),
        (spec((1, 2 * side, 2 * side, slots, c_in), BF16),),
        "d",
        (dz1, w_reduce0, dzs, w_short),
        "dddd",
        (pltpu.VMEM((all_rows, c_in), F32),),
    )
    block_out = block_out.transpose(0, 3, 1, 2, 4)
    image_grad, wide_got, narrow_got = lax.optimization_barrier((image_grad, wide_got, narrow_got))
    wide_sums = jnp.where(front, wide_front, sums6) + wide_got[:2]
    width = out // (2 * devices)
    both_short = jnp.stack([sums3[2] + wide_got[3], sums3[0] + wide_got[2]])
    short_norm = lax.dynamic_slice_in_dim(both_short, (section * devices + dp_index) * width, width, 1)
    narrow_sums = jnp.where(front, front_narrow, back_narrow) + narrow_got
    if packed:
        expand1, mid1 = first.finish()
        image_grad = tied(image_grad, (), (third,))
        third.advance()
        image_grad = tied(image_grad, (third,))
        image_grad = tied(image_grad, (), (second, third))
        third.advance()
        image_grad = tied(image_grad, (third,))
        reduce1, expand0, short_grad = second.finish()
        image_grad = tied(image_grad, (), (third,))
        mid0, reduce0 = third.finish()

        def to_owner(front_half, back_half, axis):
            mine = jnp.where(front, front_half, back_half)
            other = swapped(jnp.where(front, back_half, front_half))
            first_half = jnp.where(front, mine, other)
            second_half = jnp.where(front, other, mine)
            return jnp.concatenate([first_half, second_half], axis=axis)

        grad_mid = to_owner(mid0, mid1, 0)
        grad_expand = to_owner(expand0, expand1, 1)
    else:

        def product(left, right):
            return dot_rows(left, right).astype(BF16)

        def of_block(front_grad, back_grad):
            mine = jnp.where(front, front_grad, back_grad)
            both = mine + swapped(jnp.where(front, back_grad, front_grad))
            return lax.psum_scatter(both, "dp", scatter_dimension=0, tiled=True).astype(F32)

        def of_both(grad):
            return lax.psum_scatter(grad, ("section", "dp"), scatter_dimension=0, tiled=True).astype(F32)

        grad_mid = of_block(product(taps0, dz2), product(taps1, du2))
        grad_expand = of_block(product(a2, dz3), product(c2, du3))
        reduce1 = of_both(product(joined, du1))
        short_grad = of_both(product(x[:rows], dzs))
        reduce0 = of_both(product(x, dz1))
    return (
        block_out,
        image_grad.transpose(0, 3, 1, 2, 4),
        reduce0,
        short_grad,
        short_norm,
        reduce1,
        grad_mid[None],
        grad_expand[None],
        narrow_sums[None, :, 1],
        narrow_sums[None, :, 0],
        wide_sums[None, 1],
        wide_sums[None, 0],
    )


def solution(mesh):
    return jax.shard_map(
        body,
        mesh=mesh,
        in_specs=(
            P(None, "dp", None, None, None),
            P(None, "dp", None, None, None),
            P(),
            P(),
            P(),
            P(),
            P(),
            P(),
            P("section", None, None),
            P("section", None, None),
            P("section", None, None),
            P("section", None, None),
            P("section", None),
            P("section", None),
        ),
        out_specs=(
            P("section", "dp", None, None, None),
            P("section", "dp", None, None, None),
            P(("section", "dp"), None),
            P(("section", "dp"), None),
            P(None, ("section", "dp")),
            P(("section", "dp"), None),
            P("section", "dp", None),
            P("section", "dp", None),
            P("section", None, None),
            P("section", None, None),
            P("section", None),
            P("section", None),
        ),
        check_vma=False,
    )
```

```python
import jax
import jax.numpy as jnp
from jax import lax
from jax.experimental import pallas as pl
from jax.experimental.pallas import tpu as pltpu
from jax.sharding import PartitionSpec as P


EPSILON = 1e-05
F32 = jnp.float32
BF16 = jnp.bfloat16
VMEM = pl.BlockSpec(memory_space=pltpu.VMEM)
SMEM = pl.BlockSpec(memory_space=pltpu.SMEM)
ANY = pl.BlockSpec(memory_space=pl.ANY)


def spec(shape, dtype=F32):
    return jax.ShapeDtypeStruct(shape, dtype)


class Late:
    def __init__(self, source, target, sem):
        self.copy = pltpu.make_async_copy(source, target, sem)
        self.copy.start()
        self.target = target
        self.shape = target.shape
        self.waiting = True

    def get(self):
        if self.waiting:
            self.copy.wait()
            self.waiting = False
        return self.target

    def __getitem__(self, index):
        return self.get()[index]


class Out:
    def __init__(self, buffer, target, sem):
        self.ref = buffer
        self.shape = buffer.shape
        self.copy = pltpu.make_async_copy(buffer, target, sem)
        self.sent = False

    def __setitem__(self, index, value):
        self.ref[index] = value

    def send(self):
        self.copy.start()
        self.sent = True


def stage(kernel, outs, out_places, args, places, scratch=()):
    kinds = {"g": VMEM, "s": SMEM, "a": ANY, "d": ANY}
    late = [n for n, kind in enumerate(places) if kind == "d"]
    late_out = [n for n, kind in enumerate(out_places) if kind == "d"]
    buffers = [pltpu.VMEM(args[n].shape, args[n].dtype) for n in late]
    buffers += [pltpu.VMEM(outs[n].shape, outs[n].dtype) for n in late_out]
    args = [
        pltpu.with_memory_space_constraint(arg, pltpu.VMEM) if kind == "g" else arg
        for arg, kind in zip(args, places)
    ]

    def run(*refs):
        inputs = list(refs[: len(args)])
        results = list(refs[len(args) : len(args) + len(outs)])
        rest = refs[len(args) + len(outs) :]
        own, held, sem = rest[: len(scratch)], rest[len(scratch) : -1], rest[-1]
        for place, n in enumerate(late):
            inputs[n] = Late(inputs[n], held[place], sem.at[place])
        waiting = []
        for place, n in enumerate(late_out):
            place += len(late)
            results[n] = Out(held[place], results[n], sem.at[place])
            waiting.append(results[n])
        kernel(*inputs, *results, *own)
        for one in inputs:
            if isinstance(one, Late):
                one.get()
        for one in waiting:
            if not one.sent:
                one.send()
        for one in waiting:
            one.copy.wait()

    return pl.pallas_call(
        run,
        out_shape=list(outs),
        in_specs=[kinds[kind] for kind in places],
        out_specs=[kinds[kind] for kind in out_places],
        scratch_shapes=list(scratch) + buffers + [pltpu.SemaphoreType.DMA((max(1, len(buffers)),))],
        compiler_params=pltpu.CompilerParams(vmem_limit_bytes=58 << 20),
    )(*args)


def split(value, size):
    if size & (size - 1) == 0:
        return value >> (size.bit_length() - 1), value & (size - 1)
    return value // size, value % size


class Geometry:
    def __init__(self, slots, side):
        self.slots = slots
        self.side = side
        self.pitch = side + 1
        self.line = self.pitch * slots
        self.rows = self.pitch * self.line
        self.pixels = side * side

    def mask(self, start, step, width, count=None):
        row = start + lax.broadcasted_iota(jnp.int32, (step, 128), 0)
        position, image = split(row, self.slots)
        line, column = split(position, self.pitch)
        line = split(line, self.pitch)[1]
        good = (column < self.side) & (line < self.side)
        if count is not None:
            good = good & (image < count)
        value = jnp.where(good, 1.0, 0.0).astype(F32)
        return jnp.concatenate([value] * (width // 128), axis=1) if width > 128 else value


def over_rows(rows, step, body, init):
    def one(i, carry):
        return body(pl.multiple_of(i * step, step), carry)

    return lax.fori_loop(0, rows // step, one, init)


def fold_rows(block):
    rows, width = block.shape
    return jnp.sum(block.reshape(rows // 8, 8, width), axis=0)


def step_of(width):
    return 64 if width <= 512 else 16


def local_stats(z_ref, geo, count, planes):
    rows, width = z_ref.shape
    step = step_of(width)
    total = (count * (geo.pixels * planes)).astype(F32)

    def plain(start, acc):
        return acc + fold_rows(z_ref[pl.ds(start, step), :] * geo.mask(start, step, width, count))

    zero = jnp.zeros((8, width), F32)
    average = jnp.sum(over_rows(rows, step, plain, zero), axis=0, keepdims=True) / total

    def squared(start, acc):
        centered = z_ref[pl.ds(start, step), :] - average
        return acc + fold_rows(centered * centered * geo.mask(start, step, width, count))

    spread = jnp.sum(over_rows(rows, step, squared, zero), axis=0, keepdims=True)
    return average, spread


def send_short(out_ref, values):
    values = values.astype(BF16)
    for device in range(out_ref.shape[0]):
        out_ref[device] = values


def packed_stats(pairs):
    average = jnp.concatenate([pair[0] for pair in pairs], axis=1)
    spread = jnp.concatenate([pair[1] for pair in pairs], axis=1)
    high = average.astype(BF16).astype(F32)
    half = spread.shape[1] // 2
    return jnp.concatenate(
        [
            jnp.concatenate([high, spread[:, :half]], axis=1),
            jnp.concatenate([average - high, spread[:, half:]], axis=1),
        ],
        axis=0,
    )


class Unpacked:
    def __init__(self, got):
        self.devices = got.shape[0]
        width = got.shape[2] * 2 // 3
        self.average, self.spread = [], []
        for device in range(self.devices):
            rows = got[device].astype(F32)
            self.average.append(rows[0:1, :width] + rows[1:2, :width])
            self.spread.append(jnp.concatenate([rows[0:1, width:], rows[1:2, width:]], axis=1))
        self.shape = (self.devices, 2, width)

    def __getitem__(self, index):
        device, row, lanes = index
        return (self.average if row.start == 0 else self.spread)[device][:, lanes]


def send_rows(out_ref, values):
    lane = 0
    for pair in values:
        width = pair[0].shape[1]
        for row, value in enumerate(pair):
            for device in range(out_ref.shape[0]):
                out_ref[device, row : row + 1, lane : lane + width] = value
        lane += width


def total_of(counts, section, pixels):
    total = counts[section, 0]
    for device in range(1, counts.shape[1]):
        total = total + counts[section, device]
    return (total * pixels).astype(F32)


def combined(got_ref, lanes, counts, section, pixels):
    devices = got_ref.shape[0]
    total = total_of(counts, section, pixels)
    sizes = [(counts[section, device] * pixels).astype(F32) for device in range(devices)]
    average = sizes[0] * got_ref[0, 0:1, lanes]
    for device in range(1, devices):
        average = average + sizes[device] * got_ref[device, 0:1, lanes]
    average = average / total
    spread = jnp.zeros_like(average)
    for device in range(devices):
        apart = got_ref[device, 0:1, lanes] - average
        spread = spread + (got_ref[device, 1:2, lanes] + sizes[device] * (apart * apart))
    return average, lax.rsqrt(spread / total + EPSILON)


def summed(got_ref):
    total = got_ref[0].astype(F32)
    for device in range(1, got_ref.shape[0]):
        total = total + got_ref[device].astype(F32)
    return total


def sigmoid(values):
    return 1.0 / (1.0 + jnp.exp(-values))


def slope(values):
    part = sigmoid(values)
    return part * (1.0 + values * (1.0 - part))


class Choice:
    def __init__(self, section, wanted, own, other, target, sem):
        self.mine = section == wanted
        self.copies = (
            pltpu.make_async_copy(own.at[0], target, sem),
            pltpu.make_async_copy(other.at[0], target, sem),
        )

    def start(self):
        @pl.when(self.mine)
        def _():
            self.copies[0].start()

        @pl.when(jnp.logical_not(self.mine))
        def _():
            self.copies[1].start()

    def wait(self):
        @pl.when(self.mine)
        def _():
            self.copies[0].wait()

        @pl.when(jnp.logical_not(self.mine))
        def _():
            self.copies[1].wait()


def dot(left, right):
    return jnp.dot(left, right, preferred_element_type=F32)


def dot_back(left, right):
    return lax.dot_general(left, right, (((1,), (1,)), ((), ())), preferred_element_type=F32)


def dot_rows(left, right):
    return lax.dot_general(left, right, (((0,), (0,)), ((), ())), preferred_element_type=F32)


def turned(values, shift):
    shift = shift % values.shape[0]
    if shift == 0:
        return values
    return jnp.concatenate([values[-shift:], values[:-shift]], axis=0)


def taps_of(stride):
    found = []
    for tap_row in range(3):
        for column in range(3):
            if stride == 1:
                found.append((0, tap_row - 1, column - 1))
            else:
                plane = 2 * (tap_row != 1) + (column != 1)
                found.append((plane, -(tap_row == 0), -(column == 0)))
    return found


def first_kernel(geo, place, counts, images, weight, x_out, z_out, sent, raw, slabs, sem):
    section = place[1]
    count = counts[section, place[0]]
    load = pltpu.make_async_copy(images.at[section], raw, sem.at[0])
    load.start()
    used = geo.side * geo.slots
    x_ref = x_out.ref
    for plane in range(4):
        last = (plane + 1) * geo.rows
        x_ref[last - geo.line : last, :] = jnp.zeros((geo.line, x_ref.shape[1]), BF16)
        slabs[plane, used : geo.line, :] = jnp.zeros((geo.slots, x_ref.shape[1]), F32)
    load.wait()
    for line in range(geo.side):
        for plane in range(4):
            for column in range(geo.side):
                at = column * geo.slots
                slabs[plane, at : at + geo.slots, :] = raw[
                    2 * line + plane // 2, 2 * column + plane % 2
                ].astype(F32)
            at = plane * geo.rows + line * geo.line
            x_ref[at : at + geo.line, :] = slabs[plane].astype(BF16)
    x_out.send()
    weight = weight.get()
    z_ref = z_out.ref
    for plane in range(4):
        at = plane * geo.rows
        z_ref[at : at + geo.rows, :] = dot(x_ref[at : at + geo.rows, :], weight[...])
    z_out.send()
    send_rows(sent, (local_stats(z_ref, geo, count, 4),))


def short_kernel(geo, place, counts, x_any, weight, z_out, stats, x_vmem, sem):
    count = counts[place[1], place[0]]
    load = pltpu.make_async_copy(x_any.at[pl.ds(0, geo.rows)], x_vmem, sem.at[0])
    load.start()
    load.wait()
    z_ref = z_out.ref
    z_ref[...] = dot(x_vmem[...], weight.get()[...])
    z_out.send()
    average, spread = local_stats(z_ref, geo, count, 1)
    stats[0:1, :] = average
    stats[1:2, :] = spread


def tap_kernel(geo, planes, block, place, counts, got, z_in, narrow, own, other, *rest):
    if planes == 4:
        stats, taps, z_out, moments, sent, active, weight, sem = rest
    else:
        taps, z_out, moments, sent, active, weight, sem = rest
    section = place[1]
    count = counts[section, place[0]]
    choice = Choice(section, block, own, other, weight, sem.at[0])
    choice.start()
    average, inverse = combined(got, slice(None), counts, section, geo.pixels * planes)
    moments[0:1, :] = average
    moments[1:2, :] = inverse
    gain = narrow[0:1, :] * inverse
    offset = narrow[2:3, :]
    z_ref = z_in.get()
    rows_of, width = z_ref.shape

    def activate(start, carry):
        pre = (z_ref[pl.ds(start, 64), :] - average) * gain + offset
        active[pl.ds(start, 64), :] = pre * sigmoid(pre) * geo.mask(start, 64, width)
        return carry

    over_rows(rows_of, 64, activate, 0)
    ready = {}
    for tap, (plane, line, column) in enumerate(taps_of(2 if planes == 4 else 1)):
        if (plane, column) not in ready:
            values = active[plane * geo.rows : (plane + 1) * geo.rows, :]
            if column != 0:
                values = pltpu.roll(values, (-column * geo.slots) % geo.rows, 0)
            ready[plane, column] = values.astype(BF16)
        taps.ref[:, tap * width : (tap + 1) * width] = turned(ready[plane, column], -line * geo.line)
    taps.send()
    choice.wait()
    z_out.ref[...] = dot(taps.ref[...], weight[...])
    z_out.send()
    values = local_stats(z_out.ref, geo, count, 1)
    if planes == 4:
        send_short(sent, packed_stats((values, (stats[0:1, :], stats[1:2, :]))))
    else:
        send_rows(sent, (values,))


def expand_kernel(geo, block, extra, place, counts, got, z_in, narrow, own, other, *rest):
    if extra:
        a_out, z_out, moments, moments_s, sent, weight, sem = rest
    else:
        a_out, z_out, moments, sent, weight, sem = rest
    section = place[1]
    count = counts[section, place[0]]
    choice = Choice(section, block, own, other, weight, sem.at[0])
    choice.start()
    if extra:
        got = Unpacked(got)
    average, inverse = combined(got, slice(0, z_in.shape[1]), counts, section, geo.pixels)
    moments[0:1, :] = average
    moments[1:2, :] = inverse
    gain = narrow[1:2, :] * inverse
    offset = narrow[3:4, :]
    z_ref = z_in.get()

    def activate(start, carry):
        pre = (z_ref[pl.ds(start, 64), :] - average) * gain + offset
        a_out.ref[pl.ds(start, 64), :] = (pre * sigmoid(pre)).astype(BF16)
        return carry

    over_rows(geo.rows, 64, activate, 0)
    a_out.send()
    choice.wait()
    z_out.ref[...] = dot(a_out.ref[...], weight[...])
    z_out.send()
    send_rows(sent, (local_stats(z_out.ref, geo, count, 1),))
    sent.send()
    if extra:
        lanes = slice(z_ref.shape[1], got.shape[2])
        for row, value in enumerate(combined(got, lanes, counts, section, geo.pixels)):
            moments_s[row : row + 1, :] = value


def join_kernel(geo, place, counts, got, z3, zs, moments_s, wide, short, weight, joined, u_out, moments, sent):
    section = place[1]
    count = counts[section, place[0]]
    average_c, inverse_c = combined(got, slice(None), counts, section, geo.pixels)
    average_s, inverse_s = moments_s[0:1, :], moments_s[1:2, :]
    for number, value in enumerate((average_c, inverse_c, average_s, inverse_s)):
        moments[number : number + 1, :] = value
    gain_c = wide[0:1, :] * inverse_c
    gain_s = short[0:1, :] * inverse_s
    offset = wide[1:2, :] + short[1:2, :]
    z3, zs = z3.get(), zs.get()

    def activate(start, carry):
        rows = pl.ds(start, 16)
        pre = (z3[rows, :] - average_c) * gain_c + (zs[rows, :] - average_s) * gain_s + offset
        joined.ref[rows, :] = (pre * sigmoid(pre)).astype(BF16)
        return carry

    over_rows(geo.rows, 16, activate, 0)
    joined.send()
    u_out.ref[...] = dot(joined.ref[...], weight.get()[...])
    u_out.send()
    send_rows(sent, (local_stats(u_out.ref, geo, count, 1),))


def turn_kernel(geo, place, counts, got, u3, joined, wide, out_grad, block_out, g_out, moments, sent, raw, flat, sem):
    section = place[1]
    count = counts[section, place[0]]
    load = pltpu.make_async_copy(out_grad.at[section], raw, sem.at[0])
    load.start()
    average, inverse = combined(got, slice(None), counts, section, geo.pixels)
    moments[0:1, :] = average
    moments[1:2, :] = inverse
    g_ref = g_out.ref
    width = g_ref.shape[1]
    empty = jnp.zeros((geo.slots, width), F32)
    for line in range(geo.side):
        at = line * geo.line + geo.side * geo.slots
        g_ref[at : at + geo.slots, :] = empty
    g_ref[geo.rows - geo.line : geo.rows, :] = jnp.zeros((geo.line, width), F32)
    load.wait()
    for line in range(geo.side):
        for column in range(geo.side):
            at = line * geo.line + column * geo.slots
            g_ref[at : at + geo.slots, :] = raw[line, column].astype(F32)
    weight = wide[0:1, :]
    offset = wide[1:2, :]
    u3, joined = u3.get(), joined.get()

    def activate(start, carry):
        plain, scaled = carry
        rows = pl.ds(start, 16)
        normed = (u3[rows, :] - average) * inverse
        pre = normed * weight + offset + joined[rows, :].astype(F32)
        part = sigmoid(pre)
        flat[rows, :] = pre * part
        upstream = g_ref[rows, :] * geo.mask(start, 16, width, count) * (part * (1.0 + pre * (1.0 - part)))
        g_ref[rows, :] = upstream
        return plain + fold_rows(upstream), scaled + fold_rows(upstream * normed)

    zero = jnp.zeros((8, width), F32)
    plain, scaled = over_rows(geo.rows, 16, activate, (zero, zero))
    g_out.send()
    send_rows(sent, ((jnp.sum(plain, axis=0, keepdims=True), jnp.sum(scaled, axis=0, keepdims=True)),))
    sent.send()
    for line in range(geo.side):
        for column in range(geo.side):
            at = line * geo.line + column * geo.slots
            block_out.ref[0, line, column] = flat[at : at + geo.slots, :].astype(BF16)


def norm_grad(geo, rows_of, z_ref, g_ref, average, inverse, gain, plain, scaled, total, count, out_ref):
    width = z_ref.shape[1]
    step = step_of(width)
    factor = gain * inverse
    plain_part = plain / total
    scaled_part = scaled / total * inverse

    def one(start, carry):
        rows = pl.ds(start, step)
        centered = z_ref[rows, :] - average
        value = factor * (g_ref[rows, :] - plain_part - centered * scaled_part)
        out_ref[rows, :] = (value * geo.mask(start, step, width, count)).astype(out_ref.dtype)
        return carry

    over_rows(rows_of, step, one, 0)


def silu_back(geo, z_ref, average, inverse, gain, offset, g_ref):
    rows_of, width = z_ref.shape
    step = step_of(width)

    def one(start, carry):
        plain, scaled = carry
        rows = pl.ds(start, step)
        normed = (z_ref[rows, :] - average) * inverse
        upstream = g_ref[rows, :] * slope(normed * gain + offset) * geo.mask(start, step, width)
        g_ref[rows, :] = upstream
        return plain + fold_rows(upstream), scaled + fold_rows(upstream * normed)

    zero = jnp.zeros((8, width), F32)
    plain, scaled = over_rows(rows_of, step, one, (zero, zero))
    return jnp.sum(plain, axis=0, keepdims=True), jnp.sum(scaled, axis=0, keepdims=True)


def expand_back(geo, block, two, place, counts, got, g_in, z3, mom3, wide, *rest):
    if two:
        zs, short, z2, mom2, narrow, own, other, dv, dvs, g_out, sums, sent, weight, sem = rest
    else:
        z2, mom2, narrow, own, other, dv, g_out, sums, sent, weight, sem = rest
    section = place[1]
    count = counts[section, place[0]]
    choice = Choice(section, block, own, other, weight, sem.at[0])
    choice.start()
    total = total_of(counts, section, geo.pixels)
    main = dv.shape[1]
    both = summed(got)
    plain, scaled = both[0:1, :main], both[1:2, :main]
    sums[0:1, :] = plain
    sums[1:2, :] = scaled
    g_ref = g_in.get()
    norm_grad(
        geo, geo.rows, z3.get(), g_ref, mom3[0:1, :], mom3[1:2, :], wide[0:1, :], plain, scaled, total, count, dv.ref
    )
    dv.send()
    choice.wait()
    g_out.ref[...] = dot_back(dv.ref[...], weight[...])
    send_rows(
        sent,
        (silu_back(geo, z2.get(), mom2[0:1, :], mom2[1:2, :], narrow[1:2, :], narrow[3:4, :], g_out.ref),),
    )
    sent.send()
    g_out.send()
    if two:
        scaled = jnp.concatenate([both[0:1, main:], both[1:2, main:]], axis=1)
        sums[2:3, :] = scaled
        norm_grad(
            geo, geo.rows, zs.get(), g_ref, mom3[2:3, :], mom3[3:4, :], short[0:1, :], plain, scaled, total, count,
            dvs.ref,
        )
        dvs.send()


def tap_back(geo, planes, block, place, counts, got, g_in, z2, mom2, narrow, z1, mom1, own, other, dv, g_out, sums, sent,
             wide_dv, weight, sem):
    section = place[1]
    count = counts[section, place[0]]
    choice = Choice(section, block, own, other, weight, sem.at[0])
    choice.start()
    total = total_of(counts, section, geo.pixels)
    both = summed(got)
    plain, scaled = both[0:1, :], both[1:2, :]
    sums[0:1, :] = plain
    sums[1:2, :] = scaled
    norm_grad(
        geo, geo.rows, z2.get(), g_in.get(), mom2[0:1, :], mom2[1:2, :], narrow[1:2, :], plain, scaled, total, count,
        wide_dv,
    )
    dv.ref[...] = wide_dv[...].astype(BF16)
    dv.send()
    choice.wait()
    g_ref = g_out.ref
    width = g_ref.shape[1]
    ready = {}
    totals = [None] * planes
    for tap, (plane, line, column) in enumerate(taps_of(2 if planes == 4 else 1)):
        if column not in ready:
            values = wide_dv[...]
            if column != 0:
                values = pltpu.roll(values, (column * geo.slots) % geo.rows, 0)
            ready[column] = values.astype(BF16)
        left = turned(ready[column], line * geo.line)
        product = dot_back(left, weight[tap * width : (tap + 1) * width, :])
        totals[plane] = product if totals[plane] is None else totals[plane] + product
    for plane in range(planes):
        g_ref[plane * geo.rows : (plane + 1) * geo.rows, :] = totals[plane]
    send_rows(
        sent,
        (silu_back(geo, z1.get(), mom1[0:1, :], mom1[1:2, :], narrow[0:1, :], narrow[2:3, :], g_ref),),
    )


def join_back(geo, place, counts, got, g_in, u1, mom4, narrow, weight, g3, z3, zs, mom3, wide, short, dv, g_out, sums,
              sent):
    section = place[1]
    count = counts[section, place[0]]
    total = total_of(counts, section, geo.pixels)
    both = summed(got)
    plain, scaled = both[0:1, :], both[1:2, :]
    sums[0:1, :] = plain
    sums[1:2, :] = scaled
    norm_grad(
        geo, geo.rows, u1.get(), g_in.get(), mom4[0:1, :], mom4[1:2, :], narrow[0:1, :], plain, scaled, total, count,
        dv.ref,
    )
    dv.send()
    g_ref = g_out.ref
    g_ref[...] = dot_back(dv.ref[...], weight.get()[...])
    average_c, inverse_c = mom3[0:1, :], mom3[1:2, :]
    average_s, inverse_s = mom3[2:3, :], mom3[3:4, :]
    gain_c, gain_s = wide[0:1, :], short[0:1, :]
    offset = wide[1:2, :] + short[1:2, :]
    width = g_ref.shape[1]
    g3, z3, zs = g3.get(), z3.get(), zs.get()

    def one(start, carry):
        plain, scaled_c, scaled_s = carry
        rows = pl.ds(start, 16)
        normed_c = (z3[rows, :] - average_c) * inverse_c
        normed_s = (zs[rows, :] - average_s) * inverse_s
        arrived = (g_ref[rows, :] + g3[rows, :]).astype(BF16).astype(F32)
        upstream = arrived * slope(normed_c * gain_c + normed_s * gain_s + offset) * geo.mask(start, 16, width)
        g_ref[rows, :] = upstream
        return (
            plain + fold_rows(upstream),
            scaled_c + fold_rows(upstream * normed_c),
            scaled_s + fold_rows(upstream * normed_s),
        )

    zero = jnp.zeros((8, width), F32)
    results = over_rows(geo.rows, 16, one, (zero, zero, zero))
    g_out.send()
    plain, scaled_c, scaled_s = [jnp.sum(value, axis=0, keepdims=True) for value in results]
    half = width // 2
    send_short(
        sent,
        jnp.concatenate(
            [
                jnp.concatenate([plain, scaled_s[:, :half]], axis=1),
                jnp.concatenate([scaled_c, scaled_s[:, half:]], axis=1),
            ],
            axis=0,
        ),
    )


def reduce_back(geo, place, counts, got, g_in, z1, mom1, narrow, dv, sums):
    section = place[1]
    count = counts[section, place[0]]
    total = total_of(counts, section, geo.pixels * 4)
    both = summed(got)
    plain, scaled = both[0:1, :], both[1:2, :]
    sums[0:1, :] = plain
    sums[1:2, :] = scaled
    norm_grad(
        geo, 4 * geo.rows, z1.get(), g_in.get(), mom1[0:1, :], mom1[1:2, :], narrow[0:1, :], plain, scaled, total, count,
        dv.ref,
    )


def image_kernel(geo, dv, weight, dvs, weight_s, image_grad, flat):
    dv, weight = dv.get(), weight.get()
    for plane in (1, 2, 3, 0):
        at = plane * geo.rows
        product = dot_back(dv[at : at + geo.rows, :], weight[...])
        if plane == 0:
            product = product + dot_back(dvs.get()[...], weight_s.get()[...])
        flat[at : at + geo.rows, :] = product
        for line in range(geo.side):
            for column in range(geo.side):
                row = at + line * geo.line + column * geo.slots
                image_grad.ref[0, 2 * line + plane // 2, 2 * column + plane % 2] = flat[
                    row : row + geo.slots, :
                ].astype(BF16)


def exchange(sent):
    return lax.all_to_all(sent, "dp", 0, 0)


def swapped(value):
    return lax.ppermute(value, "section", [(0, 1), (1, 0)])


def across(value, mask):
    return lax.ppermute(value, "dp", [(i, i ^ mask) for i in range(lax.axis_size("dp"))])


class Piece:
    def __init__(self, rows, columns, devices, split, width):
        self.split = split
        self.width = width
        self.rows = rows // 2 if split == "rows" else rows
        self.columns = columns if split == "rows" else columns // 2
        self.height = self.rows // devices
        self.folded = self.columns < width
        self.lines = self.height // 2 if self.folded else self.height * (self.columns // width)

    def product(self, section, left, right):
        pixels = right.shape[0]
        if self.split == "rows":
            half = pl.ds(pl.multiple_of(section * self.rows, self.rows), self.rows)
            return dot_rows(left[0:pixels, half], right[...])
        half = pl.ds(pl.multiple_of(section * self.columns, self.columns), self.columns)
        return dot_rows(left[0:pixels, :], right[:, half])

    def blocks(self):
        if self.folded:
            half = self.height // 2
            return [(0, 0, half, self.columns, 0, 0), (half, 0, half, self.columns, 0, self.columns)]
        return [
            (0, block * self.width, self.height, self.width, block * self.height, 0)
            for block in range(self.columns // self.width)
        ]


def pieces_kernel(pieces, place, *refs):
    count = len(pieces)
    inputs = refs[: 4 * count]
    send_left, keep_left, send_right, keep_right, total = refs[4 * count :]
    me, section = place[0], place[1]
    half = send_left.shape[3]
    devices = 4 * send_left.shape[1]
    line = 0
    for number, piece in enumerate(pieces):
        left, left_other, right, right_other = [
            one.get() if isinstance(one, Late) else one for one in inputs[4 * number : 4 * number + 4]
        ]
        total[0 : piece.rows, 0 : piece.columns] = piece.product(section, left, right) + piece.product(
            section, left_other, right_other
        )
        for step in range(devices):
            first, second = step & 1, (step >> 1) & 1
            for row, column, height, width, at, lane in piece.blocks():
                start = pl.multiple_of((me ^ step) * piece.height, piece.height) + row
                value = total[pl.ds(start, height), column : column + width].astype(BF16)
                to = slice(line + at, line + at + height)
                for start_lane in range(0, width, half):
                    part = value[:, start_lane : start_lane + half]
                    if lane + start_lane < half:
                        (send_left if first else keep_left).ref[second, step >> 2, to, :] = part
                    else:
                        (send_right if second else keep_right).ref[first, step >> 2, to, :] = part
        line += piece.lines


class Reduction:
    def __init__(self, place, pieces, factors, helds=None):
        devices = lax.axis_size("dp")
        helds = helds or (False,) * len(pieces)
        lines = sum(piece.lines for piece in pieces)
        shape = spec((2, devices // 4, lines, pieces[0].width // 2), BF16)
        self.pieces = pieces
        args = [place]
        for four in factors:
            args += four
        tall = max(piece.rows for piece in pieces)
        wide = max(piece.columns for piece in pieces)
        send_left, keep_left, send_right, keep_right = stage(
            lambda *refs: pieces_kernel(pieces, *refs),
            (shape,) * 4,
            "dddd",
            args,
            "s" + "".join("dddg" if held else "dddd" for held in helds),
            (pltpu.VMEM((tall, wide), F32),),
        )
        self.sent = (send_left, send_right)
        self.rest = (keep_left, keep_right)
        self.masks = (1, 2)
        self.step = 1

    def advance(self):
        self.step += 1
        if self.step == 2:
            self.sent = tuple(rest[1] + got[1] for rest, got in zip(self.rest, self.got))
            self.rest = tuple(rest[0] + got[0] for rest, got in zip(self.rest, self.got))
            self.masks = (2, 1)
        else:
            total = jnp.concatenate([rest + got for rest, got in zip(self.rest, self.got)], axis=-1)
            self.rest = (total[0],)
            self.sent = tuple(total[number] for number in range(1, total.shape[0]))
            self.masks = tuple(number << 2 for number in range(1, total.shape[0]))

    def fly(self):
        self.got = tuple(across(value, mask) for value, mask in zip(self.sent, self.masks))

    def finish(self):
        total = self.rest[0].astype(F32)
        for value in self.got:
            total = total + value.astype(F32)
        results = []
        line = 0
        for piece in self.pieces:
            blocks = [
                total[line + at : line + at + height, lane : lane + width]
                for _, _, height, width, at, lane in piece.blocks()
            ]
            results.append(
                blocks[0] if len(blocks) == 1 else jnp.concatenate(blocks, axis=0 if piece.folded else 1)
            )
            line += piece.lines
        return results


def body(
    images,
    out_grad,
    live_counts,
    w_reduce0,
    w_short,
    short_gain,
    short_bias,
    w_reduce1,
    w_mid,
    w_expand,
    gain_narrow,
    bias_narrow,
    gain_wide,
    bias_wide,
):
    section = lax.axis_index("section")
    dp_index = lax.axis_index("dp")
    devices = lax.axis_size("dp")
    slots = images.shape[1]
    side = images.shape[2] // 2
    geo = Geometry(slots, side)
    c_in = images.shape[4]
    mid = w_mid.shape[2]
    out = w_expand.shape[2]
    rows = geo.rows
    all_rows = 4 * rows
    place = jnp.stack([dp_index, section]).astype(jnp.int32)

    def bound(kernel, *fixed):
        def run(*refs):
            kernel(geo, *fixed, *refs)

        return run

    own_narrow = jnp.concatenate([gain_narrow[0], bias_narrow[0]], axis=0)
    own_wide = jnp.concatenate([gain_wide, bias_wide], axis=0)
    mid_other = swapped(w_mid)
    expand_other = swapped(w_expand)
    other_narrow = swapped(own_narrow)
    other_wide = swapped(own_wide)
    front = section == 0
    narrow0 = jnp.where(front, own_narrow, other_narrow)
    narrow1 = jnp.where(front, other_narrow, own_narrow)
    wide0 = jnp.where(front, own_wide, other_wide)
    wide1 = jnp.where(front, other_wide, own_wide)
    short = jnp.stack([short_gain, short_bias])
    counts = live_counts.T
    images = images.transpose(0, 2, 3, 1, 4)
    out_grad = out_grad.transpose(0, 2, 3, 1, 4)

    def dma(number):
        return pltpu.SemaphoreType.DMA((number,))

    piece_mid = Piece(9 * mid, mid, devices, "columns", mid)
    piece_expand = Piece(mid, out, devices, "columns", mid)
    piece_reduce1 = Piece(out, mid, devices, "rows", mid)
    piece_short = Piece(c_in, out, devices, "rows", mid)
    piece_reduce0 = Piece(c_in, mid, devices, "rows", mid)
    heights = [block[2] for piece in (piece_mid, piece_expand, piece_reduce1, piece_short, piece_reduce0) for block in piece.blocks()]
    packed = devices == 16 and all(height % 16 == 0 for height in heights)

    def partner(value, got):
        if not packed:
            return got, value
        return lax.optimization_barrier((got, swapped(value)))

    x, z1, sent = stage(
        bound(first_kernel),
        (spec((all_rows, c_in), BF16), spec((all_rows, mid)), spec((devices, 2, mid))),
        "ddd",
        (place, counts, images, w_reduce0),
        "ssad",
        (
            pltpu.VMEM((2 * side, 2 * side, slots, c_in), BF16),
            pltpu.VMEM((4, geo.line, c_in), F32),
            dma(1),
        ),
    )
    got = exchange(sent)
    zs, stats_s = stage(
        bound(short_kernel),
        (spec((rows, out)), spec((2, out))),
        "dd",
        (place, counts, x, w_short),
        "ssad",
        (pltpu.VMEM((rows, c_in), BF16), dma(1)),
    )
    tap_scratch = (pltpu.VMEM((9 * mid, mid), BF16), dma(1))
    taps0, z2, mom1, sent = stage(
        bound(tap_kernel, 4, 0),
        (spec((rows, 9 * mid), BF16), spec((rows, mid)), spec((2, mid)), spec((devices, 2, 3 * (mid + out) // 2), BF16)),
        "dddd",
        (place, counts, got, z1, narrow0, w_mid, mid_other, stats_s),
        "ssgddaad",
        (pltpu.VMEM((all_rows, mid), F32),) + tap_scratch,
    )
    got = exchange(sent)
    got, x_other = partner(x, got)
    expand_scratch = (pltpu.VMEM((mid, out), BF16), dma(1))
    a2, z3, mom2, moments_s, sent = stage(
        bound(expand_kernel, 0, True),
        (spec((rows, mid), BF16), spec((rows, out)), spec((2, mid)), spec((2, out)), spec((devices, 2, out))),
        "ddddd",
        (place, counts, got, z2, narrow0, w_expand, expand_other),
        "ssgddaa",
        expand_scratch,
    )
    got = exchange(sent)
    got, taps0_other = partner(taps0, got)
    joined, u1, mom3, sent = stage(
        bound(join_kernel),
        (spec((rows, out), BF16), spec((rows, mid)), spec((4, out)), spec((devices, 2, mid))),
        "dddd",
        (place, counts, got, z3, zs, moments_s, wide0, short, w_reduce1),
        "ssgdddddd",
    )
    got = exchange(sent)
    got, a2_other = partner(a2, got)
    taps1, u2, mom4, sent = stage(
        bound(tap_kernel, 1, 1),
        (spec((rows, 9 * mid), BF16), spec((rows, mid)), spec((2, mid)), spec((devices, 2, mid))),
        "dddd",
        (place, counts, got, u1, narrow1, w_mid, mid_other),
        "ssgddaa",
        (pltpu.VMEM((rows, mid), F32),) + tap_scratch,
    )
    got = exchange(sent)
    got, joined_other = partner(joined, got)
    c2, u3, mom5, sent = stage(
        bound(expand_kernel, 1, False),
        (spec((rows, mid), BF16), spec((rows, out)), spec((2, mid)), spec((devices, 2, out))),
        "dddd",
        (place, counts, got, u2, narrow1, w_expand, expand_other),
        "ssgddaa",
        expand_scratch,
    )
    got = exchange(sent)
    got, taps1_other = partner(taps1, got)
    block_out, g3, mom6, sent = stage(
        bound(turn_kernel),
        (
            spec((1, side, side, slots, out), BF16),
            spec((rows, out)),
            spec((2, out)),
            spec((devices, 2, out)),
        ),
        "dddd",
        (place, counts, got, u3, joined, wide1, out_grad),
        "ssgddda",
        (pltpu.VMEM((side, side, slots, out), BF16), pltpu.VMEM((rows, out), F32), dma(1)),
    )
    got = exchange(sent)
    got, c2_other = partner(c2, got)
    du3, g2, sums6, sent = stage(
        bound(expand_back, 1, False),
        (spec((rows, out), BF16), spec((rows, mid)), spec((2, out)), spec((devices, 2, mid))),
        "dddd",
        (place, counts, got, g3, u3, mom6, wide1, u2, mom5, narrow1, w_expand, expand_other),
        "ssgdddddddaa",
        expand_scratch,
    )
    got = exchange(sent)
    got, du3_other = partner(du3, got)
    tap_back_scratch = (pltpu.VMEM((rows, mid), F32),) + tap_scratch
    du2, g1, sums5, sent = stage(
        bound(tap_back, 1, 1),
        (spec((rows, mid), BF16), spec((rows, mid)), spec((2, mid)), spec((devices, 2, mid))),
        "dddd",
        (place, counts, got, g2, u2, mom5, narrow1, u1, mom4, w_mid, mid_other),
        "ssgddddddaa",
        tap_back_scratch,
    )
    got = exchange(sent)
    def tied(value, starting=(), arrived=()):
        values = lax.optimization_barrier(
            (value, tuple(one.sent for one in starting), tuple(one.got for one in arrived))
        )
        for one, sent in zip(starting, values[1]):
            one.sent = sent
            one.fly()
        for one, got in zip(arrived, values[2]):
            one.got = got
        return values[0]

    if packed:
        first = Reduction(
            place,
            (piece_expand, piece_mid),
            ((c2, c2_other, du3, du3_other), (taps1, taps1_other, du2, swapped(du2))),
            (False, True),
        )
        got = tied(got, (first,))
    du1, gj, sums4, sent = stage(
        bound(join_back),
        (spec((rows, mid), BF16), spec((rows, out)), spec((2, mid)), spec((devices, 2, out + out // 2), BF16)),
        "dddd",
        (place, counts, got, g1, u1, mom4, narrow1, w_reduce1, g3, z3, zs, mom3, wide0, short),
        "ssgddddddddddd",
    )
    got = exchange(sent)
    got, du1_other = partner(du1, got)
    if packed:
        first.advance()
        got = tied(got, (first,))
    dz3, dzs, g2, sums3, sent = stage(
        bound(expand_back, 0, True),
        (
            spec((rows, out), BF16),
            spec((rows, out), BF16),
            spec((rows, mid)),
            spec((3, out)),
            spec((devices, 2, mid)),
        ),
        "ddddd",
        (place, counts, got, gj, z3, mom3, wide0, zs, short, z2, mom2, narrow0, w_expand, expand_other),
        "ssgdddddddddaa",
        expand_scratch,
    )
    got = exchange(sent)
    if packed:
        second = Reduction(
            place,
            (piece_reduce1, piece_expand, piece_short),
            (
                (joined, joined_other, du1, du1_other),
                (a2, a2_other, dz3, swapped(dz3)),
                (x, x_other, dzs, swapped(dzs)),
            ),
            (False, True, True),
        )
        got = tied(got, (second,), (first,))
    dz2, g1, sums2, sent = stage(
        bound(tap_back, 4, 0),
        (spec((rows, mid), BF16), spec((all_rows, mid)), spec((2, mid)), spec((devices, 2, mid))),
        "dddd",
        (place, counts, got, g2, z2, mom2, narrow0, z1, mom1, w_mid, mid_other),
        "ssgddddddaa",
        tap_back_scratch,
    )
    got = exchange(sent)
    got, dz2_other = partner(dz2, got)
    if packed:
        second.advance()
        first.advance()
        got = tied(got, (second, first))
    dz1, sums1 = stage(
        bound(reduce_back),
        (spec((all_rows, mid), BF16), spec((2, mid))),
        "dd",
        (place, counts, got, g1, z1, mom1, narrow0),
        "ssgdddd",
    )
    if packed:
        third = Reduction(
            place,
            (piece_mid, piece_reduce0),
            ((taps0, taps0_other, dz2, dz2_other), (x, x_other, dz1, swapped(dz1))),
        )
        dz1 = tied(dz1, (third,), (second,))
        second.advance()
        dz1 = tied(dz1, (second,), (first,))
    wide_front = sums3[:2]
    wide_sent = jnp.concatenate([jnp.where(front, sums6, wide_front), sums3[0:1], sums3[2:3]], axis=0)
    front_narrow = jnp.stack([sums1, sums2])
    back_narrow = jnp.stack([sums4, sums5])
    narrow_sent = jnp.where(front, back_narrow, front_narrow)
    dz1, wide_sent, narrow_sent = lax.optimization_barrier((dz1, wide_sent, narrow_sent))
    wide_got = swapped(wide_sent)
    narrow_got = swapped(narrow_sent)
    (image_grad,) = stage(
        bound(image_kernel),
        (spec((1, 2 * side, 2 * side, slots, c_in), BF16),),
        "d",
        (dz1, w_reduce0, dzs, w_short),
        "dddd",
        (pltpu.VMEM((all_rows, c_in), F32),),
    )
    block_out = block_out.transpose(0, 3, 1, 2, 4)
    image_grad, wide_got, narrow_got = lax.optimization_barrier((image_grad, wide_got, narrow_got))
    wide_sums = jnp.where(front, wide_front, sums6) + wide_got[:2]
    width = out // (2 * devices)
    both_short = jnp.stack([sums3[2] + wide_got[3], sums3[0] + wide_got[2]])
    short_norm = lax.dynamic_slice_in_dim(both_short, (section * devices + dp_index) * width, width, 1)
    narrow_sums = jnp.where(front, front_narrow, back_narrow) + narrow_got
    if packed:
        expand1, mid1 = first.finish()
        image_grad = tied(image_grad, (), (third,))
        third.advance()
        image_grad = tied(image_grad, (third,))
        image_grad = tied(image_grad, (), (third,))
        third.advance()
        image_grad = tied(image_grad, (third,))
        reduce1, expand0, short_grad = second.finish()
        image_grad = tied(image_grad, (), (third,))
        mid0, reduce0 = third.finish()

        def to_owner(front_half, back_half, axis):
            mine = jnp.where(front, front_half, back_half)
            other = swapped(jnp.where(front, back_half, front_half))
            first_half = jnp.where(front, mine, other)
            second_half = jnp.where(front, other, mine)
            return jnp.concatenate([first_half, second_half], axis=axis)

        grad_mid = to_owner(mid0, mid1, 1)
        grad_expand = to_owner(expand0, expand1, 1)
    else:

        def product(left, right):
            return dot_rows(left, right).astype(BF16)

        def of_block(front_grad, back_grad):
            mine = jnp.where(front, front_grad, back_grad)
            both = mine + swapped(jnp.where(front, back_grad, front_grad))
            return lax.psum_scatter(both, "dp", scatter_dimension=0, tiled=True).astype(F32)

        def of_both(grad):
            return lax.psum_scatter(grad, ("section", "dp"), scatter_dimension=0, tiled=True).astype(F32)

        grad_mid = of_block(product(taps0, dz2), product(taps1, du2))
        grad_expand = of_block(product(a2, dz3), product(c2, du3))
        reduce1 = of_both(product(joined, du1))
        short_grad = of_both(product(x[:rows], dzs))
        reduce0 = of_both(product(x, dz1))
    return (
        block_out,
        image_grad.transpose(0, 3, 1, 2, 4),
        reduce0,
        short_grad,
        short_norm,
        reduce1,
        grad_mid[None],
        grad_expand[None],
        narrow_sums[None, :, 1],
        narrow_sums[None, :, 0],
        wide_sums[None, 1],
        wide_sums[None, 0],
    )


def solution(mesh):
    return jax.shard_map(
        body,
        mesh=mesh,
        in_specs=(
            P(None, "dp", None, None, None),
            P(None, "dp", None, None, None),
            P(),
            P(),
            P(),
            P(),
            P(),
            P(),
            P("section", None, None),
            P("section", None, None),
            P("section", None, None),
            P("section", None, None),
            P("section", None),
            P("section", None),
        ),
        out_specs=(
            P("section", "dp", None, None, None),
            P("section", "dp", None, None, None),
            P(("section", "dp"), None),
            P(("section", "dp"), None),
            P(None, ("section", "dp")),
            P(("section", "dp"), None),
            P("section", "dp", None),
            P("section", "dp", None),
            P("section", None, None),
            P("section", None, None),
            P("section", None),
            P("section", None),
        ),
        check_vma=False,
    )
```

```python
import jax
import jax.numpy as jnp
from jax import lax
from jax.experimental import pallas as pl
from jax.experimental.pallas import tpu as pltpu
from jax.sharding import PartitionSpec as P


EPSILON = 1e-05
F32 = jnp.float32
BF16 = jnp.bfloat16
VMEM = pl.BlockSpec(memory_space=pltpu.VMEM)
SMEM = pl.BlockSpec(memory_space=pltpu.SMEM)
ANY = pl.BlockSpec(memory_space=pl.ANY)


def spec(shape, dtype=F32):
    return jax.ShapeDtypeStruct(shape, dtype)


class Late:
    def __init__(self, source, target, sem):
        self.copy = pltpu.make_async_copy(source, target, sem)
        self.copy.start()
        self.target = target
        self.shape = target.shape
        self.waiting = True

    def get(self):
        if self.waiting:
            self.copy.wait()
            self.waiting = False
        return self.target

    def __getitem__(self, index):
        return self.get()[index]


class Out:
    def __init__(self, buffer, target, sem):
        self.ref = buffer
        self.shape = buffer.shape
        self.copy = pltpu.make_async_copy(buffer, target, sem)
        self.sent = False

    def __setitem__(self, index, value):
        self.ref[index] = value

    def send(self):
        self.copy.start()
        self.sent = True


def stage(kernel, outs, out_places, args, places, scratch=()):
    kinds = {"g": VMEM, "s": SMEM, "a": ANY, "d": ANY}
    late = [n for n, kind in enumerate(places) if kind == "d"]
    late_out = [n for n, kind in enumerate(out_places) if kind == "d"]
    buffers = [pltpu.VMEM(args[n].shape, args[n].dtype) for n in late]
    buffers += [pltpu.VMEM(outs[n].shape, outs[n].dtype) for n in late_out]
    args = [
        pltpu.with_memory_space_constraint(arg, pltpu.VMEM) if kind == "g" else arg
        for arg, kind in zip(args, places)
    ]

    def run(*refs):
        inputs = list(refs[: len(args)])
        results = list(refs[len(args) : len(args) + len(outs)])
        rest = refs[len(args) + len(outs) :]
        own, held, sem = rest[: len(scratch)], rest[len(scratch) : -1], rest[-1]
        for place, n in enumerate(late):
            inputs[n] = Late(inputs[n], held[place], sem.at[place])
        waiting = []
        for place, n in enumerate(late_out):
            place += len(late)
            results[n] = Out(held[place], results[n], sem.at[place])
            waiting.append(results[n])
        kernel(*inputs, *results, *own)
        for one in inputs:
            if isinstance(one, Late):
                one.get()
        for one in waiting:
            if not one.sent:
                one.send()
        for one in waiting:
            one.copy.wait()

    return pl.pallas_call(
        run,
        out_shape=list(outs),
        in_specs=[kinds[kind] for kind in places],
        out_specs=[kinds[kind] for kind in out_places],
        scratch_shapes=list(scratch) + buffers + [pltpu.SemaphoreType.DMA((max(1, len(buffers)),))],
        compiler_params=pltpu.CompilerParams(vmem_limit_bytes=58 << 20),
    )(*args)


def split(value, size):
    if size & (size - 1) == 0:
        return value >> (size.bit_length() - 1), value & (size - 1)
    return value // size, value % size


class Geometry:
    def __init__(self, slots, side):
        self.slots = slots
        self.side = side
        self.pitch = side + 1
        self.line = self.pitch * slots
        self.rows = self.pitch * self.line
        self.pixels = side * side

    def mask(self, start, step, width, count=None):
        row = start + lax.broadcasted_iota(jnp.int32, (step, 128), 0)
        position, image = split(row, self.slots)
        line, column = split(position, self.pitch)
        line = split(line, self.pitch)[1]
        good = (column < self.side) & (line < self.side)
        if count is not None:
            good = good & (image < count)
        value = jnp.where(good, 1.0, 0.0).astype(F32)
        return jnp.concatenate([value] * (width // 128), axis=1) if width > 128 else value


def over_rows(rows, step, body, init):
    def one(i, carry):
        return body(pl.multiple_of(i * step, step), carry)

    return lax.fori_loop(0, rows // step, one, init)


def fold_rows(block):
    rows, width = block.shape
    return jnp.sum(block.reshape(rows // 8, 8, width), axis=0)


def step_of(width):
    return 64 if width <= 512 else 16


def local_stats(z_ref, geo, count, planes):
    rows, width = z_ref.shape
    step = step_of(width)
    total = (count * (geo.pixels * planes)).astype(F32)

    def plain(start, acc):
        return acc + fold_rows(z_ref[pl.ds(start, step), :].astype(F32) * geo.mask(start, step, width, count))

    zero = jnp.zeros((8, width), F32)
    average = jnp.sum(over_rows(rows, step, plain, zero), axis=0, keepdims=True) / total

    def squared(start, acc):
        centered = z_ref[pl.ds(start, step), :].astype(F32) - average
        return acc + fold_rows(centered * centered * geo.mask(start, step, width, count))

    spread = jnp.sum(over_rows(rows, step, squared, zero), axis=0, keepdims=True)
    return average, spread


def send_short(out_ref, values):
    values = values.astype(BF16)
    for device in range(out_ref.shape[0]):
        out_ref[device] = values


def packed_stats(pairs):
    average = jnp.concatenate([pair[0] for pair in pairs], axis=1)
    spread = jnp.concatenate([pair[1] for pair in pairs], axis=1)
    high = average.astype(BF16).astype(F32)
    half = spread.shape[1] // 2
    return jnp.concatenate(
        [
            jnp.concatenate([high, spread[:, :half]], axis=1),
            jnp.concatenate([average - high, spread[:, half:]], axis=1),
        ],
        axis=0,
    )


class Unpacked:
    def __init__(self, got):
        self.devices = got.shape[0]
        width = got.shape[2] * 2 // 3
        self.average, self.spread = [], []
        for device in range(self.devices):
            rows = got[device].astype(F32)
            self.average.append(rows[0:1, :width] + rows[1:2, :width])
            self.spread.append(jnp.concatenate([rows[0:1, width:], rows[1:2, width:]], axis=1))
        self.shape = (self.devices, 2, width)

    def __getitem__(self, index):
        device, row, lanes = index
        return (self.average if row.start == 0 else self.spread)[device][:, lanes]


def send_rows(out_ref, values):
    lane = 0
    for pair in values:
        width = pair[0].shape[1]
        for row, value in enumerate(pair):
            for device in range(out_ref.shape[0]):
                out_ref[device, row : row + 1, lane : lane + width] = value
        lane += width


def total_of(counts, section, pixels):
    total = counts[section, 0]
    for device in range(1, counts.shape[1]):
        total = total + counts[section, device]
    return (total * pixels).astype(F32)


def combined(got_ref, lanes, counts, section, pixels):
    devices = got_ref.shape[0]
    total = total_of(counts, section, pixels)
    sizes = [(counts[section, device] * pixels).astype(F32) for device in range(devices)]
    average = sizes[0] * got_ref[0, 0:1, lanes]
    for device in range(1, devices):
        average = average + sizes[device] * got_ref[device, 0:1, lanes]
    average = average / total
    spread = jnp.zeros_like(average)
    for device in range(devices):
        apart = got_ref[device, 0:1, lanes] - average
        spread = spread + (got_ref[device, 1:2, lanes] + sizes[device] * (apart * apart))
    return average, lax.rsqrt(spread / total + EPSILON)


def summed(got_ref):
    total = got_ref[0].astype(F32)
    for device in range(1, got_ref.shape[0]):
        total = total + got_ref[device].astype(F32)
    return total


def sigmoid(values):
    return 1.0 / (1.0 + jnp.exp(-values))


def slope(values):
    part = sigmoid(values)
    return part * (1.0 + values * (1.0 - part))


class Choice:
    def __init__(self, section, wanted, own, other, target, sem):
        self.mine = section == wanted
        self.copies = (
            pltpu.make_async_copy(own.at[0], target, sem),
            pltpu.make_async_copy(other.at[0], target, sem),
        )

    def start(self):
        @pl.when(self.mine)
        def _():
            self.copies[0].start()

        @pl.when(jnp.logical_not(self.mine))
        def _():
            self.copies[1].start()

    def wait(self):
        @pl.when(self.mine)
        def _():
            self.copies[0].wait()

        @pl.when(jnp.logical_not(self.mine))
        def _():
            self.copies[1].wait()


def dot(left, right):
    return jnp.dot(left, right, preferred_element_type=F32)


def dot_back(left, right):
    return lax.dot_general(left, right, (((1,), (1,)), ((), ())), preferred_element_type=F32)


def dot_rows(left, right):
    return lax.dot_general(left, right, (((0,), (0,)), ((), ())), preferred_element_type=F32)


def turned(values, shift):
    shift = shift % values.shape[0]
    if shift == 0:
        return values
    return jnp.concatenate([values[-shift:], values[:-shift]], axis=0)


def taps_of(stride):
    found = []
    for tap_row in range(3):
        for column in range(3):
            if stride == 1:
                found.append((0, tap_row - 1, column - 1))
            else:
                plane = 2 * (tap_row != 1) + (column != 1)
                found.append((plane, -(tap_row == 0), -(column == 0)))
    return found


def first_kernel(geo, place, counts, images, weight, x_out, z_out, sent, raw, slabs, sem):
    section = place[1]
    count = counts[section, place[0]]
    load = pltpu.make_async_copy(images.at[section], raw, sem.at[0])
    load.start()
    used = geo.side * geo.slots
    x_ref = x_out.ref
    for plane in range(4):
        last = (plane + 1) * geo.rows
        x_ref[last - geo.line : last, :] = jnp.zeros((geo.line, x_ref.shape[1]), BF16)
        slabs[plane, used : geo.line, :] = jnp.zeros((geo.slots, x_ref.shape[1]), F32)
    load.wait()
    for line in range(geo.side):
        for plane in range(4):
            for column in range(geo.side):
                at = column * geo.slots
                slabs[plane, at : at + geo.slots, :] = raw[
                    2 * line + plane // 2, 2 * column + plane % 2
                ].astype(F32)
            at = plane * geo.rows + line * geo.line
            x_ref[at : at + geo.line, :] = slabs[plane].astype(BF16)
    x_out.send()
    weight = weight.get()
    z_ref = z_out.ref
    for plane in range(4):
        at = plane * geo.rows
        z_ref[at : at + geo.rows, :] = dot(x_ref[at : at + geo.rows, :], weight[...]).astype(z_ref.dtype)
    z_out.send()
    send_rows(sent, (local_stats(z_ref, geo, count, 4),))


def short_kernel(geo, place, counts, x_any, weight, z_out, stats, x_vmem, sem):
    count = counts[place[1], place[0]]
    load = pltpu.make_async_copy(x_any.at[pl.ds(0, geo.rows)], x_vmem, sem.at[0])
    load.start()
    load.wait()
    z_ref = z_out.ref
    z_ref[...] = dot(x_vmem[...], weight.get()[...]).astype(BF16)
    z_out.send()
    average, spread = local_stats(z_ref, geo, count, 1)
    stats[0:1, :] = average
    stats[1:2, :] = spread


def tap_kernel(geo, planes, block, place, counts, got, z_in, narrow, own, other, *rest):
    if planes == 4:
        stats, taps, z_out, moments, sent, active, weight, sem = rest
    else:
        taps, z_out, moments, sent, active, weight, sem = rest
    section = place[1]
    count = counts[section, place[0]]
    choice = Choice(section, block, own, other, weight, sem.at[0])
    choice.start()
    average, inverse = combined(got, slice(None), counts, section, geo.pixels * planes)
    moments[0:1, :] = average
    moments[1:2, :] = inverse
    gain = narrow[0:1, :] * inverse
    offset = narrow[2:3, :]
    z_ref = z_in.get()
    rows_of, width = z_ref.shape

    def activate(start, carry):
        pre = (z_ref[pl.ds(start, 64), :].astype(F32) - average) * gain + offset
        active[pl.ds(start, 64), :] = pre * sigmoid(pre) * geo.mask(start, 64, width)
        return carry

    over_rows(rows_of, 64, activate, 0)
    ready = {}
    for tap, (plane, line, column) in enumerate(taps_of(2 if planes == 4 else 1)):
        if (plane, column) not in ready:
            values = active[plane * geo.rows : (plane + 1) * geo.rows, :]
            if column != 0:
                values = pltpu.roll(values, (-column * geo.slots) % geo.rows, 0)
            ready[plane, column] = values.astype(BF16)
        taps.ref[:, tap * width : (tap + 1) * width] = turned(ready[plane, column], -line * geo.line)
    taps.send()
    choice.wait()
    z_out.ref[...] = dot(taps.ref[...], weight[...])
    z_out.send()
    values = local_stats(z_out.ref, geo, count, 1)
    if planes == 4:
        send_short(sent, packed_stats((values, (stats[0:1, :], stats[1:2, :]))))
    else:
        send_rows(sent, (values,))


def expand_kernel(geo, block, extra, place, counts, got, z_in, narrow, own, other, *rest):
    if extra:
        a_out, z_out, moments, moments_s, sent, weight, sem = rest
    else:
        a_out, z_out, moments, sent, weight, sem = rest
    section = place[1]
    count = counts[section, place[0]]
    choice = Choice(section, block, own, other, weight, sem.at[0])
    choice.start()
    if extra:
        got = Unpacked(got)
    average, inverse = combined(got, slice(0, z_in.shape[1]), counts, section, geo.pixels)
    moments[0:1, :] = average
    moments[1:2, :] = inverse
    gain = narrow[1:2, :] * inverse
    offset = narrow[3:4, :]
    z_ref = z_in.get()

    def activate(start, carry):
        pre = (z_ref[pl.ds(start, 64), :] - average) * gain + offset
        a_out.ref[pl.ds(start, 64), :] = (pre * sigmoid(pre)).astype(BF16)
        return carry

    over_rows(geo.rows, 64, activate, 0)
    a_out.send()
    choice.wait()
    z_out.ref[...] = dot(a_out.ref[...], weight[...]).astype(BF16)
    z_out.send()
    send_rows(sent, (local_stats(z_out.ref, geo, count, 1),))
    sent.send()
    if extra:
        lanes = slice(z_ref.shape[1], got.shape[2])
        for row, value in enumerate(combined(got, lanes, counts, section, geo.pixels)):
            moments_s[row : row + 1, :] = value


def join_kernel(geo, place, counts, got, z3, zs, moments_s, wide, short, weight, joined, u_out, moments, sent):
    section = place[1]
    count = counts[section, place[0]]
    average_c, inverse_c = combined(got, slice(None), counts, section, geo.pixels)
    average_s, inverse_s = moments_s[0:1, :], moments_s[1:2, :]
    for number, value in enumerate((average_c, inverse_c, average_s, inverse_s)):
        moments[number : number + 1, :] = value
    gain_c = wide[0:1, :] * inverse_c
    gain_s = short[0:1, :] * inverse_s
    offset = wide[1:2, :] + short[1:2, :]
    z3, zs = z3.get(), zs.get()

    def activate(start, carry):
        rows = pl.ds(start, 16)
        pre = (
            (z3[rows, :].astype(F32) - average_c) * gain_c
            + (zs[rows, :].astype(F32) - average_s) * gain_s
            + offset
        )
        joined.ref[rows, :] = (pre * sigmoid(pre)).astype(BF16)
        return carry

    over_rows(geo.rows, 16, activate, 0)
    joined.send()
    u_out.ref[...] = dot(joined.ref[...], weight.get()[...])
    u_out.send()
    send_rows(sent, (local_stats(u_out.ref, geo, count, 1),))


def turn_kernel(geo, place, counts, got, u3, joined, wide, out_grad, block_out, g_out, moments, sent, raw, flat, sem):
    section = place[1]
    count = counts[section, place[0]]
    load = pltpu.make_async_copy(out_grad.at[section], raw, sem.at[0])
    load.start()
    average, inverse = combined(got, slice(None), counts, section, geo.pixels)
    moments[0:1, :] = average
    moments[1:2, :] = inverse
    g_ref = flat
    width = g_ref.shape[1]
    empty = jnp.zeros((geo.slots, width), F32)
    for line in range(geo.side):
        at = line * geo.line + geo.side * geo.slots
        g_ref[at : at + geo.slots, :] = empty
    g_ref[geo.rows - geo.line : geo.rows, :] = jnp.zeros((geo.line, width), F32)
    load.wait()
    for line in range(geo.side):
        for column in range(geo.side):
            at = line * geo.line + column * geo.slots
            g_ref[at : at + geo.slots, :] = raw[line, column].astype(F32)
    weight = wide[0:1, :]
    offset = wide[1:2, :]
    u3, joined = u3.get(), joined.get()

    def activate(start, carry):
        plain, scaled = carry
        rows = pl.ds(start, 16)
        normed = (u3[rows, :].astype(F32) - average) * inverse
        pre = normed * weight + offset + joined[rows, :].astype(F32)
        part = sigmoid(pre)
        upstream = g_ref[rows, :] * geo.mask(start, 16, width, count) * (part * (1.0 + pre * (1.0 - part)))
        flat[rows, :] = pre * part
        g_out.ref[rows, :] = upstream.astype(BF16)
        return plain + fold_rows(upstream), scaled + fold_rows(upstream * normed)

    zero = jnp.zeros((8, width), F32)
    plain, scaled = over_rows(geo.rows, 16, activate, (zero, zero))
    g_out.send()
    send_rows(sent, ((jnp.sum(plain, axis=0, keepdims=True), jnp.sum(scaled, axis=0, keepdims=True)),))
    sent.send()
    for line in range(geo.side):
        for column in range(geo.side):
            at = line * geo.line + column * geo.slots
            block_out.ref[0, line, column] = flat[at : at + geo.slots, :].astype(BF16)


def norm_grad(geo, rows_of, z_ref, g_ref, average, inverse, gain, plain, scaled, total, count, out_ref):
    width = z_ref.shape[1]
    step = step_of(width)
    factor = gain * inverse
    plain_part = plain / total
    scaled_part = scaled / total * inverse

    def one(start, carry):
        rows = pl.ds(start, step)
        centered = z_ref[rows, :].astype(F32) - average
        value = factor * (g_ref[rows, :].astype(F32) - plain_part - centered * scaled_part)
        out_ref[rows, :] = (value * geo.mask(start, step, width, count)).astype(out_ref.dtype)
        return carry

    over_rows(rows_of, step, one, 0)


def silu_back(geo, z_ref, average, inverse, gain, offset, g_ref, out_ref):
    rows_of, width = z_ref.shape
    step = step_of(width)

    def one(start, carry):
        plain, scaled = carry
        rows = pl.ds(start, step)
        normed = (z_ref[rows, :].astype(F32) - average) * inverse
        upstream = g_ref[rows, :] * slope(normed * gain + offset) * geo.mask(start, step, width)
        out_ref[rows, :] = upstream.astype(out_ref.dtype)
        return plain + fold_rows(upstream), scaled + fold_rows(upstream * normed)

    zero = jnp.zeros((8, width), F32)
    plain, scaled = over_rows(rows_of, step, one, (zero, zero))
    return jnp.sum(plain, axis=0, keepdims=True), jnp.sum(scaled, axis=0, keepdims=True)


def expand_back(geo, block, two, place, counts, got, g_in, z3, mom3, wide, *rest):
    if two:
        zs, short, z2, mom2, narrow, own, other, dv, dvs, g_out, sums, sent, weight, sem = rest
    else:
        z2, mom2, narrow, own, other, dv, g_out, sums, sent, weight, sem = rest
    section = place[1]
    count = counts[section, place[0]]
    choice = Choice(section, block, own, other, weight, sem.at[0])
    choice.start()
    total = total_of(counts, section, geo.pixels)
    main = dv.shape[1]
    both = summed(got)
    plain, scaled = both[0:1, :main], both[1:2, :main]
    sums[0:1, :] = plain
    sums[1:2, :] = scaled
    g_ref = g_in.get()
    norm_grad(
        geo, geo.rows, z3.get(), g_ref, mom3[0:1, :], mom3[1:2, :], wide[0:1, :], plain, scaled, total, count, dv.ref
    )
    dv.send()
    choice.wait()
    g_out.ref[...] = dot_back(dv.ref[...], weight[...])
    send_rows(
        sent,
        (
            silu_back(
                geo, z2.get(), mom2[0:1, :], mom2[1:2, :], narrow[1:2, :], narrow[3:4, :], g_out.ref, g_out.ref
            ),
        ),
    )
    sent.send()
    g_out.send()
    if two:
        scaled = jnp.concatenate([both[0:1, main:], both[1:2, main:]], axis=1)
        sums[2:3, :] = scaled
        norm_grad(
            geo, geo.rows, zs.get(), g_ref, mom3[2:3, :], mom3[3:4, :], short[0:1, :], plain, scaled, total, count,
            dvs.ref,
        )
        dvs.send()


def tap_back(geo, planes, block, place, counts, got, g_in, z2, mom2, narrow, z1, mom1, own, other, dv, g_out, sums, sent,
             work, wide_dv, weight, sem):
    section = place[1]
    count = counts[section, place[0]]
    choice = Choice(section, block, own, other, weight, sem.at[0])
    choice.start()
    total = total_of(counts, section, geo.pixels)
    both = summed(got)
    plain, scaled = both[0:1, :], both[1:2, :]
    sums[0:1, :] = plain
    sums[1:2, :] = scaled
    norm_grad(
        geo, geo.rows, z2.get(), g_in.get(), mom2[0:1, :], mom2[1:2, :], narrow[1:2, :], plain, scaled, total, count,
        wide_dv,
    )
    dv.ref[...] = wide_dv[...].astype(BF16)
    dv.send()
    choice.wait()
    width = work.shape[1]
    ready = {}
    totals = [None] * planes
    for tap, (plane, line, column) in enumerate(taps_of(2 if planes == 4 else 1)):
        if column not in ready:
            values = wide_dv[...]
            if column != 0:
                values = pltpu.roll(values, (column * geo.slots) % geo.rows, 0)
            ready[column] = values.astype(BF16)
        left = turned(ready[column], line * geo.line)
        product = dot_back(left, weight[tap * width : (tap + 1) * width, :])
        totals[plane] = product if totals[plane] is None else totals[plane] + product
    for plane in range(planes):
        work[plane * geo.rows : (plane + 1) * geo.rows, :] = totals[plane]
    send_rows(
        sent,
        (
            silu_back(
                geo, z1.get(), mom1[0:1, :], mom1[1:2, :], narrow[0:1, :], narrow[2:3, :], work, g_out.ref
            ),
        ),
    )


def join_back(geo, place, counts, got, g_in, u1, mom4, narrow, weight, g3, z3, zs, mom3, wide, short, dv, g_out, sums,
              sent, flat):
    section = place[1]
    count = counts[section, place[0]]
    total = total_of(counts, section, geo.pixels)
    both = summed(got)
    plain, scaled = both[0:1, :], both[1:2, :]
    sums[0:1, :] = plain
    sums[1:2, :] = scaled
    norm_grad(
        geo, geo.rows, u1.get(), g_in.get(), mom4[0:1, :], mom4[1:2, :], narrow[0:1, :], plain, scaled, total, count,
        dv.ref,
    )
    dv.send()
    flat[...] = dot_back(dv.ref[...], weight.get()[...])
    average_c, inverse_c = mom3[0:1, :], mom3[1:2, :]
    average_s, inverse_s = mom3[2:3, :], mom3[3:4, :]
    gain_c, gain_s = wide[0:1, :], short[0:1, :]
    offset = wide[1:2, :] + short[1:2, :]
    width = flat.shape[1]
    g3, z3, zs = g3.get(), z3.get(), zs.get()

    def one(start, carry):
        plain, scaled_c, scaled_s = carry
        rows = pl.ds(start, 16)
        normed_c = (z3[rows, :].astype(F32) - average_c) * inverse_c
        normed_s = (zs[rows, :].astype(F32) - average_s) * inverse_s
        arrived = (flat[rows, :] + g3[rows, :].astype(F32)).astype(BF16).astype(F32)
        upstream = arrived * slope(normed_c * gain_c + normed_s * gain_s + offset) * geo.mask(start, 16, width)
        g_out.ref[rows, :] = upstream.astype(BF16)
        return (
            plain + fold_rows(upstream),
            scaled_c + fold_rows(upstream * normed_c),
            scaled_s + fold_rows(upstream * normed_s),
        )

    zero = jnp.zeros((8, width), F32)
    results = over_rows(geo.rows, 16, one, (zero, zero, zero))
    g_out.send()
    plain, scaled_c, scaled_s = [jnp.sum(value, axis=0, keepdims=True) for value in results]
    half = width // 2
    send_short(
        sent,
        jnp.concatenate(
            [
                jnp.concatenate([plain, scaled_s[:, :half]], axis=1),
                jnp.concatenate([scaled_c, scaled_s[:, half:]], axis=1),
            ],
            axis=0,
        ),
    )


def reduce_back(geo, place, counts, got, g_in, z1, mom1, narrow, dv, sums):
    section = place[1]
    count = counts[section, place[0]]
    total = total_of(counts, section, geo.pixels * 4)
    both = summed(got)
    plain, scaled = both[0:1, :], both[1:2, :]
    sums[0:1, :] = plain
    sums[1:2, :] = scaled
    norm_grad(
        geo, 4 * geo.rows, z1.get(), g_in.get(), mom1[0:1, :], mom1[1:2, :], narrow[0:1, :], plain, scaled, total, count,
        dv.ref,
    )


def image_kernel(geo, dv, weight, dvs, weight_s, image_grad, flat):
    dv, weight = dv.get(), weight.get()
    for plane in (1, 2, 3, 0):
        at = plane * geo.rows
        product = dot_back(dv[at : at + geo.rows, :], weight[...])
        if plane == 0:
            product = product + dot_back(dvs.get()[...], weight_s.get()[...])
        flat[at : at + geo.rows, :] = product
        for line in range(geo.side):
            for column in range(geo.side):
                row = at + line * geo.line + column * geo.slots
                image_grad.ref[0, 2 * line + plane // 2, 2 * column + plane % 2] = flat[
                    row : row + geo.slots, :
                ].astype(BF16)


def exchange(sent):
    return lax.all_to_all(sent, "dp", 0, 0)


def swapped(value):
    return lax.ppermute(value, "section", [(0, 1), (1, 0)])


def across(value, mask):
    return lax.ppermute(value, "dp", [(i, i ^ mask) for i in range(lax.axis_size("dp"))])


class Piece:
    def __init__(self, rows, columns, devices, split, width):
        self.split = split
        self.width = width
        self.rows = rows // 2 if split == "rows" else rows
        self.columns = columns if split == "rows" else columns // 2
        self.height = self.rows // devices
        self.folded = self.columns < width
        self.lines = self.height // 2 if self.folded else self.height * (self.columns // width)

    def product(self, section, left, right):
        pixels = right.shape[0]
        if self.split == "rows":
            half = pl.ds(pl.multiple_of(section * self.rows, self.rows), self.rows)
            return dot_rows(left[0:pixels, half], right[...])
        half = pl.ds(pl.multiple_of(section * self.columns, self.columns), self.columns)
        return dot_rows(left[0:pixels, :], right[:, half])

    def blocks(self):
        if self.folded:
            half = self.height // 2
            return [(0, 0, half, self.columns, 0, 0), (half, 0, half, self.columns, 0, self.columns)]
        return [
            (0, block * self.width, self.height, self.width, block * self.height, 0)
            for block in range(self.columns // self.width)
        ]


def pieces_kernel(pieces, place, *refs):
    count = len(pieces)
    inputs = refs[: 4 * count]
    send_left, keep_left, send_right, keep_right, total = refs[4 * count :]
    me, section = place[0], place[1]
    half = send_left.shape[3]
    devices = 4 * send_left.shape[1]
    line = 0
    for number, piece in enumerate(pieces):
        left, left_other, right, right_other = [
            one.get() if isinstance(one, Late) else one for one in inputs[4 * number : 4 * number + 4]
        ]
        total[0 : piece.rows, 0 : piece.columns] = piece.product(section, left, right) + piece.product(
            section, left_other, right_other
        )
        for step in range(devices):
            first, second = step & 1, (step >> 1) & 1
            for row, column, height, width, at, lane in piece.blocks():
                start = pl.multiple_of((me ^ step) * piece.height, piece.height) + row
                value = total[pl.ds(start, height), column : column + width].astype(BF16)
                to = slice(line + at, line + at + height)
                for start_lane in range(0, width, half):
                    part = value[:, start_lane : start_lane + half]
                    if lane + start_lane < half:
                        (send_left if first else keep_left).ref[second, step >> 2, to, :] = part
                    else:
                        (send_right if second else keep_right).ref[first, step >> 2, to, :] = part
        line += piece.lines


class Reduction:
    def __init__(self, place, pieces, factors, helds=None):
        devices = lax.axis_size("dp")
        helds = helds or (False,) * len(pieces)
        lines = sum(piece.lines for piece in pieces)
        shape = spec((2, devices // 4, lines, pieces[0].width // 2), BF16)
        self.pieces = pieces
        args = [place]
        for four in factors:
            args += four
        tall = max(piece.rows for piece in pieces)
        wide = max(piece.columns for piece in pieces)
        send_left, keep_left, send_right, keep_right = stage(
            lambda *refs: pieces_kernel(pieces, *refs),
            (shape,) * 4,
            "dddd",
            args,
            "s" + "".join("dddg" if held else "dddd" for held in helds),
            (pltpu.VMEM((tall, wide), F32),),
        )
        self.sent = (send_left, send_right)
        self.rest = (keep_left, keep_right)
        self.masks = (1, 2)
        self.step = 1

    def advance(self):
        self.step += 1
        if self.step == 2:
            self.sent = tuple(rest[1] + got[1] for rest, got in zip(self.rest, self.got))
            self.rest = tuple(rest[0] + got[0] for rest, got in zip(self.rest, self.got))
            self.masks = (2, 1)
        else:
            total = jnp.concatenate([rest + got for rest, got in zip(self.rest, self.got)], axis=-1)
            self.rest = (total[0],)
            self.sent = tuple(total[number] for number in range(1, total.shape[0]))
            self.masks = tuple(number << 2 for number in range(1, total.shape[0]))

    def fly(self):
        self.got = tuple(across(value, mask) for value, mask in zip(self.sent, self.masks))

    def finish(self):
        total = self.rest[0].astype(F32)
        for value in self.got:
            total = total + value.astype(F32)
        results = []
        line = 0
        for piece in self.pieces:
            blocks = [
                total[line + at : line + at + height, lane : lane + width]
                for _, _, height, width, at, lane in piece.blocks()
            ]
            results.append(
                blocks[0] if len(blocks) == 1 else jnp.concatenate(blocks, axis=0 if piece.folded else 1)
            )
            line += piece.lines
        return results


def body(
    images,
    out_grad,
    live_counts,
    w_reduce0,
    w_short,
    short_gain,
    short_bias,
    w_reduce1,
    w_mid,
    w_expand,
    gain_narrow,
    bias_narrow,
    gain_wide,
    bias_wide,
):
    section = lax.axis_index("section")
    dp_index = lax.axis_index("dp")
    devices = lax.axis_size("dp")
    slots = images.shape[1]
    side = images.shape[2] // 2
    geo = Geometry(slots, side)
    c_in = images.shape[4]
    mid = w_mid.shape[2]
    out = w_expand.shape[2]
    rows = geo.rows
    all_rows = 4 * rows
    place = jnp.stack([dp_index, section]).astype(jnp.int32)

    def bound(kernel, *fixed):
        def run(*refs):
            kernel(geo, *fixed, *refs)

        return run

    own_narrow = jnp.concatenate([gain_narrow[0], bias_narrow[0]], axis=0)
    own_wide = jnp.concatenate([gain_wide, bias_wide], axis=0)
    mid_other = swapped(w_mid)
    expand_other = swapped(w_expand)
    other_narrow = swapped(own_narrow)
    other_wide = swapped(own_wide)
    front = section == 0
    narrow0 = jnp.where(front, own_narrow, other_narrow)
    narrow1 = jnp.where(front, other_narrow, own_narrow)
    wide0 = jnp.where(front, own_wide, other_wide)
    wide1 = jnp.where(front, other_wide, own_wide)
    short = jnp.stack([short_gain, short_bias])
    counts = live_counts.T
    images = images.transpose(0, 2, 3, 1, 4)
    out_grad = out_grad.transpose(0, 2, 3, 1, 4)

    def dma(number):
        return pltpu.SemaphoreType.DMA((number,))

    piece_mid = Piece(9 * mid, mid, devices, "columns", mid)
    piece_expand = Piece(mid, out, devices, "columns", mid)
    piece_reduce1 = Piece(out, mid, devices, "rows", mid)
    piece_short = Piece(c_in, out, devices, "rows", mid)
    piece_reduce0 = Piece(c_in, mid, devices, "rows", mid)
    heights = [block[2] for piece in (piece_mid, piece_expand, piece_reduce1, piece_short, piece_reduce0) for block in piece.blocks()]
    packed = devices == 16 and all(height % 16 == 0 for height in heights)

    def partner(value, got):
        if not packed:
            return got, value
        return lax.optimization_barrier((got, swapped(value)))

    x, z1, sent = stage(
        bound(first_kernel),
        (spec((all_rows, c_in), BF16), spec((all_rows, mid), BF16), spec((devices, 2, mid))),
        "ddd",
        (place, counts, images, w_reduce0),
        "ssad",
        (
            pltpu.VMEM((2 * side, 2 * side, slots, c_in), BF16),
            pltpu.VMEM((4, geo.line, c_in), F32),
            dma(1),
        ),
    )
    got = exchange(sent)
    zs, stats_s = stage(
        bound(short_kernel),
        (spec((rows, out), BF16), spec((2, out))),
        "dd",
        (place, counts, x, w_short),
        "ssad",
        (pltpu.VMEM((rows, c_in), BF16), dma(1)),
    )
    tap_scratch = (pltpu.VMEM((9 * mid, mid), BF16), dma(1))
    taps0, z2, mom1, sent = stage(
        bound(tap_kernel, 4, 0),
        (spec((rows, 9 * mid), BF16), spec((rows, mid)), spec((2, mid)), spec((devices, 2, 3 * (mid + out) // 2), BF16)),
        "dddd",
        (place, counts, got, z1, narrow0, w_mid, mid_other, stats_s),
        "ssgddaad",
        (pltpu.VMEM((all_rows, mid), F32),) + tap_scratch,
    )
    got = exchange(sent)
    got, x_other = partner(x, got)
    expand_scratch = (pltpu.VMEM((mid, out), BF16), dma(1))
    a2, z3, mom2, moments_s, sent = stage(
        bound(expand_kernel, 0, True),
        (spec((rows, mid), BF16), spec((rows, out), BF16), spec((2, mid)), spec((2, out)), spec((devices, 2, out))),
        "ddddd",
        (place, counts, got, z2, narrow0, w_expand, expand_other),
        "ssgddaa",
        expand_scratch,
    )
    got = exchange(sent)
    got, taps0_other = partner(taps0, got)
    joined, u1, mom3, sent = stage(
        bound(join_kernel),
        (spec((rows, out), BF16), spec((rows, mid)), spec((4, out)), spec((devices, 2, mid))),
        "dddd",
        (place, counts, got, z3, zs, moments_s, wide0, short, w_reduce1),
        "ssgdddddd",
    )
    got = exchange(sent)
    got, a2_other = partner(a2, got)
    taps1, u2, mom4, sent = stage(
        bound(tap_kernel, 1, 1),
        (spec((rows, 9 * mid), BF16), spec((rows, mid)), spec((2, mid)), spec((devices, 2, mid))),
        "dddd",
        (place, counts, got, u1, narrow1, w_mid, mid_other),
        "ssgddaa",
        (pltpu.VMEM((rows, mid), F32),) + tap_scratch,
    )
    got = exchange(sent)
    got, joined_other = partner(joined, got)
    c2, u3, mom5, sent = stage(
        bound(expand_kernel, 1, False),
        (spec((rows, mid), BF16), spec((rows, out), BF16), spec((2, mid)), spec((devices, 2, out))),
        "dddd",
        (place, counts, got, u2, narrow1, w_expand, expand_other),
        "ssgddaa",
        expand_scratch,
    )
    got = exchange(sent)
    got, taps1_other = partner(taps1, got)
    block_out, g3, mom6, sent = stage(
        bound(turn_kernel),
        (
            spec((1, side, side, slots, out), BF16),
            spec((rows, out), BF16),
            spec((2, out)),
            spec((devices, 2, out)),
        ),
        "dddd",
        (place, counts, got, u3, joined, wide1, out_grad),
        "ssgddda",
        (pltpu.VMEM((side, side, slots, out), BF16), pltpu.VMEM((rows, out), F32), dma(1)),
    )
    got = exchange(sent)
    got, c2_other = partner(c2, got)
    du3, g2, sums6, sent = stage(
        bound(expand_back, 1, False),
        (spec((rows, out), BF16), spec((rows, mid)), spec((2, out)), spec((devices, 2, mid))),
        "dddd",
        (place, counts, got, g3, u3, mom6, wide1, u2, mom5, narrow1, w_expand, expand_other),
        "ssgdddddddaa",
        expand_scratch,
    )
    got = exchange(sent)
    got, du3_other = partner(du3, got)
    tap_back_scratch = (pltpu.VMEM((rows, mid), F32),) + tap_scratch
    du2, g1, sums5, sent = stage(
        bound(tap_back, 1, 1),
        (spec((rows, mid), BF16), spec((rows, mid)), spec((2, mid)), spec((devices, 2, mid))),
        "dddd",
        (place, counts, got, g2, u2, mom5, narrow1, u1, mom4, w_mid, mid_other),
        "ssgddddddaa",
        (pltpu.VMEM((rows, mid), F32),) + tap_back_scratch,
    )
    got = exchange(sent)
    def tied(value, starting=(), arrived=()):
        values = lax.optimization_barrier(
            (value, tuple(one.sent for one in starting), tuple(one.got for one in arrived))
        )
        for one, sent in zip(starting, values[1]):
            one.sent = sent
            one.fly()
        for one, got in zip(arrived, values[2]):
            one.got = got
        return values[0]

    if packed:
        first = Reduction(
            place,
            (piece_expand, piece_mid),
            ((c2, c2_other, du3, du3_other), (taps1, taps1_other, du2, swapped(du2))),
            (False, True),
        )
        got = tied(got, (first,))
    du1, gj, sums4, sent = stage(
        bound(join_back),
        (spec((rows, mid), BF16), spec((rows, out), BF16), spec((2, mid)), spec((devices, 2, out + out // 2), BF16)),
        "dddd",
        (place, counts, got, g1, u1, mom4, narrow1, w_reduce1, g3, z3, zs, mom3, wide0, short),
        "ssgddddddddddd",
        (pltpu.VMEM((rows, out), F32),),
    )
    got = exchange(sent)
    got, du1_other = partner(du1, got)
    if packed:
        first.advance()
        got = tied(got, (first,))
    dz3, dzs, g2, sums3, sent = stage(
        bound(expand_back, 0, True),
        (
            spec((rows, out), BF16),
            spec((rows, out), BF16),
            spec((rows, mid)),
            spec((3, out)),
            spec((devices, 2, mid)),
        ),
        "ddddd",
        (place, counts, got, gj, z3, mom3, wide0, zs, short, z2, mom2, narrow0, w_expand, expand_other),
        "ssgdddddddddaa",
        expand_scratch,
    )
    got = exchange(sent)
    if packed:
        second = Reduction(
            place,
            (piece_reduce1, piece_expand, piece_short),
            (
                (joined, joined_other, du1, du1_other),
                (a2, a2_other, dz3, swapped(dz3)),
                (x, x_other, dzs, swapped(dzs)),
            ),
            (False, True, True),
        )
        got = tied(got, (second,), (first,))
    dz2, g1, sums2, sent = stage(
        bound(tap_back, 4, 0),
        (spec((rows, mid), BF16), spec((all_rows, mid), BF16), spec((2, mid)), spec((devices, 2, mid))),
        "dddd",
        (place, counts, got, g2, z2, mom2, narrow0, z1, mom1, w_mid, mid_other),
        "ssgddddddaa",
        (pltpu.VMEM((all_rows, mid), F32),) + tap_back_scratch,
    )
    got = exchange(sent)
    got, dz2_other = partner(dz2, got)
    if packed:
        second.advance()
        first.advance()
        got = tied(got, (second, first))
    dz1, sums1 = stage(
        bound(reduce_back),
        (spec((all_rows, mid), BF16), spec((2, mid))),
        "dd",
        (place, counts, got, g1, z1, mom1, narrow0),
        "ssgdddd",
    )
    if packed:
        third = Reduction(
            place,
            (piece_mid, piece_reduce0),
            ((taps0, taps0_other, dz2, dz2_other), (x, x_other, dz1, swapped(dz1))),
        )
        dz1 = tied(dz1, (third,), (second,))
        second.advance()
        dz1 = tied(dz1, (second,), (first,))
    wide_front = sums3[:2]
    wide_sent = jnp.concatenate([jnp.where(front, sums6, wide_front), sums3[0:1], sums3[2:3]], axis=0)
    front_narrow = jnp.stack([sums1, sums2])
    back_narrow = jnp.stack([sums4, sums5])
    narrow_sent = jnp.where(front, back_narrow, front_narrow)
    dz1, wide_sent, narrow_sent = lax.optimization_barrier((dz1, wide_sent, narrow_sent))
    wide_got = swapped(wide_sent)
    narrow_got = swapped(narrow_sent)
    (image_grad,) = stage(
        bound(image_kernel),
        (spec((1, 2 * side, 2 * side, slots, c_in), BF16),),
        "d",
        (dz1, w_reduce0, dzs, w_short),
        "dddd",
        (pltpu.VMEM((all_rows, c_in), F32),),
    )
    block_out = block_out.transpose(0, 3, 1, 2, 4)
    image_grad, wide_got, narrow_got = lax.optimization_barrier((image_grad, wide_got, narrow_got))
    wide_sums = jnp.where(front, wide_front, sums6) + wide_got[:2]
    width = out // (2 * devices)
    both_short = jnp.stack([sums3[2] + wide_got[3], sums3[0] + wide_got[2]])
    short_norm = lax.dynamic_slice_in_dim(both_short, (section * devices + dp_index) * width, width, 1)
    narrow_sums = jnp.where(front, front_narrow, back_narrow) + narrow_got
    if packed:
        expand1, mid1 = first.finish()
        image_grad = tied(image_grad, (), (third,))
        third.advance()
        image_grad = tied(image_grad, (third,))
        image_grad = tied(image_grad, (), (third,))
        third.advance()
        image_grad = tied(image_grad, (third,))
        reduce1, expand0, short_grad = second.finish()
        image_grad = tied(image_grad, (), (third,))
        mid0, reduce0 = third.finish()

        def to_owner(front_half, back_half, axis):
            mine = jnp.where(front, front_half, back_half)
            other = swapped(jnp.where(front, back_half, front_half))
            first_half = jnp.where(front, mine, other)
            second_half = jnp.where(front, other, mine)
            return jnp.concatenate([first_half, second_half], axis=axis)

        grad_mid = to_owner(mid0, mid1, 1)
        grad_expand = to_owner(expand0, expand1, 1)
    else:

        def product(left, right):
            return dot_rows(left, right).astype(BF16)

        def of_block(front_grad, back_grad):
            mine = jnp.where(front, front_grad, back_grad)
            both = mine + swapped(jnp.where(front, back_grad, front_grad))
            return lax.psum_scatter(both, "dp", scatter_dimension=0, tiled=True).astype(F32)

        def of_both(grad):
            return lax.psum_scatter(grad, ("section", "dp"), scatter_dimension=0, tiled=True).astype(F32)

        grad_mid = of_block(product(taps0, dz2), product(taps1, du2))
        grad_expand = of_block(product(a2, dz3), product(c2, du3))
        reduce1 = of_both(product(joined, du1))
        short_grad = of_both(product(x[:rows], dzs))
        reduce0 = of_both(product(x, dz1))
    return (
        block_out,
        image_grad.transpose(0, 3, 1, 2, 4),
        reduce0,
        short_grad,
        short_norm,
        reduce1,
        grad_mid[None],
        grad_expand[None],
        narrow_sums[None, :, 1],
        narrow_sums[None, :, 0],
        wide_sums[None, 1],
        wide_sums[None, 0],
    )


def solution(mesh):
    return jax.shard_map(
        body,
        mesh=mesh,
        in_specs=(
            P(None, "dp", None, None, None),
            P(None, "dp", None, None, None),
            P(),
            P(),
            P(),
            P(),
            P(),
            P(),
            P("section", None, None),
            P("section", None, None),
            P("section", None, None),
            P("section", None, None),
            P("section", None),
            P("section", None),
        ),
        out_specs=(
            P("section", "dp", None, None, None),
            P("section", "dp", None, None, None),
            P(("section", "dp"), None),
            P(("section", "dp"), None),
            P(None, ("section", "dp")),
            P(("section", "dp"), None),
            P("section", "dp", None),
            P("section", "dp", None),
            P("section", None, None),
            P("section", None, None),
            P("section", None),
            P("section", None),
        ),
        check_vma=False,
    )
```

```python
import jax
import jax.numpy as jnp
from jax import lax
from jax.experimental import pallas as pl
from jax.experimental.pallas import tpu as pltpu
from jax.sharding import PartitionSpec as P


EPSILON = 1e-05
F32 = jnp.float32
BF16 = jnp.bfloat16
VMEM = pl.BlockSpec(memory_space=pltpu.VMEM)
SMEM = pl.BlockSpec(memory_space=pltpu.SMEM)
ANY = pl.BlockSpec(memory_space=pl.ANY)


def spec(shape, dtype=F32):
    return jax.ShapeDtypeStruct(shape, dtype)


class Late:
    def __init__(self, source, target, sem):
        self.copy = pltpu.make_async_copy(source, target, sem)
        self.copy.start()
        self.target = target
        self.shape = target.shape
        self.waiting = True

    def get(self):
        if self.waiting:
            self.copy.wait()
            self.waiting = False
        return self.target

    def __getitem__(self, index):
        return self.get()[index]


class Out:
    def __init__(self, buffer, target, sem):
        self.ref = buffer
        self.shape = buffer.shape
        self.copy = pltpu.make_async_copy(buffer, target, sem)
        self.sent = False

    def __setitem__(self, index, value):
        self.ref[index] = value

    def send(self):
        self.copy.start()
        self.sent = True


def stage(kernel, outs, out_places, args, places, scratch=()):
    kinds = {"g": VMEM, "s": SMEM, "a": ANY, "d": ANY}
    late = [n for n, kind in enumerate(places) if kind == "d"]
    late_out = [n for n, kind in enumerate(out_places) if kind == "d"]
    buffers = [pltpu.VMEM(args[n].shape, args[n].dtype) for n in late]
    buffers += [pltpu.VMEM(outs[n].shape, outs[n].dtype) for n in late_out]
    args = [
        pltpu.with_memory_space_constraint(arg, pltpu.VMEM) if kind == "g" else arg
        for arg, kind in zip(args, places)
    ]

    def run(*refs):
        inputs = list(refs[: len(args)])
        results = list(refs[len(args) : len(args) + len(outs)])
        rest = refs[len(args) + len(outs) :]
        own, held, sem = rest[: len(scratch)], rest[len(scratch) : -1], rest[-1]
        for place, n in enumerate(late):
            inputs[n] = Late(inputs[n], held[place], sem.at[place])
        waiting = []
        for place, n in enumerate(late_out):
            place += len(late)
            results[n] = Out(held[place], results[n], sem.at[place])
            waiting.append(results[n])
        kernel(*inputs, *results, *own)
        for one in inputs:
            if isinstance(one, Late):
                one.get()
        for one in waiting:
            if not one.sent:
                one.send()
        for one in waiting:
            one.copy.wait()

    return pl.pallas_call(
        run,
        out_shape=list(outs),
        in_specs=[kinds[kind] for kind in places],
        out_specs=[kinds[kind] for kind in out_places],
        scratch_shapes=list(scratch) + buffers + [pltpu.SemaphoreType.DMA((max(1, len(buffers)),))],
        compiler_params=pltpu.CompilerParams(vmem_limit_bytes=58 << 20),
    )(*args)


def split(value, size):
    if size & (size - 1) == 0:
        return value >> (size.bit_length() - 1), value & (size - 1)
    return value // size, value % size


class Geometry:
    def __init__(self, slots, side):
        self.slots = slots
        self.side = side
        self.pitch = side + 1
        self.line = self.pitch * slots
        self.rows = self.pitch * self.line
        self.pixels = side * side

    def mask(self, start, step, width, count=None):
        row = start + lax.broadcasted_iota(jnp.int32, (step, 128), 0)
        position, image = split(row, self.slots)
        line, column = split(position, self.pitch)
        line = split(line, self.pitch)[1]
        good = (column < self.side) & (line < self.side)
        if count is not None:
            good = good & (image < count)
        value = jnp.where(good, 1.0, 0.0).astype(F32)
        return jnp.concatenate([value] * (width // 128), axis=1) if width > 128 else value


def over_rows(rows, step, body, init):
    def one(i, carry):
        return body(pl.multiple_of(i * step, step), carry)

    return lax.fori_loop(0, rows // step, one, init)


def fold_rows(block):
    rows, width = block.shape
    return jnp.sum(block.reshape(rows // 8, 8, width), axis=0)


def step_of(width):
    return 64 if width <= 512 else 16


def local_stats(z_ref, geo, count, planes):
    rows, width = z_ref.shape
    step = step_of(width)
    total = (count * (geo.pixels * planes)).astype(F32)

    def plain(start, acc):
        return acc + fold_rows(z_ref[pl.ds(start, step), :].astype(F32) * geo.mask(start, step, width, count))

    zero = jnp.zeros((8, width), F32)
    average = jnp.sum(over_rows(rows, step, plain, zero), axis=0, keepdims=True) / total

    def squared(start, acc):
        centered = z_ref[pl.ds(start, step), :].astype(F32) - average
        return acc + fold_rows(centered * centered * geo.mask(start, step, width, count))

    spread = jnp.sum(over_rows(rows, step, squared, zero), axis=0, keepdims=True)
    return average, spread


def send_short(out_ref, values):
    values = values.astype(BF16)
    for device in range(out_ref.shape[0]):
        out_ref[device] = values


def packed_stats(pairs):
    average = jnp.concatenate([pair[0] for pair in pairs], axis=1)
    spread = jnp.concatenate([pair[1] for pair in pairs], axis=1)
    high = average.astype(BF16).astype(F32)
    half = spread.shape[1] // 2
    return jnp.concatenate(
        [
            jnp.concatenate([high, spread[:, :half]], axis=1),
            jnp.concatenate([average - high, spread[:, half:]], axis=1),
        ],
        axis=0,
    )


class Unpacked:
    def __init__(self, got):
        self.devices = got.shape[0]
        width = got.shape[2] * 2 // 3
        self.average, self.spread = [], []
        for device in range(self.devices):
            rows = got[device].astype(F32)
            self.average.append(rows[0:1, :width] + rows[1:2, :width])
            self.spread.append(jnp.concatenate([rows[0:1, width:], rows[1:2, width:]], axis=1))
        self.shape = (self.devices, 2, width)

    def __getitem__(self, index):
        device, row, lanes = index
        return (self.average if row.start == 0 else self.spread)[device][:, lanes]


def send_rows(out_ref, values):
    lane = 0
    for pair in values:
        width = pair[0].shape[1]
        for row, value in enumerate(pair):
            for device in range(out_ref.shape[0]):
                out_ref[device, row : row + 1, lane : lane + width] = value
        lane += width


def total_of(counts, section, pixels):
    total = counts[section, 0]
    for device in range(1, counts.shape[1]):
        total = total + counts[section, device]
    return (total * pixels).astype(F32)


def combined(got_ref, lanes, counts, section, pixels):
    devices = got_ref.shape[0]
    total = total_of(counts, section, pixels)
    sizes = [(counts[section, device] * pixels).astype(F32) for device in range(devices)]
    average = sizes[0] * got_ref[0, 0:1, lanes]
    for device in range(1, devices):
        average = average + sizes[device] * got_ref[device, 0:1, lanes]
    average = average / total
    spread = jnp.zeros_like(average)
    for device in range(devices):
        apart = got_ref[device, 0:1, lanes] - average
        spread = spread + (got_ref[device, 1:2, lanes] + sizes[device] * (apart * apart))
    return average, lax.rsqrt(spread / total + EPSILON)


def summed(got_ref):
    total = got_ref[0].astype(F32)
    for device in range(1, got_ref.shape[0]):
        total = total + got_ref[device].astype(F32)
    return total


def sigmoid(values):
    return 1.0 / (1.0 + jnp.exp(-values))


def slope(values):
    part = sigmoid(values)
    return part * (1.0 + values * (1.0 - part))


class Choice:
    def __init__(self, section, wanted, own, other, target, sem):
        self.mine = section == wanted
        self.copies = (
            pltpu.make_async_copy(own.at[0], target, sem),
            pltpu.make_async_copy(other.at[0], target, sem),
        )

    def start(self):
        @pl.when(self.mine)
        def _():
            self.copies[0].start()

        @pl.when(jnp.logical_not(self.mine))
        def _():
            self.copies[1].start()

    def wait(self):
        @pl.when(self.mine)
        def _():
            self.copies[0].wait()

        @pl.when(jnp.logical_not(self.mine))
        def _():
            self.copies[1].wait()


def dot(left, right):
    return jnp.dot(left, right, preferred_element_type=F32)


def dot_back(left, right):
    return lax.dot_general(left, right, (((1,), (1,)), ((), ())), preferred_element_type=F32)


def dot_rows(left, right):
    return lax.dot_general(left, right, (((0,), (0,)), ((), ())), preferred_element_type=F32)


def turned(values, shift):
    shift = shift % values.shape[0]
    if shift == 0:
        return values
    return jnp.concatenate([values[-shift:], values[:-shift]], axis=0)


def taps_of(stride):
    found = []
    for tap_row in range(3):
        for column in range(3):
            if stride == 1:
                found.append((0, tap_row - 1, column - 1))
            else:
                plane = 2 * (tap_row != 1) + (column != 1)
                found.append((plane, -(tap_row == 0), -(column == 0)))
    return found


def first_kernel(geo, place, counts, images, weight, x_out, z_out, sent, raw, slabs, sem):
    section = place[1]
    count = counts[section, place[0]]
    load = pltpu.make_async_copy(images.at[section], raw, sem.at[0])
    load.start()
    used = geo.side * geo.slots
    x_ref = x_out.ref
    for plane in range(4):
        last = (plane + 1) * geo.rows
        x_ref[last - geo.line : last, :] = jnp.zeros((geo.line, x_ref.shape[1]), BF16)
        slabs[plane, used : geo.line, :] = jnp.zeros((geo.slots, x_ref.shape[1]), F32)
    load.wait()
    for line in range(geo.side):
        for plane in range(4):
            for column in range(geo.side):
                at = column * geo.slots
                slabs[plane, at : at + geo.slots, :] = raw[
                    2 * line + plane // 2, 2 * column + plane % 2
                ].astype(F32)
            at = plane * geo.rows + line * geo.line
            x_ref[at : at + geo.line, :] = slabs[plane].astype(BF16)
    x_out.send()
    weight = weight.get()
    z_ref = z_out.ref
    for plane in range(4):
        at = plane * geo.rows
        z_ref[at : at + geo.rows, :] = dot(x_ref[at : at + geo.rows, :], weight[...]).astype(z_ref.dtype)
    z_out.send()
    send_rows(sent, (local_stats(z_ref, geo, count, 4),))


def short_kernel(geo, place, counts, x_any, weight, z_out, stats, x_vmem, sem):
    count = counts[place[1], place[0]]
    load = pltpu.make_async_copy(x_any.at[pl.ds(0, geo.rows)], x_vmem, sem.at[0])
    load.start()
    load.wait()
    z_ref = z_out.ref
    z_ref[...] = dot(x_vmem[...], weight.get()[...]).astype(BF16)
    z_out.send()
    average, spread = local_stats(z_ref, geo, count, 1)
    stats[0:1, :] = average
    stats[1:2, :] = spread


def tap_kernel(geo, planes, block, place, counts, got, z_in, narrow, own, other, *rest):
    if planes == 4:
        stats, taps, z_out, moments, sent, active, weight, sem = rest
    else:
        taps, z_out, moments, sent, active, weight, sem = rest
    section = place[1]
    count = counts[section, place[0]]
    choice = Choice(section, block, own, other, weight, sem.at[0])
    choice.start()
    average, inverse = combined(got, slice(None), counts, section, geo.pixels * planes)
    moments[0:1, :] = average
    moments[1:2, :] = inverse
    gain = narrow[0:1, :] * inverse
    offset = narrow[2:3, :]
    z_ref = z_in.get()
    rows_of, width = z_ref.shape

    def activate(start, carry):
        pre = (z_ref[pl.ds(start, 64), :].astype(F32) - average) * gain + offset
        active[pl.ds(start, 64), :] = pre * sigmoid(pre) * geo.mask(start, 64, width)
        return carry

    over_rows(rows_of, 64, activate, 0)
    ready = {}
    for tap, (plane, line, column) in enumerate(taps_of(2 if planes == 4 else 1)):
        if (plane, column) not in ready:
            values = active[plane * geo.rows : (plane + 1) * geo.rows, :]
            if column != 0:
                values = pltpu.roll(values, (-column * geo.slots) % geo.rows, 0)
            ready[plane, column] = values.astype(BF16)
        taps.ref[:, tap * width : (tap + 1) * width] = turned(ready[plane, column], -line * geo.line)
    taps.send()
    choice.wait()
    z_out.ref[...] = dot(taps.ref[...], weight[...])
    z_out.send()
    values = local_stats(z_out.ref, geo, count, 1)
    if planes == 4:
        send_short(sent, packed_stats((values, (stats[0:1, :], stats[1:2, :]))))
    else:
        send_rows(sent, (values,))


def expand_kernel(geo, block, extra, place, counts, got, z_in, narrow, own, other, *rest):
    if extra:
        a_out, z_out, moments, moments_s, sent, weight, sem = rest
    else:
        a_out, z_out, moments, sent, weight, sem = rest
    section = place[1]
    count = counts[section, place[0]]
    choice = Choice(section, block, own, other, weight, sem.at[0])
    choice.start()
    if extra:
        got = Unpacked(got)
    average, inverse = combined(got, slice(0, z_in.shape[1]), counts, section, geo.pixels)
    moments[0:1, :] = average
    moments[1:2, :] = inverse
    gain = narrow[1:2, :] * inverse
    offset = narrow[3:4, :]
    z_ref = z_in.get()

    def activate(start, carry):
        pre = (z_ref[pl.ds(start, 64), :] - average) * gain + offset
        a_out.ref[pl.ds(start, 64), :] = (pre * sigmoid(pre)).astype(BF16)
        return carry

    over_rows(geo.rows, 64, activate, 0)
    a_out.send()
    choice.wait()
    z_out.ref[...] = dot(a_out.ref[...], weight[...]).astype(BF16)
    z_out.send()
    send_rows(sent, (local_stats(z_out.ref, geo, count, 1),))
    sent.send()
    if extra:
        lanes = slice(z_ref.shape[1], got.shape[2])
        for row, value in enumerate(combined(got, lanes, counts, section, geo.pixels)):
            moments_s[row : row + 1, :] = value


def join_kernel(geo, place, counts, got, z3, zs, moments_s, wide, short, weight, joined, u_out, moments, sent):
    section = place[1]
    count = counts[section, place[0]]
    average_c, inverse_c = combined(got, slice(None), counts, section, geo.pixels)
    average_s, inverse_s = moments_s[0:1, :], moments_s[1:2, :]
    for number, value in enumerate((average_c, inverse_c, average_s, inverse_s)):
        moments[number : number + 1, :] = value
    gain_c = wide[0:1, :] * inverse_c
    gain_s = short[0:1, :] * inverse_s
    offset = wide[1:2, :] + short[1:2, :]
    z3, zs = z3.get(), zs.get()

    def activate(start, carry):
        rows = pl.ds(start, 16)
        pre = (
            (z3[rows, :].astype(F32) - average_c) * gain_c
            + (zs[rows, :].astype(F32) - average_s) * gain_s
            + offset
        )
        joined.ref[rows, :] = (pre * sigmoid(pre)).astype(BF16)
        return carry

    over_rows(geo.rows, 16, activate, 0)
    joined.send()
    u_out.ref[...] = dot(joined.ref[...], weight.get()[...])
    u_out.send()
    send_rows(sent, (local_stats(u_out.ref, geo, count, 1),))


def turn_kernel(geo, place, counts, got, u3, joined, wide, out_grad, block_out, g_out, moments, sent, raw, flat, sem):
    section = place[1]
    count = counts[section, place[0]]
    load = pltpu.make_async_copy(out_grad.at[section], raw, sem.at[0])
    load.start()
    average, inverse = combined(got, slice(None), counts, section, geo.pixels)
    moments[0:1, :] = average
    moments[1:2, :] = inverse
    g_ref = flat
    width = g_ref.shape[1]
    empty = jnp.zeros((geo.slots, width), F32)
    for line in range(geo.side):
        at = line * geo.line + geo.side * geo.slots
        g_ref[at : at + geo.slots, :] = empty
    g_ref[geo.rows - geo.line : geo.rows, :] = jnp.zeros((geo.line, width), F32)
    load.wait()
    for line in range(geo.side):
        for column in range(geo.side):
            at = line * geo.line + column * geo.slots
            g_ref[at : at + geo.slots, :] = raw[line, column].astype(F32)
    weight = wide[0:1, :]
    offset = wide[1:2, :]
    u3, joined = u3.get(), joined.get()

    def activate(start, carry):
        plain, scaled = carry
        rows = pl.ds(start, 16)
        normed = (u3[rows, :].astype(F32) - average) * inverse
        pre = normed * weight + offset + joined[rows, :].astype(F32)
        part = sigmoid(pre)
        upstream = g_ref[rows, :] * geo.mask(start, 16, width, count) * (part * (1.0 + pre * (1.0 - part)))
        flat[rows, :] = pre * part
        g_out.ref[rows, :] = upstream.astype(BF16)
        return plain + fold_rows(upstream), scaled + fold_rows(upstream * normed)

    zero = jnp.zeros((8, width), F32)
    plain, scaled = over_rows(geo.rows, 16, activate, (zero, zero))
    g_out.send()
    sums = (jnp.sum(plain, axis=0, keepdims=True), jnp.sum(scaled, axis=0, keepdims=True))
    send_short(sent, jnp.concatenate(sums, axis=0))
    sent.send()
    for line in range(geo.side):
        for column in range(geo.side):
            at = line * geo.line + column * geo.slots
            block_out.ref[0, line, column] = flat[at : at + geo.slots, :].astype(BF16)


def norm_grad(geo, rows_of, z_ref, g_ref, average, inverse, gain, plain, scaled, total, count, out_ref):
    width = z_ref.shape[1]
    step = step_of(width)
    factor = gain * inverse
    plain_part = plain / total
    scaled_part = scaled / total * inverse

    def one(start, carry):
        rows = pl.ds(start, step)
        centered = z_ref[rows, :].astype(F32) - average
        value = factor * (g_ref[rows, :].astype(F32) - plain_part - centered * scaled_part)
        out_ref[rows, :] = (value * geo.mask(start, step, width, count)).astype(out_ref.dtype)
        return carry

    over_rows(rows_of, step, one, 0)


def silu_back(geo, z_ref, average, inverse, gain, offset, g_ref, out_ref):
    rows_of, width = z_ref.shape
    step = step_of(width)

    def one(start, carry):
        plain, scaled = carry
        rows = pl.ds(start, step)
        normed = (z_ref[rows, :].astype(F32) - average) * inverse
        upstream = g_ref[rows, :] * slope(normed * gain + offset) * geo.mask(start, step, width)
        out_ref[rows, :] = upstream.astype(out_ref.dtype)
        return plain + fold_rows(upstream), scaled + fold_rows(upstream * normed)

    zero = jnp.zeros((8, width), F32)
    plain, scaled = over_rows(rows_of, step, one, (zero, zero))
    return jnp.sum(plain, axis=0, keepdims=True), jnp.sum(scaled, axis=0, keepdims=True)


def expand_back(geo, block, two, place, counts, got, g_in, z3, mom3, wide, *rest):
    if two:
        zs, short, z2, mom2, narrow, own, other, dv, dvs, g_out, sums, sent, weight, sem = rest
    else:
        z2, mom2, narrow, own, other, dv, g_out, sums, sent, weight, sem = rest
    section = place[1]
    count = counts[section, place[0]]
    choice = Choice(section, block, own, other, weight, sem.at[0])
    choice.start()
    total = total_of(counts, section, geo.pixels)
    main = dv.shape[1]
    both = summed(got)
    plain, scaled = both[0:1, :main], both[1:2, :main]
    sums[0:1, :] = plain
    sums[1:2, :] = scaled
    g_ref = g_in.get()
    norm_grad(
        geo, geo.rows, z3.get(), g_ref, mom3[0:1, :], mom3[1:2, :], wide[0:1, :], plain, scaled, total, count, dv.ref
    )
    dv.send()
    choice.wait()
    g_out.ref[...] = dot_back(dv.ref[...], weight[...])
    send_rows(
        sent,
        (
            silu_back(
                geo, z2.get(), mom2[0:1, :], mom2[1:2, :], narrow[1:2, :], narrow[3:4, :], g_out.ref, g_out.ref
            ),
        ),
    )
    sent.send()
    g_out.send()
    if two:
        scaled = jnp.concatenate([both[0:1, main:], both[1:2, main:]], axis=1)
        sums[2:3, :] = scaled
        norm_grad(
            geo, geo.rows, zs.get(), g_ref, mom3[2:3, :], mom3[3:4, :], short[0:1, :], plain, scaled, total, count,
            dvs.ref,
        )
        dvs.send()


def tap_back(geo, planes, block, place, counts, got, g_in, z2, mom2, narrow, z1, mom1, own, other, dv, g_out, sums, sent,
             work, wide_dv, weight, sem):
    section = place[1]
    count = counts[section, place[0]]
    choice = Choice(section, block, own, other, weight, sem.at[0])
    choice.start()
    total = total_of(counts, section, geo.pixels)
    both = summed(got)
    plain, scaled = both[0:1, :], both[1:2, :]
    sums[0:1, :] = plain
    sums[1:2, :] = scaled
    norm_grad(
        geo, geo.rows, z2.get(), g_in.get(), mom2[0:1, :], mom2[1:2, :], narrow[1:2, :], plain, scaled, total, count,
        wide_dv,
    )
    dv.ref[...] = wide_dv[...].astype(BF16)
    dv.send()
    choice.wait()
    width = work.shape[1]
    ready = {}
    totals = [None] * planes
    for tap, (plane, line, column) in enumerate(taps_of(2 if planes == 4 else 1)):
        if column not in ready:
            values = wide_dv[...]
            if column != 0:
                values = pltpu.roll(values, (column * geo.slots) % geo.rows, 0)
            ready[column] = values.astype(BF16)
        left = turned(ready[column], line * geo.line)
        product = dot_back(left, weight[tap * width : (tap + 1) * width, :])
        totals[plane] = product if totals[plane] is None else totals[plane] + product
    for plane in range(planes):
        work[plane * geo.rows : (plane + 1) * geo.rows, :] = totals[plane]
    send_rows(
        sent,
        (
            silu_back(
                geo, z1.get(), mom1[0:1, :], mom1[1:2, :], narrow[0:1, :], narrow[2:3, :], work, g_out.ref
            ),
        ),
    )


def join_back(geo, place, counts, got, g_in, u1, mom4, narrow, weight, g3, z3, zs, mom3, wide, short, dv, g_out, sums,
              sent, flat):
    section = place[1]
    count = counts[section, place[0]]
    total = total_of(counts, section, geo.pixels)
    both = summed(got)
    plain, scaled = both[0:1, :], both[1:2, :]
    sums[0:1, :] = plain
    sums[1:2, :] = scaled
    norm_grad(
        geo, geo.rows, u1.get(), g_in.get(), mom4[0:1, :], mom4[1:2, :], narrow[0:1, :], plain, scaled, total, count,
        dv.ref,
    )
    dv.send()
    flat[...] = dot_back(dv.ref[...], weight.get()[...])
    average_c, inverse_c = mom3[0:1, :], mom3[1:2, :]
    average_s, inverse_s = mom3[2:3, :], mom3[3:4, :]
    gain_c, gain_s = wide[0:1, :], short[0:1, :]
    offset = wide[1:2, :] + short[1:2, :]
    width = flat.shape[1]
    g3, z3, zs = g3.get(), z3.get(), zs.get()

    def one(start, carry):
        plain, scaled_c, scaled_s = carry
        rows = pl.ds(start, 16)
        normed_c = (z3[rows, :].astype(F32) - average_c) * inverse_c
        normed_s = (zs[rows, :].astype(F32) - average_s) * inverse_s
        arrived = (flat[rows, :] + g3[rows, :].astype(F32)).astype(BF16).astype(F32)
        upstream = arrived * slope(normed_c * gain_c + normed_s * gain_s + offset) * geo.mask(start, 16, width)
        g_out.ref[rows, :] = upstream.astype(BF16)
        return (
            plain + fold_rows(upstream),
            scaled_c + fold_rows(upstream * normed_c),
            scaled_s + fold_rows(upstream * normed_s),
        )

    zero = jnp.zeros((8, width), F32)
    results = over_rows(geo.rows, 16, one, (zero, zero, zero))
    g_out.send()
    plain, scaled_c, scaled_s = [jnp.sum(value, axis=0, keepdims=True) for value in results]
    half = width // 2
    send_short(
        sent,
        jnp.concatenate(
            [
                jnp.concatenate([plain, scaled_s[:, :half]], axis=1),
                jnp.concatenate([scaled_c, scaled_s[:, half:]], axis=1),
            ],
            axis=0,
        ),
    )


def reduce_back(geo, place, counts, got, g_in, z1, mom1, narrow, dv, sums):
    section = place[1]
    count = counts[section, place[0]]
    total = total_of(counts, section, geo.pixels * 4)
    both = summed(got)
    plain, scaled = both[0:1, :], both[1:2, :]
    sums[0:1, :] = plain
    sums[1:2, :] = scaled
    norm_grad(
        geo, 4 * geo.rows, z1.get(), g_in.get(), mom1[0:1, :], mom1[1:2, :], narrow[0:1, :], plain, scaled, total, count,
        dv.ref,
    )


def image_kernel(geo, dv, weight, dvs, weight_s, image_grad, flat):
    dv, weight = dv.get(), weight.get()
    for plane in (1, 2, 3, 0):
        at = plane * geo.rows
        product = dot_back(dv[at : at + geo.rows, :], weight[...])
        if plane == 0:
            product = product + dot_back(dvs.get()[...], weight_s.get()[...])
        flat[at : at + geo.rows, :] = product
        for line in range(geo.side):
            for column in range(geo.side):
                row = at + line * geo.line + column * geo.slots
                image_grad.ref[0, 2 * line + plane // 2, 2 * column + plane % 2] = flat[
                    row : row + geo.slots, :
                ].astype(BF16)


def exchange(sent):
    return lax.all_to_all(sent, "dp", 0, 0)


def swapped(value):
    return lax.ppermute(value, "section", [(0, 1), (1, 0)])


def across(value, mask):
    return lax.ppermute(value, "dp", [(i, i ^ mask) for i in range(lax.axis_size("dp"))])


class Piece:
    def __init__(self, rows, columns, devices, split, width):
        self.split = split
        self.width = width
        self.rows = rows // 2 if split == "rows" else rows
        self.columns = columns if split == "rows" else columns // 2
        self.height = self.rows // devices
        self.folded = self.columns < width
        self.lines = self.height // 2 if self.folded else self.height * (self.columns // width)

    def product(self, section, left, right):
        pixels = right.shape[0]
        if self.split == "rows":
            half = pl.ds(pl.multiple_of(section * self.rows, self.rows), self.rows)
            return dot_rows(left[0:pixels, half], right[...])
        half = pl.ds(pl.multiple_of(section * self.columns, self.columns), self.columns)
        return dot_rows(left[0:pixels, :], right[:, half])

    def blocks(self):
        if self.folded:
            half = self.height // 2
            return [(0, 0, half, self.columns, 0, 0), (half, 0, half, self.columns, 0, self.columns)]
        return [
            (0, block * self.width, self.height, self.width, block * self.height, 0)
            for block in range(self.columns // self.width)
        ]


def pieces_kernel(pieces, place, *refs):
    count = len(pieces)
    inputs = refs[: 4 * count]
    send_left, keep_left, send_right, keep_right, total = refs[4 * count :]
    me, section = place[0], place[1]
    half = send_left.shape[3]
    devices = 4 * send_left.shape[1]
    line = 0
    for number, piece in enumerate(pieces):
        left, left_other, right, right_other = [
            one.get() if isinstance(one, Late) else one for one in inputs[4 * number : 4 * number + 4]
        ]
        total[0 : piece.rows, 0 : piece.columns] = piece.product(section, left, right) + piece.product(
            section, left_other, right_other
        )
        for step in range(devices):
            first, second = step & 1, (step >> 1) & 1
            for row, column, height, width, at, lane in piece.blocks():
                start = pl.multiple_of((me ^ step) * piece.height, piece.height) + row
                value = total[pl.ds(start, height), column : column + width].astype(BF16)
                to = slice(line + at, line + at + height)
                for start_lane in range(0, width, half):
                    part = value[:, start_lane : start_lane + half]
                    if lane + start_lane < half:
                        (send_left if first else keep_left).ref[second, step >> 2, to, :] = part
                    else:
                        (send_right if second else keep_right).ref[first, step >> 2, to, :] = part
        line += piece.lines


class Reduction:
    def __init__(self, place, pieces, factors, helds=None):
        devices = lax.axis_size("dp")
        helds = helds or (False,) * len(pieces)
        lines = sum(piece.lines for piece in pieces)
        shape = spec((2, devices // 4, lines, pieces[0].width // 2), BF16)
        self.pieces = pieces
        args = [place]
        for four in factors:
            args += four
        tall = max(piece.rows for piece in pieces)
        wide = max(piece.columns for piece in pieces)
        send_left, keep_left, send_right, keep_right = stage(
            lambda *refs: pieces_kernel(pieces, *refs),
            (shape,) * 4,
            "dddd",
            args,
            "s" + "".join("dddg" if held else "dddd" for held in helds),
            (pltpu.VMEM((tall, wide), F32),),
        )
        self.sent = (send_left, send_right)
        self.rest = (keep_left, keep_right)
        self.masks = (1, 2)
        self.step = 1

    def advance(self):
        self.step += 1
        if self.step == 2:
            self.sent = tuple(rest[1] + got[1] for rest, got in zip(self.rest, self.got))
            self.rest = tuple(rest[0] + got[0] for rest, got in zip(self.rest, self.got))
            self.masks = (2, 1)
        else:
            total = jnp.concatenate([rest + got for rest, got in zip(self.rest, self.got)], axis=-1)
            self.rest = (total[0],)
            self.sent = tuple(total[number] for number in range(1, total.shape[0]))
            self.masks = tuple(number << 2 for number in range(1, total.shape[0]))

    def fly(self):
        self.got = tuple(across(value, mask) for value, mask in zip(self.sent, self.masks))

    def finish(self):
        total = self.rest[0].astype(F32)
        for value in self.got:
            total = total + value.astype(F32)
        results = []
        line = 0
        for piece in self.pieces:
            blocks = [
                total[line + at : line + at + height, lane : lane + width]
                for _, _, height, width, at, lane in piece.blocks()
            ]
            results.append(
                blocks[0] if len(blocks) == 1 else jnp.concatenate(blocks, axis=0 if piece.folded else 1)
            )
            line += piece.lines
        return results


def body(
    images,
    out_grad,
    live_counts,
    w_reduce0,
    w_short,
    short_gain,
    short_bias,
    w_reduce1,
    w_mid,
    w_expand,
    gain_narrow,
    bias_narrow,
    gain_wide,
    bias_wide,
):
    section = lax.axis_index("section")
    dp_index = lax.axis_index("dp")
    devices = lax.axis_size("dp")
    slots = images.shape[1]
    side = images.shape[2] // 2
    geo = Geometry(slots, side)
    c_in = images.shape[4]
    mid = w_mid.shape[2]
    out = w_expand.shape[2]
    rows = geo.rows
    all_rows = 4 * rows
    place = jnp.stack([dp_index, section]).astype(jnp.int32)

    def bound(kernel, *fixed):
        def run(*refs):
            kernel(geo, *fixed, *refs)

        return run

    own_narrow = jnp.concatenate([gain_narrow[0], bias_narrow[0]], axis=0)
    own_wide = jnp.concatenate([gain_wide, bias_wide], axis=0)
    mid_other = swapped(w_mid)
    expand_other = swapped(w_expand)
    other_narrow = swapped(own_narrow)
    other_wide = swapped(own_wide)
    front = section == 0
    narrow0 = jnp.where(front, own_narrow, other_narrow)
    narrow1 = jnp.where(front, other_narrow, own_narrow)
    wide0 = jnp.where(front, own_wide, other_wide)
    wide1 = jnp.where(front, other_wide, own_wide)
    short = jnp.stack([short_gain, short_bias])
    counts = live_counts.T
    images = images.transpose(0, 2, 3, 1, 4)
    out_grad = out_grad.transpose(0, 2, 3, 1, 4)

    def dma(number):
        return pltpu.SemaphoreType.DMA((number,))

    piece_mid = Piece(9 * mid, mid, devices, "columns", mid)
    piece_expand = Piece(mid, out, devices, "columns", mid)
    piece_reduce1 = Piece(out, mid, devices, "rows", mid)
    piece_short = Piece(c_in, out, devices, "rows", mid)
    piece_reduce0 = Piece(c_in, mid, devices, "rows", mid)
    heights = [block[2] for piece in (piece_mid, piece_expand, piece_reduce1, piece_short, piece_reduce0) for block in piece.blocks()]
    packed = devices == 16 and all(height % 16 == 0 for height in heights)

    def partner(value, got):
        if not packed:
            return got, value
        return lax.optimization_barrier((got, swapped(value)))

    x, z1, sent = stage(
        bound(first_kernel),
        (spec((all_rows, c_in), BF16), spec((all_rows, mid), BF16), spec((devices, 2, mid))),
        "ddd",
        (place, counts, images, w_reduce0),
        "ssad",
        (
            pltpu.VMEM((2 * side, 2 * side, slots, c_in), BF16),
            pltpu.VMEM((4, geo.line, c_in), F32),
            dma(1),
        ),
    )
    got = exchange(sent)
    zs, stats_s = stage(
        bound(short_kernel),
        (spec((rows, out), BF16), spec((2, out))),
        "dd",
        (place, counts, x, w_short),
        "ssad",
        (pltpu.VMEM((rows, c_in), BF16), dma(1)),
    )
    tap_scratch = (pltpu.VMEM((9 * mid, mid), BF16), dma(1))
    taps0, z2, mom1, sent = stage(
        bound(tap_kernel, 4, 0),
        (spec((rows, 9 * mid), BF16), spec((rows, mid)), spec((2, mid)), spec((devices, 2, 3 * (mid + out) // 2), BF16)),
        "dddd",
        (place, counts, got, z1, narrow0, w_mid, mid_other, stats_s),
        "ssgddaad",
        (pltpu.VMEM((all_rows, mid), F32),) + tap_scratch,
    )
    got = exchange(sent)
    got, x_other = partner(x, got)
    expand_scratch = (pltpu.VMEM((mid, out), BF16), dma(1))
    a2, z3, mom2, moments_s, sent = stage(
        bound(expand_kernel, 0, True),
        (spec((rows, mid), BF16), spec((rows, out), BF16), spec((2, mid)), spec((2, out)), spec((devices, 2, out))),
        "ddddd",
        (place, counts, got, z2, narrow0, w_expand, expand_other),
        "ssgddaa",
        expand_scratch,
    )
    got = exchange(sent)
    got, taps0_other = partner(taps0, got)
    joined, u1, mom3, sent = stage(
        bound(join_kernel),
        (spec((rows, out), BF16), spec((rows, mid)), spec((4, out)), spec((devices, 2, mid))),
        "dddd",
        (place, counts, got, z3, zs, moments_s, wide0, short, w_reduce1),
        "ssgdddddd",
    )
    got = exchange(sent)
    got, a2_other = partner(a2, got)
    taps1, u2, mom4, sent = stage(
        bound(tap_kernel, 1, 1),
        (spec((rows, 9 * mid), BF16), spec((rows, mid)), spec((2, mid)), spec((devices, 2, mid))),
        "dddd",
        (place, counts, got, u1, narrow1, w_mid, mid_other),
        "ssgddaa",
        (pltpu.VMEM((rows, mid), F32),) + tap_scratch,
    )
    got = exchange(sent)
    got, joined_other = partner(joined, got)
    c2, u3, mom5, sent = stage(
        bound(expand_kernel, 1, False),
        (spec((rows, mid), BF16), spec((rows, out), BF16), spec((2, mid)), spec((devices, 2, out))),
        "dddd",
        (place, counts, got, u2, narrow1, w_expand, expand_other),
        "ssgddaa",
        expand_scratch,
    )
    got = exchange(sent)
    got, taps1_other = partner(taps1, got)
    block_out, g3, mom6, sent = stage(
        bound(turn_kernel),
        (
            spec((1, side, side, slots, out), BF16),
            spec((rows, out), BF16),
            spec((2, out)),
            spec((devices, 2, out), BF16),
        ),
        "dddd",
        (place, counts, got, u3, joined, wide1, out_grad),
        "ssgddda",
        (pltpu.VMEM((side, side, slots, out), BF16), pltpu.VMEM((rows, out), F32), dma(1)),
    )
    got = exchange(sent)
    got, c2_other = partner(c2, got)
    du3, g2, sums6, sent = stage(
        bound(expand_back, 1, False),
        (spec((rows, out), BF16), spec((rows, mid)), spec((2, out)), spec((devices, 2, mid))),
        "dddd",
        (place, counts, got, g3, u3, mom6, wide1, u2, mom5, narrow1, w_expand, expand_other),
        "ssgdddddddaa",
        expand_scratch,
    )
    got = exchange(sent)
    got, du3_other = partner(du3, got)
    tap_back_scratch = (pltpu.VMEM((rows, mid), F32),) + tap_scratch
    du2, g1, sums5, sent = stage(
        bound(tap_back, 1, 1),
        (spec((rows, mid), BF16), spec((rows, mid)), spec((2, mid)), spec((devices, 2, mid))),
        "dddd",
        (place, counts, got, g2, u2, mom5, narrow1, u1, mom4, w_mid, mid_other),
        "ssgddddddaa",
        (pltpu.VMEM((rows, mid), F32),) + tap_back_scratch,
    )
    got = exchange(sent)
    def tied(value, starting=(), arrived=()):
        values = lax.optimization_barrier(
            (value, tuple(one.sent for one in starting), tuple(one.got for one in arrived))
        )
        for one, sent in zip(starting, values[1]):
            one.sent = sent
            one.fly()
        for one, got in zip(arrived, values[2]):
            one.got = got
        return values[0]

    if packed:
        first = Reduction(
            place,
            (piece_expand, piece_mid),
            ((c2, c2_other, du3, du3_other), (taps1, taps1_other, du2, swapped(du2))),
            (False, True),
        )
        got = tied(got, (first,))
    du1, gj, sums4, sent = stage(
        bound(join_back),
        (spec((rows, mid), BF16), spec((rows, out), BF16), spec((2, mid)), spec((devices, 2, out + out // 2), BF16)),
        "dddd",
        (place, counts, got, g1, u1, mom4, narrow1, w_reduce1, g3, z3, zs, mom3, wide0, short),
        "ssgddddddddddd",
        (pltpu.VMEM((rows, out), F32),),
    )
    got = exchange(sent)
    got, du1_other = partner(du1, got)
    if packed:
        first.advance()
        got = tied(got, (first,))
    dz3, dzs, g2, sums3, sent = stage(
        bound(expand_back, 0, True),
        (
            spec((rows, out), BF16),
            spec((rows, out), BF16),
            spec((rows, mid)),
            spec((3, out)),
            spec((devices, 2, mid)),
        ),
        "ddddd",
        (place, counts, got, gj, z3, mom3, wide0, zs, short, z2, mom2, narrow0, w_expand, expand_other),
        "ssgdddddddddaa",
        expand_scratch,
    )
    got = exchange(sent)
    if packed:
        second = Reduction(
            place,
            (piece_reduce1, piece_expand, piece_short),
            (
                (joined, joined_other, du1, du1_other),
                (a2, a2_other, dz3, swapped(dz3)),
                (x, x_other, dzs, swapped(dzs)),
            ),
            (False, True, True),
        )
        got = tied(got, (second,), (first,))
    dz2, g1, sums2, sent = stage(
        bound(tap_back, 4, 0),
        (spec((rows, mid), BF16), spec((all_rows, mid), BF16), spec((2, mid)), spec((devices, 2, mid))),
        "dddd",
        (place, counts, got, g2, z2, mom2, narrow0, z1, mom1, w_mid, mid_other),
        "ssgddddddaa",
        (pltpu.VMEM((all_rows, mid), F32),) + tap_back_scratch,
    )
    got = exchange(sent)
    got, dz2_other = partner(dz2, got)
    if packed:
        second.advance()
        first.advance()
        got = tied(got, (second, first))
    dz1, sums1 = stage(
        bound(reduce_back),
        (spec((all_rows, mid), BF16), spec((2, mid))),
        "dd",
        (place, counts, got, g1, z1, mom1, narrow0),
        "ssgdddd",
    )
    if packed:
        third = Reduction(
            place,
            (piece_mid, piece_reduce0),
            ((taps0, taps0_other, dz2, dz2_other), (x, x_other, dz1, swapped(dz1))),
        )
        dz1 = tied(dz1, (third,), (second,))
        second.advance()
        dz1 = tied(dz1, (second,), (first,))
    wide_front = sums3[:2]
    wide_sent = jnp.concatenate([jnp.where(front, sums6, wide_front), sums3[0:1], sums3[2:3]], axis=0)
    front_narrow = jnp.stack([sums1, sums2])
    back_narrow = jnp.stack([sums4, sums5])
    narrow_sent = jnp.where(front, back_narrow, front_narrow)
    dz1, wide_sent, narrow_sent = lax.optimization_barrier((dz1, wide_sent, narrow_sent))
    wide_got = swapped(wide_sent)
    narrow_got = swapped(narrow_sent)
    (image_grad,) = stage(
        bound(image_kernel),
        (spec((1, 2 * side, 2 * side, slots, c_in), BF16),),
        "d",
        (dz1, w_reduce0, dzs, w_short),
        "dddd",
        (pltpu.VMEM((all_rows, c_in), F32),),
    )
    block_out = block_out.transpose(0, 3, 1, 2, 4)
    image_grad, wide_got, narrow_got = lax.optimization_barrier((image_grad, wide_got, narrow_got))
    wide_sums = jnp.where(front, wide_front, sums6) + wide_got[:2]
    width = out // (2 * devices)
    both_short = jnp.stack([sums3[2] + wide_got[3], sums3[0] + wide_got[2]])
    short_norm = lax.dynamic_slice_in_dim(both_short, (section * devices + dp_index) * width, width, 1)
    narrow_sums = jnp.where(front, front_narrow, back_narrow) + narrow_got
    if packed:
        expand1, mid1 = first.finish()
        image_grad = tied(image_grad, (), (third,))
        third.advance()
        image_grad = tied(image_grad, (third,))
        image_grad = tied(image_grad, (), (third,))
        third.advance()
        image_grad = tied(image_grad, (third,))
        reduce1, expand0, short_grad = second.finish()
        image_grad = tied(image_grad, (), (third,))
        mid0, reduce0 = third.finish()

        def to_owner(front_half, back_half, axis):
            mine = jnp.where(front, front_half, back_half)
            other = swapped(jnp.where(front, back_half, front_half))
            first_half = jnp.where(front, mine, other)
            second_half = jnp.where(front, other, mine)
            return jnp.concatenate([first_half, second_half], axis=axis)

        grad_mid = to_owner(mid0, mid1, 1)
        grad_expand = to_owner(expand0, expand1, 1)
    else:

        def product(left, right):
            return dot_rows(left, right).astype(BF16)

        def of_block(front_grad, back_grad):
            mine = jnp.where(front, front_grad, back_grad)
            both = mine + swapped(jnp.where(front, back_grad, front_grad))
            return lax.psum_scatter(both, "dp", scatter_dimension=0, tiled=True).astype(F32)

        def of_both(grad):
            return lax.psum_scatter(grad, ("section", "dp"), scatter_dimension=0, tiled=True).astype(F32)

        grad_mid = of_block(product(taps0, dz2), product(taps1, du2))
        grad_expand = of_block(product(a2, dz3), product(c2, du3))
        reduce1 = of_both(product(joined, du1))
        short_grad = of_both(product(x[:rows], dzs))
        reduce0 = of_both(product(x, dz1))
    return (
        block_out,
        image_grad.transpose(0, 3, 1, 2, 4),
        reduce0,
        short_grad,
        short_norm,
        reduce1,
        grad_mid[None],
        grad_expand[None],
        narrow_sums[None, :, 1],
        narrow_sums[None, :, 0],
        wide_sums[None, 1],
        wide_sums[None, 0],
    )


def solution(mesh):
    return jax.shard_map(
        body,
        mesh=mesh,
        in_specs=(
            P(None, "dp", None, None, None),
            P(None, "dp", None, None, None),
            P(),
            P(),
            P(),
            P(),
            P(),
            P(),
            P("section", None, None),
            P("section", None, None),
            P("section", None, None),
            P("section", None, None),
            P("section", None),
            P("section", None),
        ),
        out_specs=(
            P("section", "dp", None, None, None),
            P("section", "dp", None, None, None),
            P(("section", "dp"), None),
            P(("section", "dp"), None),
            P(None, ("section", "dp")),
            P(("section", "dp"), None),
            P("section", "dp", None),
            P("section", "dp", None),
            P("section", None, None),
            P("section", None, None),
            P("section", None),
            P("section", None),
        ),
        check_vma=False,
    )
```

```python
import jax
import jax.numpy as jnp
from jax import lax
from jax.experimental import pallas as pl
from jax.experimental.pallas import tpu as pltpu
from jax.sharding import PartitionSpec as P


EPSILON = 1e-05
F32 = jnp.float32
BF16 = jnp.bfloat16
VMEM = pl.BlockSpec(memory_space=pltpu.VMEM)
SMEM = pl.BlockSpec(memory_space=pltpu.SMEM)
ANY = pl.BlockSpec(memory_space=pl.ANY)


def spec(shape, dtype=F32):
    return jax.ShapeDtypeStruct(shape, dtype)


class Late:
    def __init__(self, source, target, sem):
        self.copy = pltpu.make_async_copy(source, target, sem)
        self.copy.start()
        self.target = target
        self.shape = target.shape
        self.waiting = True

    def get(self):
        if self.waiting:
            self.copy.wait()
            self.waiting = False
        return self.target

    def __getitem__(self, index):
        return self.get()[index]


class Out:
    def __init__(self, buffer, target, sem):
        self.ref = buffer
        self.shape = buffer.shape
        self.copy = pltpu.make_async_copy(buffer, target, sem)
        self.sent = False

    def __setitem__(self, index, value):
        self.ref[index] = value

    def send(self):
        self.copy.start()
        self.sent = True


def stage(kernel, outs, out_places, args, places, scratch=()):
    kinds = {"g": VMEM, "s": SMEM, "a": ANY, "d": ANY}
    late = [n for n, kind in enumerate(places) if kind == "d"]
    late_out = [n for n, kind in enumerate(out_places) if kind == "d"]
    buffers = [pltpu.VMEM(args[n].shape, args[n].dtype) for n in late]
    buffers += [pltpu.VMEM(outs[n].shape, outs[n].dtype) for n in late_out]
    args = [
        pltpu.with_memory_space_constraint(arg, pltpu.VMEM) if kind == "g" else arg
        for arg, kind in zip(args, places)
    ]

    def run(*refs):
        inputs = list(refs[: len(args)])
        results = list(refs[len(args) : len(args) + len(outs)])
        rest = refs[len(args) + len(outs) :]
        own, held, sem = rest[: len(scratch)], rest[len(scratch) : -1], rest[-1]
        for place, n in enumerate(late):
            inputs[n] = Late(inputs[n], held[place], sem.at[place])
        waiting = []
        for place, n in enumerate(late_out):
            place += len(late)
            results[n] = Out(held[place], results[n], sem.at[place])
            waiting.append(results[n])
        kernel(*inputs, *results, *own)
        for one in inputs:
            if isinstance(one, Late):
                one.get()
        for one in waiting:
            if not one.sent:
                one.send()
        for one in waiting:
            one.copy.wait()

    return pl.pallas_call(
        run,
        out_shape=list(outs),
        in_specs=[kinds[kind] for kind in places],
        out_specs=[kinds[kind] for kind in out_places],
        scratch_shapes=list(scratch) + buffers + [pltpu.SemaphoreType.DMA((max(1, len(buffers)),))],
        compiler_params=pltpu.CompilerParams(vmem_limit_bytes=58 << 20),
    )(*args)


def split(value, size):
    if size & (size - 1) == 0:
        return value >> (size.bit_length() - 1), value & (size - 1)
    return value // size, value % size


class Geometry:
    def __init__(self, slots, side):
        self.slots = slots
        self.side = side
        self.pitch = side + 1
        self.line = self.pitch * slots
        self.rows = self.pitch * self.line
        self.pixels = side * side

    def mask(self, start, step, width, count=None):
        row = start + lax.broadcasted_iota(jnp.int32, (step, 128), 0)
        position, image = split(row, self.slots)
        line, column = split(position, self.pitch)
        line = split(line, self.pitch)[1]
        good = (column < self.side) & (line < self.side)
        if count is not None:
            good = good & (image < count)
        value = jnp.where(good, 1.0, 0.0).astype(F32)
        return jnp.concatenate([value] * (width // 128), axis=1) if width > 128 else value


def over_rows(rows, step, body, init):
    def one(i, carry):
        return body(pl.multiple_of(i * step, step), carry)

    return lax.fori_loop(0, rows // step, one, init)


def fold_rows(block):
    rows, width = block.shape
    return jnp.sum(block.reshape(rows // 8, 8, width), axis=0)


def step_of(width):
    return 64 if width <= 512 else 16


def local_stats(z_ref, geo, count, planes):
    rows, width = z_ref.shape
    step = step_of(width)
    total = (count * (geo.pixels * planes)).astype(F32)

    def plain(start, acc):
        return acc + fold_rows(z_ref[pl.ds(start, step), :].astype(F32) * geo.mask(start, step, width, count))

    zero = jnp.zeros((8, width), F32)
    average = jnp.sum(over_rows(rows, step, plain, zero), axis=0, keepdims=True) / total

    def squared(start, acc):
        centered = z_ref[pl.ds(start, step), :].astype(F32) - average
        return acc + fold_rows(centered * centered * geo.mask(start, step, width, count))

    spread = jnp.sum(over_rows(rows, step, squared, zero), axis=0, keepdims=True)
    return average, spread


def send_short(out_ref, values):
    values = values.astype(BF16)
    for device in range(out_ref.shape[0]):
        out_ref[device] = values


def packed_stats(pairs):
    average = jnp.concatenate([pair[0] for pair in pairs], axis=1)
    spread = jnp.concatenate([pair[1] for pair in pairs], axis=1)
    high = average.astype(BF16).astype(F32)
    half = spread.shape[1] // 2
    return jnp.concatenate(
        [
            jnp.concatenate([high, spread[:, :half]], axis=1),
            jnp.concatenate([average - high, spread[:, half:]], axis=1),
        ],
        axis=0,
    )


class Unpacked:
    def __init__(self, got):
        self.devices = got.shape[0]
        width = got.shape[2] * 2 // 3
        self.average, self.spread = [], []
        for device in range(self.devices):
            rows = got[device].astype(F32)
            self.average.append(rows[0:1, :width] + rows[1:2, :width])
            self.spread.append(jnp.concatenate([rows[0:1, width:], rows[1:2, width:]], axis=1))
        self.shape = (self.devices, 2, width)

    def __getitem__(self, index):
        device, row, lanes = index
        return (self.average if row.start == 0 else self.spread)[device][:, lanes]


def send_rows(out_ref, values):
    lane = 0
    for pair in values:
        width = pair[0].shape[1]
        for row, value in enumerate(pair):
            for device in range(out_ref.shape[0]):
                out_ref[device, row : row + 1, lane : lane + width] = value
        lane += width


def total_of(counts, section, pixels):
    total = counts[section, 0]
    for device in range(1, counts.shape[1]):
        total = total + counts[section, device]
    return (total * pixels).astype(F32)


def combined(got_ref, lanes, counts, section, pixels):
    devices = got_ref.shape[0]
    total = total_of(counts, section, pixels)
    sizes = [(counts[section, device] * pixels).astype(F32) for device in range(devices)]
    average = sizes[0] * got_ref[0, 0:1, lanes]
    for device in range(1, devices):
        average = average + sizes[device] * got_ref[device, 0:1, lanes]
    average = average / total
    spread = jnp.zeros_like(average)
    for device in range(devices):
        apart = got_ref[device, 0:1, lanes] - average
        spread = spread + (got_ref[device, 1:2, lanes] + sizes[device] * (apart * apart))
    return average, lax.rsqrt(spread / total + EPSILON)


def summed(got_ref):
    total = got_ref[0].astype(F32)
    for device in range(1, got_ref.shape[0]):
        total = total + got_ref[device].astype(F32)
    return total


def sigmoid(values):
    return 1.0 / (1.0 + jnp.exp(-values))


def slope(values):
    part = sigmoid(values)
    return part * (1.0 + values * (1.0 - part))


class Choice:
    def __init__(self, section, wanted, own, other, target, sem):
        self.mine = section == wanted
        self.copies = (
            pltpu.make_async_copy(own.at[0], target, sem),
            pltpu.make_async_copy(other.at[0], target, sem),
        )

    def start(self):
        @pl.when(self.mine)
        def _():
            self.copies[0].start()

        @pl.when(jnp.logical_not(self.mine))
        def _():
            self.copies[1].start()

    def wait(self):
        @pl.when(self.mine)
        def _():
            self.copies[0].wait()

        @pl.when(jnp.logical_not(self.mine))
        def _():
            self.copies[1].wait()


def dot(left, right):
    return jnp.dot(left, right, preferred_element_type=F32)


def dot_back(left, right):
    return lax.dot_general(left, right, (((1,), (1,)), ((), ())), preferred_element_type=F32)


def dot_rows(left, right):
    return lax.dot_general(left, right, (((0,), (0,)), ((), ())), preferred_element_type=F32)


def turned(values, shift):
    shift = shift % values.shape[0]
    if shift == 0:
        return values
    return jnp.concatenate([values[-shift:], values[:-shift]], axis=0)


def taps_of(stride):
    found = []
    for tap_row in range(3):
        for column in range(3):
            if stride == 1:
                found.append((0, tap_row - 1, column - 1))
            else:
                plane = 2 * (tap_row != 1) + (column != 1)
                found.append((plane, -(tap_row == 0), -(column == 0)))
    return found


def first_kernel(geo, place, counts, images, weight, x_out, z_out, sent, raw, slabs, sem):
    section = place[1]
    count = counts[section, place[0]]
    load = pltpu.make_async_copy(images.at[section], raw, sem.at[0])
    load.start()
    used = geo.side * geo.slots
    x_ref = x_out.ref
    for plane in range(4):
        last = (plane + 1) * geo.rows
        x_ref[last - geo.line : last, :] = jnp.zeros((geo.line, x_ref.shape[1]), BF16)
        slabs[plane, used : geo.line, :] = jnp.zeros((geo.slots, x_ref.shape[1]), F32)
    load.wait()
    for line in range(geo.side):
        for plane in range(4):
            for column in range(geo.side):
                at = column * geo.slots
                slabs[plane, at : at + geo.slots, :] = raw[
                    2 * line + plane // 2, 2 * column + plane % 2
                ].astype(F32)
            at = plane * geo.rows + line * geo.line
            x_ref[at : at + geo.line, :] = slabs[plane].astype(BF16)
    x_out.send()
    weight = weight.get()
    z_ref = z_out.ref
    for plane in range(4):
        at = plane * geo.rows
        z_ref[at : at + geo.rows, :] = dot(x_ref[at : at + geo.rows, :], weight[...]).astype(z_ref.dtype)
    z_out.send()
    send_rows(sent, (local_stats(z_ref, geo, count, 4),))


def short_kernel(geo, place, counts, x_any, weight, z_out, stats, x_vmem, sem):
    count = counts[place[1], place[0]]
    load = pltpu.make_async_copy(x_any.at[pl.ds(0, geo.rows)], x_vmem, sem.at[0])
    load.start()
    load.wait()
    z_ref = z_out.ref
    z_ref[...] = dot(x_vmem[...], weight.get()[...]).astype(BF16)
    z_out.send()
    average, spread = local_stats(z_ref, geo, count, 1)
    stats[0:1, :] = average
    stats[1:2, :] = spread


def tap_kernel(geo, planes, block, place, counts, got, z_in, narrow, own, other, *rest):
    if planes == 4:
        stats, taps, z_out, moments, sent, active, weight, sem = rest
    else:
        taps, z_out, moments, sent, active, weight, sem = rest
    section = place[1]
    count = counts[section, place[0]]
    choice = Choice(section, block, own, other, weight, sem.at[0])
    choice.start()
    average, inverse = combined(got, slice(None), counts, section, geo.pixels * planes)
    moments[0:1, :] = average
    moments[1:2, :] = inverse
    gain = narrow[0:1, :] * inverse
    offset = narrow[2:3, :]
    z_ref = z_in.get()
    rows_of, width = z_ref.shape

    def activate(start, carry):
        pre = (z_ref[pl.ds(start, 64), :].astype(F32) - average) * gain + offset
        active[pl.ds(start, 64), :] = pre * sigmoid(pre) * geo.mask(start, 64, width)
        return carry

    over_rows(rows_of, 64, activate, 0)
    ready = {}
    for tap, (plane, line, column) in enumerate(taps_of(2 if planes == 4 else 1)):
        if (plane, column) not in ready:
            values = active[plane * geo.rows : (plane + 1) * geo.rows, :]
            if column != 0:
                values = pltpu.roll(values, (-column * geo.slots) % geo.rows, 0)
            ready[plane, column] = values.astype(BF16)
        taps.ref[:, tap * width : (tap + 1) * width] = turned(ready[plane, column], -line * geo.line)
    taps.send()
    choice.wait()
    z_out.ref[...] = dot(taps.ref[...], weight[...])
    z_out.send()
    values = local_stats(z_out.ref, geo, count, 1)
    if planes == 4:
        send_short(sent, packed_stats((values, (stats[0:1, :], stats[1:2, :]))))
    else:
        send_rows(sent, (values,))


def expand_kernel(geo, block, extra, place, counts, got, z_in, narrow, own, other, *rest):
    if extra:
        a_out, z_out, moments, moments_s, sent, weight, sem = rest
    else:
        a_out, z_out, moments, sent, weight, sem = rest
    section = place[1]
    count = counts[section, place[0]]
    choice = Choice(section, block, own, other, weight, sem.at[0])
    choice.start()
    if extra:
        got = Unpacked(got)
    average, inverse = combined(got, slice(0, z_in.shape[1]), counts, section, geo.pixels)
    moments[0:1, :] = average
    moments[1:2, :] = inverse
    gain = narrow[1:2, :] * inverse
    offset = narrow[3:4, :]
    z_ref = z_in.get()

    def activate(start, carry):
        pre = (z_ref[pl.ds(start, 64), :] - average) * gain + offset
        a_out.ref[pl.ds(start, 64), :] = (pre * sigmoid(pre)).astype(BF16)
        return carry

    over_rows(geo.rows, 64, activate, 0)
    a_out.send()
    choice.wait()
    z_out.ref[...] = dot(a_out.ref[...], weight[...]).astype(BF16)
    z_out.send()
    values = local_stats(z_out.ref, geo, count, 1)
    if extra:
        send_rows(sent, (values,))
    else:
        send_short(sent, packed_stats((values,)))
    sent.send()
    if extra:
        lanes = slice(z_ref.shape[1], got.shape[2])
        for row, value in enumerate(combined(got, lanes, counts, section, geo.pixels)):
            moments_s[row : row + 1, :] = value


def join_kernel(geo, place, counts, got, z3, zs, moments_s, wide, short, weight, joined, u_out, moments, sent):
    section = place[1]
    count = counts[section, place[0]]
    average_c, inverse_c = combined(got, slice(None), counts, section, geo.pixels)
    average_s, inverse_s = moments_s[0:1, :], moments_s[1:2, :]
    for number, value in enumerate((average_c, inverse_c, average_s, inverse_s)):
        moments[number : number + 1, :] = value
    gain_c = wide[0:1, :] * inverse_c
    gain_s = short[0:1, :] * inverse_s
    offset = wide[1:2, :] + short[1:2, :]
    z3, zs = z3.get(), zs.get()

    def activate(start, carry):
        rows = pl.ds(start, 16)
        pre = (
            (z3[rows, :].astype(F32) - average_c) * gain_c
            + (zs[rows, :].astype(F32) - average_s) * gain_s
            + offset
        )
        joined.ref[rows, :] = (pre * sigmoid(pre)).astype(BF16)
        return carry

    over_rows(geo.rows, 16, activate, 0)
    joined.send()
    u_out.ref[...] = dot(joined.ref[...], weight.get()[...])
    u_out.send()
    send_rows(sent, (local_stats(u_out.ref, geo, count, 1),))


def turn_kernel(geo, place, counts, got, u3, joined, wide, out_grad, block_out, g_out, moments, sent, raw, flat, sem):
    section = place[1]
    count = counts[section, place[0]]
    load = pltpu.make_async_copy(out_grad.at[section], raw, sem.at[0])
    load.start()
    average, inverse = combined(Unpacked(got), slice(None), counts, section, geo.pixels)
    moments[0:1, :] = average
    moments[1:2, :] = inverse
    g_ref = flat
    width = g_ref.shape[1]
    empty = jnp.zeros((geo.slots, width), F32)
    for line in range(geo.side):
        at = line * geo.line + geo.side * geo.slots
        g_ref[at : at + geo.slots, :] = empty
    g_ref[geo.rows - geo.line : geo.rows, :] = jnp.zeros((geo.line, width), F32)
    load.wait()
    for line in range(geo.side):
        for column in range(geo.side):
            at = line * geo.line + column * geo.slots
            g_ref[at : at + geo.slots, :] = raw[line, column].astype(F32)
    weight = wide[0:1, :]
    offset = wide[1:2, :]
    u3, joined = u3.get(), joined.get()

    def activate(start, carry):
        plain, scaled = carry
        rows = pl.ds(start, 16)
        normed = (u3[rows, :].astype(F32) - average) * inverse
        pre = normed * weight + offset + joined[rows, :].astype(F32)
        part = sigmoid(pre)
        upstream = g_ref[rows, :] * geo.mask(start, 16, width, count) * (part * (1.0 + pre * (1.0 - part)))
        flat[rows, :] = pre * part
        g_out.ref[rows, :] = upstream.astype(BF16)
        return plain + fold_rows(upstream), scaled + fold_rows(upstream * normed)

    zero = jnp.zeros((8, width), F32)
    plain, scaled = over_rows(geo.rows, 16, activate, (zero, zero))
    g_out.send()
    sums = (jnp.sum(plain, axis=0, keepdims=True), jnp.sum(scaled, axis=0, keepdims=True))
    send_short(sent, jnp.concatenate(sums, axis=0))
    sent.send()
    for line in range(geo.side):
        for column in range(geo.side):
            at = line * geo.line + column * geo.slots
            block_out.ref[0, line, column] = flat[at : at + geo.slots, :].astype(BF16)


def norm_grad(geo, rows_of, z_ref, g_ref, average, inverse, gain, plain, scaled, total, count, out_ref):
    width = z_ref.shape[1]
    step = step_of(width)
    factor = gain * inverse
    plain_part = plain / total
    scaled_part = scaled / total * inverse

    def one(start, carry):
        rows = pl.ds(start, step)
        centered = z_ref[rows, :].astype(F32) - average
        value = factor * (g_ref[rows, :].astype(F32) - plain_part - centered * scaled_part)
        out_ref[rows, :] = (value * geo.mask(start, step, width, count)).astype(out_ref.dtype)
        return carry

    over_rows(rows_of, step, one, 0)


def silu_back(geo, z_ref, average, inverse, gain, offset, g_ref, out_ref):
    rows_of, width = z_ref.shape
    step = step_of(width)

    def one(start, carry):
        plain, scaled = carry
        rows = pl.ds(start, step)
        normed = (z_ref[rows, :].astype(F32) - average) * inverse
        upstream = g_ref[rows, :] * slope(normed * gain + offset) * geo.mask(start, step, width)
        out_ref[rows, :] = upstream.astype(out_ref.dtype)
        return plain + fold_rows(upstream), scaled + fold_rows(upstream * normed)

    zero = jnp.zeros((8, width), F32)
    plain, scaled = over_rows(rows_of, step, one, (zero, zero))
    return jnp.sum(plain, axis=0, keepdims=True), jnp.sum(scaled, axis=0, keepdims=True)


def expand_back(geo, block, two, place, counts, got, g_in, z3, mom3, wide, *rest):
    if two:
        zs, short, z2, mom2, narrow, own, other, dv, dvs, g_out, sums, sent, weight, sem = rest
    else:
        z2, mom2, narrow, own, other, dv, g_out, sums, sent, weight, sem = rest
    section = place[1]
    count = counts[section, place[0]]
    choice = Choice(section, block, own, other, weight, sem.at[0])
    choice.start()
    total = total_of(counts, section, geo.pixels)
    main = dv.shape[1]
    both = summed(got)
    plain, scaled = both[0:1, :main], both[1:2, :main]
    sums[0:1, :] = plain
    sums[1:2, :] = scaled
    g_ref = g_in.get()
    norm_grad(
        geo, geo.rows, z3.get(), g_ref, mom3[0:1, :], mom3[1:2, :], wide[0:1, :], plain, scaled, total, count, dv.ref
    )
    dv.send()
    choice.wait()
    g_out.ref[...] = dot_back(dv.ref[...], weight[...])
    send_rows(
        sent,
        (
            silu_back(
                geo, z2.get(), mom2[0:1, :], mom2[1:2, :], narrow[1:2, :], narrow[3:4, :], g_out.ref, g_out.ref
            ),
        ),
    )
    sent.send()
    g_out.send()
    if two:
        scaled = jnp.concatenate([both[0:1, main:], both[1:2, main:]], axis=1)
        sums[2:3, :] = scaled
        norm_grad(
            geo, geo.rows, zs.get(), g_ref, mom3[2:3, :], mom3[3:4, :], short[0:1, :], plain, scaled, total, count,
            dvs.ref,
        )
        dvs.send()


def tap_back(geo, planes, block, place, counts, got, g_in, z2, mom2, narrow, z1, mom1, own, other, dv, g_out, sums, sent,
             work, wide_dv, weight, sem):
    section = place[1]
    count = counts[section, place[0]]
    choice = Choice(section, block, own, other, weight, sem.at[0])
    choice.start()
    total = total_of(counts, section, geo.pixels)
    both = summed(got)
    plain, scaled = both[0:1, :], both[1:2, :]
    sums[0:1, :] = plain
    sums[1:2, :] = scaled
    norm_grad(
        geo, geo.rows, z2.get(), g_in.get(), mom2[0:1, :], mom2[1:2, :], narrow[1:2, :], plain, scaled, total, count,
        wide_dv,
    )
    dv.ref[...] = wide_dv[...].astype(BF16)
    dv.send()
    choice.wait()
    width = work.shape[1]
    ready = {}
    totals = [None] * planes
    for tap, (plane, line, column) in enumerate(taps_of(2 if planes == 4 else 1)):
        if column not in ready:
            values = wide_dv[...]
            if column != 0:
                values = pltpu.roll(values, (column * geo.slots) % geo.rows, 0)
            ready[column] = values.astype(BF16)
        left = turned(ready[column], line * geo.line)
        product = dot_back(left, weight[tap * width : (tap + 1) * width, :])
        totals[plane] = product if totals[plane] is None else totals[plane] + product
    for plane in range(planes):
        work[plane * geo.rows : (plane + 1) * geo.rows, :] = totals[plane]
    send_rows(
        sent,
        (
            silu_back(
                geo, z1.get(), mom1[0:1, :], mom1[1:2, :], narrow[0:1, :], narrow[2:3, :], work, g_out.ref
            ),
        ),
    )


def join_back(geo, place, counts, got, g_in, u1, mom4, narrow, weight, g3, z3, zs, mom3, wide, short, dv, g_out, sums,
              sent, flat):
    section = place[1]
    count = counts[section, place[0]]
    total = total_of(counts, section, geo.pixels)
    both = summed(got)
    plain, scaled = both[0:1, :], both[1:2, :]
    sums[0:1, :] = plain
    sums[1:2, :] = scaled
    norm_grad(
        geo, geo.rows, u1.get(), g_in.get(), mom4[0:1, :], mom4[1:2, :], narrow[0:1, :], plain, scaled, total, count,
        dv.ref,
    )
    dv.send()
    flat[...] = dot_back(dv.ref[...], weight.get()[...])
    average_c, inverse_c = mom3[0:1, :], mom3[1:2, :]
    average_s, inverse_s = mom3[2:3, :], mom3[3:4, :]
    gain_c, gain_s = wide[0:1, :], short[0:1, :]
    offset = wide[1:2, :] + short[1:2, :]
    width = flat.shape[1]
    g3, z3, zs = g3.get(), z3.get(), zs.get()

    def one(start, carry):
        plain, scaled_c, scaled_s = carry
        rows = pl.ds(start, 16)
        normed_c = (z3[rows, :].astype(F32) - average_c) * inverse_c
        normed_s = (zs[rows, :].astype(F32) - average_s) * inverse_s
        arrived = (flat[rows, :] + g3[rows, :].astype(F32)).astype(BF16).astype(F32)
        upstream = arrived * slope(normed_c * gain_c + normed_s * gain_s + offset) * geo.mask(start, 16, width)
        g_out.ref[rows, :] = upstream.astype(BF16)
        return (
            plain + fold_rows(upstream),
            scaled_c + fold_rows(upstream * normed_c),
            scaled_s + fold_rows(upstream * normed_s),
        )

    zero = jnp.zeros((8, width), F32)
    results = over_rows(geo.rows, 16, one, (zero, zero, zero))
    g_out.send()
    plain, scaled_c, scaled_s = [jnp.sum(value, axis=0, keepdims=True) for value in results]
    half = width // 2
    send_short(
        sent,
        jnp.concatenate(
            [
                jnp.concatenate([plain, scaled_s[:, :half]], axis=1),
                jnp.concatenate([scaled_c, scaled_s[:, half:]], axis=1),
            ],
            axis=0,
        ),
    )


def reduce_back(geo, place, counts, got, g_in, z1, mom1, narrow, dv, sums):
    section = place[1]
    count = counts[section, place[0]]
    total = total_of(counts, section, geo.pixels * 4)
    both = summed(got)
    plain, scaled = both[0:1, :], both[1:2, :]
    sums[0:1, :] = plain
    sums[1:2, :] = scaled
    norm_grad(
        geo, 4 * geo.rows, z1.get(), g_in.get(), mom1[0:1, :], mom1[1:2, :], narrow[0:1, :], plain, scaled, total, count,
        dv.ref,
    )


def image_kernel(geo, dv, weight, dvs, weight_s, image_grad, flat):
    dv, weight = dv.get(), weight.get()
    for plane in (1, 2, 3, 0):
        at = plane * geo.rows
        product = dot_back(dv[at : at + geo.rows, :], weight[...])
        if plane == 0:
            product = product + dot_back(dvs.get()[...], weight_s.get()[...])
        flat[at : at + geo.rows, :] = product
        for line in range(geo.side):
            for column in range(geo.side):
                row = at + line * geo.line + column * geo.slots
                image_grad.ref[0, 2 * line + plane // 2, 2 * column + plane % 2] = flat[
                    row : row + geo.slots, :
                ].astype(BF16)


def exchange(sent):
    return lax.all_to_all(sent, "dp", 0, 0)


def swapped(value):
    return lax.ppermute(value, "section", [(0, 1), (1, 0)])


def across(value, mask):
    return lax.ppermute(value, "dp", [(i, i ^ mask) for i in range(lax.axis_size("dp"))])


class Piece:
    def __init__(self, rows, columns, devices, split, width):
        self.split = split
        self.width = width
        self.rows = rows // 2 if split == "rows" else rows
        self.columns = columns if split == "rows" else columns // 2
        self.height = self.rows // devices
        self.folded = self.columns < width
        self.lines = self.height // 2 if self.folded else self.height * (self.columns // width)

    def product(self, section, left, right):
        pixels = right.shape[0]
        if self.split == "rows":
            half = pl.ds(pl.multiple_of(section * self.rows, self.rows), self.rows)
            return dot_rows(left[0:pixels, half], right[...])
        half = pl.ds(pl.multiple_of(section * self.columns, self.columns), self.columns)
        return dot_rows(left[0:pixels, :], right[:, half])

    def blocks(self):
        if self.folded:
            half = self.height // 2
            return [(0, 0, half, self.columns, 0, 0), (half, 0, half, self.columns, 0, self.columns)]
        return [
            (0, block * self.width, self.height, self.width, block * self.height, 0)
            for block in range(self.columns // self.width)
        ]


def pieces_kernel(pieces, place, *refs):
    count = len(pieces)
    inputs = refs[: 4 * count]
    send_left, keep_left, send_right, keep_right, total = refs[4 * count :]
    me, section = place[0], place[1]
    half = send_left.shape[3]
    devices = 4 * send_left.shape[1]
    line = 0
    for number, piece in enumerate(pieces):
        left, left_other, right, right_other = [
            one.get() if isinstance(one, Late) else one for one in inputs[4 * number : 4 * number + 4]
        ]
        total[0 : piece.rows, 0 : piece.columns] = piece.product(section, left, right) + piece.product(
            section, left_other, right_other
        )
        for step in range(devices):
            first, second = step & 1, (step >> 1) & 1
            for row, column, height, width, at, lane in piece.blocks():
                start = pl.multiple_of((me ^ step) * piece.height, piece.height) + row
                value = total[pl.ds(start, height), column : column + width].astype(BF16)
                to = slice(line + at, line + at + height)
                for start_lane in range(0, width, half):
                    part = value[:, start_lane : start_lane + half]
                    if lane + start_lane < half:
                        (send_left if first else keep_left).ref[second, step >> 2, to, :] = part
                    else:
                        (send_right if second else keep_right).ref[first, step >> 2, to, :] = part
        line += piece.lines


class Reduction:
    def __init__(self, place, pieces, factors, helds=None):
        devices = lax.axis_size("dp")
        helds = helds or (False,) * len(pieces)
        lines = sum(piece.lines for piece in pieces)
        shape = spec((2, devices // 4, lines, pieces[0].width // 2), BF16)
        self.pieces = pieces
        args = [place]
        for four in factors:
            args += four
        tall = max(piece.rows for piece in pieces)
        wide = max(piece.columns for piece in pieces)
        send_left, keep_left, send_right, keep_right = stage(
            lambda *refs: pieces_kernel(pieces, *refs),
            (shape,) * 4,
            "dddd",
            args,
            "s" + "".join("dddg" if held else "dddd" for held in helds),
            (pltpu.VMEM((tall, wide), F32),),
        )
        self.sent = (send_left, send_right)
        self.rest = (keep_left, keep_right)
        self.masks = (1, 2)
        self.step = 1

    def advance(self):
        self.step += 1
        if self.step == 2:
            self.sent = tuple(rest[1] + got[1] for rest, got in zip(self.rest, self.got))
            self.rest = tuple(rest[0] + got[0] for rest, got in zip(self.rest, self.got))
            self.masks = (2, 1)
        else:
            total = jnp.concatenate([rest + got for rest, got in zip(self.rest, self.got)], axis=-1)
            self.rest = (total[0],)
            self.sent = tuple(total[number] for number in range(1, total.shape[0]))
            self.masks = tuple(number << 2 for number in range(1, total.shape[0]))

    def fly(self):
        self.got = tuple(across(value, mask) for value, mask in zip(self.sent, self.masks))

    def finish(self):
        total = self.rest[0].astype(F32)
        for value in self.got:
            total = total + value.astype(F32)
        results = []
        line = 0
        for piece in self.pieces:
            blocks = [
                total[line + at : line + at + height, lane : lane + width]
                for _, _, height, width, at, lane in piece.blocks()
            ]
            results.append(
                blocks[0] if len(blocks) == 1 else jnp.concatenate(blocks, axis=0 if piece.folded else 1)
            )
            line += piece.lines
        return results


def body(
    images,
    out_grad,
    live_counts,
    w_reduce0,
    w_short,
    short_gain,
    short_bias,
    w_reduce1,
    w_mid,
    w_expand,
    gain_narrow,
    bias_narrow,
    gain_wide,
    bias_wide,
):
    section = lax.axis_index("section")
    dp_index = lax.axis_index("dp")
    devices = lax.axis_size("dp")
    slots = images.shape[1]
    side = images.shape[2] // 2
    geo = Geometry(slots, side)
    c_in = images.shape[4]
    mid = w_mid.shape[2]
    out = w_expand.shape[2]
    rows = geo.rows
    all_rows = 4 * rows
    place = jnp.stack([dp_index, section]).astype(jnp.int32)

    def bound(kernel, *fixed):
        def run(*refs):
            kernel(geo, *fixed, *refs)

        return run

    own_narrow = jnp.concatenate([gain_narrow[0], bias_narrow[0]], axis=0)
    own_wide = jnp.concatenate([gain_wide, bias_wide], axis=0)
    mid_other = swapped(w_mid)
    expand_other = swapped(w_expand)
    other_narrow = swapped(own_narrow)
    other_wide = swapped(own_wide)
    front = section == 0
    narrow0 = jnp.where(front, own_narrow, other_narrow)
    narrow1 = jnp.where(front, other_narrow, own_narrow)
    wide0 = jnp.where(front, own_wide, other_wide)
    wide1 = jnp.where(front, other_wide, own_wide)
    short = jnp.stack([short_gain, short_bias])
    counts = live_counts.T
    images = images.transpose(0, 2, 3, 1, 4)
    out_grad = out_grad.transpose(0, 2, 3, 1, 4)

    def dma(number):
        return pltpu.SemaphoreType.DMA((number,))

    piece_mid = Piece(9 * mid, mid, devices, "columns", mid)
    piece_expand = Piece(mid, out, devices, "columns", mid)
    piece_reduce1 = Piece(out, mid, devices, "rows", mid)
    piece_short = Piece(c_in, out, devices, "rows", mid)
    piece_reduce0 = Piece(c_in, mid, devices, "rows", mid)
    heights = [block[2] for piece in (piece_mid, piece_expand, piece_reduce1, piece_short, piece_reduce0) for block in piece.blocks()]
    packed = devices == 16 and all(height % 16 == 0 for height in heights)

    def partner(value, got):
        if not packed:
            return got, value
        return lax.optimization_barrier((got, swapped(value)))

    x, z1, sent = stage(
        bound(first_kernel),
        (spec((all_rows, c_in), BF16), spec((all_rows, mid), BF16), spec((devices, 2, mid))),
        "ddd",
        (place, counts, images, w_reduce0),
        "ssad",
        (
            pltpu.VMEM((2 * side, 2 * side, slots, c_in), BF16),
            pltpu.VMEM((4, geo.line, c_in), F32),
            dma(1),
        ),
    )
    got = exchange(sent)
    zs, stats_s = stage(
        bound(short_kernel),
        (spec((rows, out), BF16), spec((2, out))),
        "dd",
        (place, counts, x, w_short),
        "ssad",
        (pltpu.VMEM((rows, c_in), BF16), dma(1)),
    )
    tap_scratch = (pltpu.VMEM((9 * mid, mid), BF16), dma(1))
    taps0, z2, mom1, sent = stage(
        bound(tap_kernel, 4, 0),
        (spec((rows, 9 * mid), BF16), spec((rows, mid)), spec((2, mid)), spec((devices, 2, 3 * (mid + out) // 2), BF16)),
        "dddd",
        (place, counts, got, z1, narrow0, w_mid, mid_other, stats_s),
        "ssgddaad",
        (pltpu.VMEM((all_rows, mid), F32),) + tap_scratch,
    )
    got = exchange(sent)
    got, x_other = partner(x, got)
    expand_scratch = (pltpu.VMEM((mid, out), BF16), dma(1))
    a2, z3, mom2, moments_s, sent = stage(
        bound(expand_kernel, 0, True),
        (spec((rows, mid), BF16), spec((rows, out), BF16), spec((2, mid)), spec((2, out)), spec((devices, 2, out))),
        "ddddd",
        (place, counts, got, z2, narrow0, w_expand, expand_other),
        "ssgddaa",
        expand_scratch,
    )
    got = exchange(sent)
    got, taps0_other = partner(taps0, got)
    joined, u1, mom3, sent = stage(
        bound(join_kernel),
        (spec((rows, out), BF16), spec((rows, mid)), spec((4, out)), spec((devices, 2, mid))),
        "dddd",
        (place, counts, got, z3, zs, moments_s, wide0, short, w_reduce1),
        "ssgdddddd",
    )
    got = exchange(sent)
    got, a2_other = partner(a2, got)
    taps1, u2, mom4, sent = stage(
        bound(tap_kernel, 1, 1),
        (spec((rows, 9 * mid), BF16), spec((rows, mid)), spec((2, mid)), spec((devices, 2, mid))),
        "dddd",
        (place, counts, got, u1, narrow1, w_mid, mid_other),
        "ssgddaa",
        (pltpu.VMEM((rows, mid), F32),) + tap_scratch,
    )
    got = exchange(sent)
    got, joined_other = partner(joined, got)
    c2, u3, mom5, sent = stage(
        bound(expand_kernel, 1, False),
        (
            spec((rows, mid), BF16),
            spec((rows, out), BF16),
            spec((2, mid)),
            spec((devices, 2, 3 * out // 2), BF16),
        ),
        "dddd",
        (place, counts, got, u2, narrow1, w_expand, expand_other),
        "ssgddaa",
        expand_scratch,
    )
    got = exchange(sent)
    got, taps1_other = partner(taps1, got)
    block_out, g3, mom6, sent = stage(
        bound(turn_kernel),
        (
            spec((1, side, side, slots, out), BF16),
            spec((rows, out), BF16),
            spec((2, out)),
            spec((devices, 2, out), BF16),
        ),
        "dddd",
        (place, counts, got, u3, joined, wide1, out_grad),
        "ssgddda",
        (pltpu.VMEM((side, side, slots, out), BF16), pltpu.VMEM((rows, out), F32), dma(1)),
    )
    got = exchange(sent)
    got, c2_other = partner(c2, got)
    du3, g2, sums6, sent = stage(
        bound(expand_back, 1, False),
        (spec((rows, out), BF16), spec((rows, mid)), spec((2, out)), spec((devices, 2, mid))),
        "dddd",
        (place, counts, got, g3, u3, mom6, wide1, u2, mom5, narrow1, w_expand, expand_other),
        "ssgdddddddaa",
        expand_scratch,
    )
    got = exchange(sent)
    got, du3_other = partner(du3, got)
    tap_back_scratch = (pltpu.VMEM((rows, mid), F32),) + tap_scratch
    du2, g1, sums5, sent = stage(
        bound(tap_back, 1, 1),
        (spec((rows, mid), BF16), spec((rows, mid)), spec((2, mid)), spec((devices, 2, mid))),
        "dddd",
        (place, counts, got, g2, u2, mom5, narrow1, u1, mom4, w_mid, mid_other),
        "ssgddddddaa",
        (pltpu.VMEM((rows, mid), F32),) + tap_back_scratch,
    )
    got = exchange(sent)
    def tied(value, starting=(), arrived=()):
        values = lax.optimization_barrier(
            (value, tuple(one.sent for one in starting), tuple(one.got for one in arrived))
        )
        for one, sent in zip(starting, values[1]):
            one.sent = sent
            one.fly()
        for one, got in zip(arrived, values[2]):
            one.got = got
        return values[0]

    if packed:
        first = Reduction(
            place,
            (piece_expand, piece_mid),
            ((c2, c2_other, du3, du3_other), (taps1, taps1_other, du2, swapped(du2))),
            (False, True),
        )
        got = tied(got, (first,))
    du1, gj, sums4, sent = stage(
        bound(join_back),
        (spec((rows, mid), BF16), spec((rows, out), BF16), spec((2, mid)), spec((devices, 2, out + out // 2), BF16)),
        "dddd",
        (place, counts, got, g1, u1, mom4, narrow1, w_reduce1, g3, z3, zs, mom3, wide0, short),
        "ssgddddddddddd",
        (pltpu.VMEM((rows, out), F32),),
    )
    got = exchange(sent)
    got, du1_other = partner(du1, got)
    if packed:
        first.advance()
        got = tied(got, (first,))
    dz3, dzs, g2, sums3, sent = stage(
        bound(expand_back, 0, True),
        (
            spec((rows, out), BF16),
            spec((rows, out), BF16),
            spec((rows, mid)),
            spec((3, out)),
            spec((devices, 2, mid)),
        ),
        "ddddd",
        (place, counts, got, gj, z3, mom3, wide0, zs, short, z2, mom2, narrow0, w_expand, expand_other),
        "ssgdddddddddaa",
        expand_scratch,
    )
    got = exchange(sent)
    if packed:
        second = Reduction(
            place,
            (piece_reduce1, piece_expand, piece_short),
            (
                (joined, joined_other, du1, du1_other),
                (a2, a2_other, dz3, swapped(dz3)),
                (x, x_other, dzs, swapped(dzs)),
            ),
            (False, True, True),
        )
        got = tied(got, (second,), (first,))
    dz2, g1, sums2, sent = stage(
        bound(tap_back, 4, 0),
        (spec((rows, mid), BF16), spec((all_rows, mid), BF16), spec((2, mid)), spec((devices, 2, mid))),
        "dddd",
        (place, counts, got, g2, z2, mom2, narrow0, z1, mom1, w_mid, mid_other),
        "ssgddddddaa",
        (pltpu.VMEM((all_rows, mid), F32),) + tap_back_scratch,
    )
    got = exchange(sent)
    got, dz2_other = partner(dz2, got)
    if packed:
        second.advance()
        first.advance()
        got = tied(got, (second, first))
    dz1, sums1 = stage(
        bound(reduce_back),
        (spec((all_rows, mid), BF16), spec((2, mid))),
        "dd",
        (place, counts, got, g1, z1, mom1, narrow0),
        "ssgdddd",
    )
    if packed:
        third = Reduction(
            place,
            (piece_mid, piece_reduce0),
            ((taps0, taps0_other, dz2, dz2_other), (x, x_other, dz1, swapped(dz1))),
        )
        dz1 = tied(dz1, (third,), (second,))
        second.advance()
        dz1 = tied(dz1, (second,), (first,))
    wide_front = sums3[:2]
    wide_sent = jnp.concatenate([jnp.where(front, sums6, wide_front), sums3[0:1], sums3[2:3]], axis=0)
    front_narrow = jnp.stack([sums1, sums2])
    back_narrow = jnp.stack([sums4, sums5])
    narrow_sent = jnp.where(front, back_narrow, front_narrow)
    dz1, wide_sent, narrow_sent = lax.optimization_barrier((dz1, wide_sent, narrow_sent))
    wide_got = swapped(wide_sent)
    narrow_got = swapped(narrow_sent)
    (image_grad,) = stage(
        bound(image_kernel),
        (spec((1, 2 * side, 2 * side, slots, c_in), BF16),),
        "d",
        (dz1, w_reduce0, dzs, w_short),
        "dddd",
        (pltpu.VMEM((all_rows, c_in), F32),),
    )
    block_out = block_out.transpose(0, 3, 1, 2, 4)
    image_grad, wide_got, narrow_got = lax.optimization_barrier((image_grad, wide_got, narrow_got))
    wide_sums = jnp.where(front, wide_front, sums6) + wide_got[:2]
    width = out // (2 * devices)
    both_short = jnp.stack([sums3[2] + wide_got[3], sums3[0] + wide_got[2]])
    short_norm = lax.dynamic_slice_in_dim(both_short, (section * devices + dp_index) * width, width, 1)
    narrow_sums = jnp.where(front, front_narrow, back_narrow) + narrow_got
    if packed:
        expand1, mid1 = first.finish()
        image_grad = tied(image_grad, (), (third,))
        third.advance()
        image_grad = tied(image_grad, (third,))
        image_grad = tied(image_grad, (), (third,))
        third.advance()
        image_grad = tied(image_grad, (third,))
        reduce1, expand0, short_grad = second.finish()
        image_grad = tied(image_grad, (), (third,))
        mid0, reduce0 = third.finish()

        def to_owner(front_half, back_half, axis):
            mine = jnp.where(front, front_half, back_half)
            other = swapped(jnp.where(front, back_half, front_half))
            first_half = jnp.where(front, mine, other)
            second_half = jnp.where(front, other, mine)
            return jnp.concatenate([first_half, second_half], axis=axis)

        grad_mid = to_owner(mid0, mid1, 1)
        grad_expand = to_owner(expand0, expand1, 1)
    else:

        def product(left, right):
            return dot_rows(left, right).astype(BF16)

        def of_block(front_grad, back_grad):
            mine = jnp.where(front, front_grad, back_grad)
            both = mine + swapped(jnp.where(front, back_grad, front_grad))
            return lax.psum_scatter(both, "dp", scatter_dimension=0, tiled=True).astype(F32)

        def of_both(grad):
            return lax.psum_scatter(grad, ("section", "dp"), scatter_dimension=0, tiled=True).astype(F32)

        grad_mid = of_block(product(taps0, dz2), product(taps1, du2))
        grad_expand = of_block(product(a2, dz3), product(c2, du3))
        reduce1 = of_both(product(joined, du1))
        short_grad = of_both(product(x[:rows], dzs))
        reduce0 = of_both(product(x, dz1))
    return (
        block_out,
        image_grad.transpose(0, 3, 1, 2, 4),
        reduce0,
        short_grad,
        short_norm,
        reduce1,
        grad_mid[None],
        grad_expand[None],
        narrow_sums[None, :, 1],
        narrow_sums[None, :, 0],
        wide_sums[None, 1],
        wide_sums[None, 0],
    )


def solution(mesh):
    return jax.shard_map(
        body,
        mesh=mesh,
        in_specs=(
            P(None, "dp", None, None, None),
            P(None, "dp", None, None, None),
            P(),
            P(),
            P(),
            P(),
            P(),
            P(),
            P("section", None, None),
            P("section", None, None),
            P("section", None, None),
            P("section", None, None),
            P("section", None),
            P("section", None),
        ),
        out_specs=(
            P("section", "dp", None, None, None),
            P("section", "dp", None, None, None),
            P(("section", "dp"), None),
            P(("section", "dp"), None),
            P(None, ("section", "dp")),
            P(("section", "dp"), None),
            P("section", "dp", None),
            P("section", "dp", None),
            P("section", None, None),
            P("section", None, None),
            P("section", None),
            P("section", None),
        ),
        check_vma=False,
    )
```
